1024 devices in a mesh: gx: 8 (over x, core), gy: 4 (over y), gz: 32 (over z).
Axes of the slice: x: 4, y: 4, z: 32, core: 2. Of those that a mesh axis runs over, the one named last changes fastest.
Arguments:
- state_velocity: float32 [3, 32, 16, 4096], P(None, 'gx', 'gy', 'gz'), may hold values from -3 to 3
- objective_gradient: float32 [3, 32, 16, 4096], P(None, 'gx', 'gy', 'gz'), may hold values from -15 to 15
- wall_flags: int32 [32, 16, 4096], P('gx', 'gy', 'gz'), may hold values 0 or 1
- design_levels: int32 [16, 8, 2048], P('gx', 'gy', 'gz'), may hold values from 0 to 8
Outputs:
- adjoint_velocity: float32 [3, 32, 16, 4096], P(None, 'gx', 'gy', 'gz')
- adjoint_pressure: float32 [16, 8, 2048], P('gx', 'gy', 'gz')
The draws below stay inside these ranges and needn't reach their ends.
All inputs are finite; a program needn't handle non-finite values. No bound on the sum of `wall_flags` on one device may be relied on, other than what follows from the above.
Results may differ from the reference program's by a relative error of at most 0.0003.
Values sent between devices are 32-bit elements; how exact they have to be, the bound alone decides.
A program may use at most 64 MiB of HBM per device.

```python
import math
import jax
import jax.numpy as jnp
import numpy as np
from jax import lax

EZ = 64
ITERS = 3
LEVELS = 9
GX = 16
GY = 8
GZ = 2048
NX = 32
NY = 16
NZ = 4096
N_GZ = 32


def draw_objective_gradient(key, part):
    key = jax.random.fold_in(key, 11)
    across = (jnp.arange(NX, dtype=jnp.float32) / (NX - 1)).reshape(1, NX, 1, 1)
    envelope = 1.0 + 2.0 * across
    noise = jnp.clip(jax.random.normal(key, (3, NX, NY, NZ), jnp.float32), -5.0, 5.0)
    return noise * envelope


def touch_ends(values, key, smallest, top_value):
    dims = values.shape
    spot = [jax.random.randint(jax.random.fold_in(key, axis), (), 0, dims[axis]) for axis in range(len(dims))]
    values = values.at[tuple(spot)].set(smallest)
    longest = dims.index(max(dims))
    spot[longest] = (spot[longest] + 1) % dims[longest]
    return values.at[tuple(spot)].set(top_value)


def block_levels(key, shape, shards, least, top_value):
    def one(axis_at, blocks):
        heights = jax.random.uniform(jax.random.fold_in(jax.random.fold_in(key, 6), axis_at), (blocks,), jnp.float32, least / len(shards), top_value / len(shards))
        return jnp.repeat(jnp.exp(heights), shape[axis_at] // blocks).reshape((-1,) + (1,) * (len(shape) - axis_at - 1))

    gain = one(*shards[0])
    for cut in shards[1:]:
        gain = gain * one(*cut)
    return gain


def bell_draw(own_key, shape, width, limit, shards=(), held_as=jnp.bfloat16):
    drawn = width * jax.random.normal(own_key, shape, jnp.float32)
    if shards:
        drawn = drawn * block_levels(own_key, shape, shards, -0.22, 0.18)
    return jnp.clip(drawn, -limit, limit).astype(held_as)


def setup_inputs(seed: int = 0) -> dict:
    splits = jax.random.split(jax.random.key(seed), 5)
    state_velocity = bell_draw(splits[0], (3, NX, NY, NZ), 0.5, 3.0, ((1, 8), (2, 4), (3, 32)), jnp.float32)
    objective_gradient = draw_objective_gradient(jax.random.fold_in(splits[4], 71), 0)
    wall_flags = touch_ends((jax.random.randint(splits[2], (NX, NY, NZ), 0, 8) < 1).astype(jnp.int32), jax.random.fold_in(splits[2], 1), 0, 1)
    design_levels = touch_ends(jax.random.randint(splits[3], (GX, GY, GZ), 0, LEVELS), jax.random.fold_in(splits[3], 1), 0, LEVELS - 1).astype(jnp.int32)
    return dict(state_velocity=state_velocity, objective_gradient=objective_gradient, wall_flags=wall_flags, design_levels=design_levels)


viscosity = 1.0
brinkman_peak = 8.0
brinkman_shape = 0.1

def shape_values(abscissa):
    return (2.0 * (abscissa - 0.5) * (abscissa - 1.0), -4.0 * abscissa * (abscissa - 1.0), 2.0 * abscissa * (abscissa - 0.5))

def shape_slopes(abscissa):
    return (4.0 * abscissa - 3.0, 4.0 - 8.0 * abscissa, 4.0 * abscissa - 1.0)

def linear_values(abscissa):
    return (1.0 - abscissa, abscissa)

def flipped(matrix):
    return tuple((tuple((matrix[i][j] for i in range(len(matrix)))) for j in range(len(matrix[0]))))

def table_set():
    offset_value = math.sqrt(0.15)
    abscissae = (0.5 - offset_value, 0.5, 0.5 + offset_value)
    weight_list = np.array([5.0 / 18.0, 8.0 / 18.0, 5.0 / 18.0])
    value_matrix = tuple((shape_values(a) for a in abscissae))
    slope_matrix = tuple((shape_slopes(a) for a in abscissae))
    linear_matrix = tuple((linear_values(a) for a in abscissae))
    weight_grid = (weight_list[:, None, None] * weight_list[None, :, None] * weight_list[None, None, :]).reshape(1, 3, 3, 3, 1, 1, 1)
    return (value_matrix, slope_matrix, linear_matrix, flipped(value_matrix), flipped(slope_matrix), flipped(linear_matrix), weight_grid)

def pad_dim(values, dimension, before, after_count):
    widths = [(0, 0)] * values.ndim
    widths[dimension] = (before, after_count)
    return jnp.pad(values, widths)

def contract(element_vals, matrix, dimension):
    pieces = [lax.index_in_dim(element_vals, j, dimension, keepdims=False) for j in range(len(matrix[0]))]
    outputs = []
    for coeffs in matrix:
        running = coeffs[0] * pieces[0]
        for j in range(1, len(coeffs)):
            running = running + coeffs[j] * pieces[j]
        outputs.append(running)
    return jnp.stack(outputs, axis=dimension)

def tensor(element_vals, along_x, along_y, along_z):
    return contract(contract(contract(element_vals, along_z, 3), along_y, 2), along_x, 1)

def split_dim(node_vals, linear):
    length = node_vals.shape[3]
    if linear:
        elements = length - 1
        parts = [lax.slice_in_dim(node_vals, 0, elements, axis=3), lax.slice_in_dim(node_vals, 1, length, axis=3)]
    else:
        elements = (length - 1) // 2
        paired = node_vals.shape[:3] + (elements, 2) + node_vals.shape[4:]
        head_nodes = lax.slice_in_dim(node_vals, 0, 2 * elements, axis=3).reshape(paired)
        tail_nodes = lax.slice_in_dim(node_vals, 1, length, axis=3).reshape(paired)
        parts = [head_nodes[:, :, :, :, 0], head_nodes[:, :, :, :, 1], tail_nodes[:, :, :, :, 1]]
    return jnp.stack(parts, axis=1)

def gather_local(node_vals, linear):
    return split_dim(split_dim(split_dim(node_vals, linear), linear), linear)

def merge_dim(element_vals, linear):
    parts = [element_vals[:, j] for j in range(element_vals.shape[1])]
    if linear:
        return pad_dim(parts[0], 3, 0, 1) + pad_dim(parts[1], 3, 1, 0)
    elements = parts[0].shape[3]
    corner_nodes = pad_dim(parts[0], 3, 0, 1) + pad_dim(parts[2], 3, 1, 0)
    paired = jnp.stack([lax.slice_in_dim(corner_nodes, 0, elements, axis=3), parts[1]], axis=4)
    merged = paired.reshape(parts[1].shape[:3] + (2 * elements,) + parts[1].shape[4:])
    return jnp.concatenate([merged, lax.slice_in_dim(corner_nodes, elements, elements + 1, axis=3)], axis=3)

def scatter_local(element_vals, linear):
    return merge_dim(merge_dim(merge_dim(element_vals, linear), linear), linear)

def brinkman_field(design_levels):
    density = design_levels.astype(jnp.float32) / (LEVELS - 1)
    coeff_field = brinkman_peak * brinkman_shape * (1.0 - density) / (brinkman_shape + density)
    return coeff_field.reshape((1, 1, 1, 1) + design_levels.shape)

def state_terms(state_nodes):
    value_matrix, slope_matrix = table_set()[0:2]
    element_vals = gather_local(state_nodes, False)
    quad_vals = tensor(element_vals, value_matrix, value_matrix, value_matrix)
    grads = (tensor(element_vals, slope_matrix, value_matrix, value_matrix), tensor(element_vals, value_matrix, slope_matrix, value_matrix), tensor(element_vals, value_matrix, value_matrix, slope_matrix))
    return (quad_vals, grads)

def element_terms(velocity_local, pressure_local, state_quad, state_grads, brinkman):
    value_matrix, slope_matrix, linear_matrix, value_back, slope_back, linear_back, weight_grid = table_set()
    weights = jnp.asarray(weight_grid, dtype=jnp.float32)
    vel_quad = tensor(velocity_local, value_matrix, value_matrix, value_matrix)
    vel_grads = (tensor(velocity_local, slope_matrix, value_matrix, value_matrix), tensor(velocity_local, value_matrix, slope_matrix, value_matrix), tensor(velocity_local, value_matrix, value_matrix, slope_matrix))
    pres_quad = tensor(pressure_local, linear_matrix, linear_matrix, linear_matrix)
    flux_terms = []
    for d in range(3):
        unit_column = jnp.asarray(np.eye(3)[:, d].reshape(3, 1, 1, 1, 1, 1, 1), dtype=jnp.float32)
        flux_terms.append(weights * (viscosity * vel_grads[d] + vel_quad * state_quad[d:d + 1] - pres_quad * unit_column))
    transfer = jnp.stack([lax.optimization_barrier(jnp.sum(state_grads[d] * vel_quad, axis=0)) for d in range(3)])
    source = weights * (transfer + brinkman * vel_quad)
    divergence = -weights * (vel_grads[0][0:1] + vel_grads[1][1:2] + vel_grads[2][2:3])
    vel_out = tensor(flux_terms[0], slope_back, value_back, value_back) + tensor(flux_terms[1], value_back, slope_back, value_back) + tensor(flux_terms[2], value_back, value_back, slope_back) + tensor(source, value_back, value_back, value_back)
    pres_out = tensor(divergence, linear_back, linear_back, linear_back)
    return (vel_out, pres_out)

def least_squares(hessenberg, initial_norm):
    upper = [list(entries) for entries in hessenberg]
    target = [initial_norm] + [jnp.zeros((), jnp.float32) for j in range(ITERS)]
    for column in range(ITERS):
        diagonal = upper[column][column]
        below = upper[column + 1][column]
        radius = jnp.sqrt(diagonal * diagonal + below * below)
        cosine = diagonal / radius
        sine_part = below / radius
        for j in range(column, ITERS):
            upper_val = upper[column][j]
            lower_val = upper[column + 1][j]
            upper[column][j] = cosine * upper_val + sine_part * lower_val
            upper[column + 1][j] = cosine * lower_val - sine_part * upper_val
        upper_val = target[column]
        lower_val = target[column + 1]
        target[column] = cosine * upper_val + sine_part * lower_val
        target[column + 1] = cosine * lower_val - sine_part * upper_val
    coeffs = [None] * ITERS
    for column in reversed(range(ITERS)):
        running = target[column]
        for j in range(column + 1, ITERS):
            running = running - upper[column][j] * coeffs[j]
        coeffs[column] = running / upper[column][column]
    return coeffs

def pad_top(values):
    return jnp.pad(values, ((0, 0), (0, 1), (0, 1), (0, 1)))

def join_blocks(stacked, span):
    blocks = stacked.shape[0]
    main_planes = jnp.moveaxis(lax.slice_in_dim(stacked, 0, span, axis=stacked.ndim - 1), 0, -2)
    tail_planes = jnp.moveaxis(stacked[..., span], 0, -1)
    zero_plane = jnp.zeros(tail_planes.shape[:-1] + (1,), stacked.dtype)
    shifted = jnp.concatenate([zero_plane, tail_planes], axis=-1)
    full_planes = jnp.concatenate([main_planes, jnp.zeros(main_planes.shape[:-2] + (1, span), stacked.dtype)], axis=-2)
    full_planes = full_planes.at[..., 0].add(shifted)
    flat = full_planes.reshape(full_planes.shape[:-2] + ((blocks + 1) * span,))
    return flat[..., :blocks * span + 1]

def inner_product(first_pair, second_pair):
    return jnp.sum(first_pair[0] * second_pair[0]) + jnp.sum(first_pair[1] * second_pair[1])

def reference(state_velocity, objective_gradient, wall_flags, design_levels):
    state_nodes = pad_top(state_velocity)
    right_side = pad_top(objective_gradient)
    keep_velocity = pad_top((1.0 - wall_flags.astype(jnp.float32))[None])
    keep_pressure = pad_top(jnp.ones((1,) + design_levels.shape, jnp.float32))
    brinkman = brinkman_field(design_levels)
    right_pressure = jnp.zeros_like(keep_pressure)

    def operate(velocity, pressure):
        masked = keep_velocity * velocity

        def one_block(block_index):
            node_start = block_index * (2 * EZ)
            vel_block = lax.dynamic_slice_in_dim(masked, node_start, 2 * EZ + 1, axis=3)
            state_block = lax.dynamic_slice_in_dim(state_nodes, node_start, 2 * EZ + 1, axis=3)
            pres_block = lax.dynamic_slice_in_dim(pressure, block_index * EZ, EZ + 1, axis=3)
            brink_block = lax.dynamic_slice_in_dim(brinkman, block_index * EZ, EZ, axis=6)
            state_quad, state_grads = state_terms(state_block)
            vel_out, pres_out = element_terms(gather_local(vel_block, False), gather_local(pres_block, True), state_quad, state_grads, brink_block)
            return (scatter_local(vel_out, False), scatter_local(pres_out, True))
        stacked_vel, stacked_pres = lax.map(one_block, jnp.arange(N_GZ, dtype=jnp.int32))
        vel_sum = join_blocks(stacked_vel, 2 * EZ)
        pres_sum = join_blocks(stacked_pres, EZ)
        return (keep_velocity * vel_sum + (1.0 - keep_velocity) * velocity, keep_pressure * pres_sum)
    start_pair = (right_side, right_pressure)
    initial_norm = jnp.sqrt(inner_product(start_pair, start_pair))
    krylov_basis = [(right_side / initial_norm, right_pressure / initial_norm)]
    hessenberg = [[jnp.zeros((), jnp.float32) for j in range(ITERS)] for i in range(ITERS + 1)]
    for k in range(ITERS):
        image_pair = operate(krylov_basis[k][0], krylov_basis[k][1])
        projections = [inner_product(image_pair, krylov_basis[i]) for i in range(k + 1)]
        remainder = inner_product(image_pair, image_pair)
        for i in range(k + 1):
            remainder = remainder - projections[i] * projections[i]
        next_norm = jnp.sqrt(remainder)
        for i in range(k + 1):
            hessenberg[i][k] = projections[i]
        hessenberg[k + 1][k] = next_norm
        if k + 1 < ITERS:
            new_vel, new_pres = image_pair
            for i in range(k + 1):
                new_vel = new_vel - projections[i] * krylov_basis[i][0]
                new_pres = new_pres - projections[i] * krylov_basis[i][1]
            krylov_basis.append((new_vel / next_norm, new_pres / next_norm))
    coeffs = least_squares(hessenberg, initial_norm)
    result_vel = coeffs[0] * krylov_basis[0][0]
    result_pres = coeffs[0] * krylov_basis[0][1]
    for i in range(1, ITERS):
        result_vel = result_vel + coeffs[i] * krylov_basis[i][0]
        result_pres = result_pres + coeffs[i] * krylov_basis[i][1]
    return (result_vel[:, :-1, :-1, :-1], result_pres[0, :-1, :-1, :-1])
```

```python
import functools
import itertools
import math

import jax
import jax.numpy as jnp
from jax import lax
from jax.experimental import pallas as pl
from jax.experimental.pallas import tpu as pltpu
from jax.sharding import PartitionSpec as P

MESH = pl.DeviceIdType.MESH
F32 = jnp.float32
HIGHEST = lax.Precision.HIGHEST

LEVELS = 9
PEAK = 8.0
SHAPE = 0.1

OFFSET = math.sqrt(0.15)
RATIO = 5.0 / 8.0
SCALE = (8.0 / 18.0) ** 3

NEAR = [o for o in itertools.product((-1, 0, 1), repeat=3) if o != (0, 0, 0)]
PLANE = [o for o in NEAR if o[2] == 0]

SOURCE = {-1: (2, 4), 0: (0, 4), 1: (0, 3)}
TARGET = {-1: (0, 2), 0: (2, 6), 1: (6, 9)}


def forward_both(a, b, c):
    d = c - a
    w = (b + b) - (a + c)
    s = (4.0 * OFFSET) * w
    m = b - 0.3 * w
    e = OFFSET * d
    return (m - e, b, m + e), (d + s, d, d - s)


def forward_value(a, b, c):
    d = c - a
    w = (b + b) - (a + c)
    m = b - 0.3 * w
    e = OFFSET * d
    return (m - e, b, m + e)


def back_value(f):
    s = f[0] + f[2]
    a = (0.3 * RATIO) * s
    b = (OFFSET * RATIO) * (f[2] - f[0])
    return (a - b, f[1] + (0.4 * RATIO) * s, a + b)


def back_both(f, g):
    s = f[0] + f[2]
    b = (OFFSET * RATIO) * (f[2] - f[0]) + (RATIO * (g[0] + g[2]) + g[1])
    w = (4.0 * OFFSET * RATIO) * (g[0] - g[2])
    a = (0.3 * RATIO) * s - w
    return (a - b, f[1] + (0.4 * RATIO) * s + (w + w), a + b)


def forward_linear(a, b):
    m = 0.5 * (a + b)
    d = OFFSET * (b - a)
    return (m - d, m, m + d)


def back_linear(f):
    m = (0.5 * RATIO) * (f[0] + f[2]) + 0.5 * f[1]
    d = (OFFSET * RATIO) * (f[2] - f[0])
    return (m - d, m + d)


def next_lane(v):
    return pltpu.roll(v, 127, 1)


def last_lane(v):
    return pltpu.roll(v, 1, 1)


def next_row(v):
    return pltpu.roll(v, 7, 0)


def last_row(v):
    return pltpu.roll(v, 1, 0)


def half_turn(v):
    return pltpu.roll(v, 4, 0)


def spread(elements, chunk, fields):
    def one(ci, carry):
        along = []
        for j in range(3):
            even = elements[chunk, ci, j, 0]
            along.append(forward_both(even, elements[chunk, ci, j, 1], next_lane(even)))
        for q in range(3):
            value, slope = forward_both(*[along[j][0][q] for j in range(3)])
            zslope = forward_value(*[along[j][1][q] for j in range(3)])
            for p in range(3):
                fields[ci, 0, p * 3 + q] = value[p]
                fields[ci, 1, p * 3 + q] = slope[p]
                fields[ci, 2, p * 3 + q] = zslope[p]
        return carry

    lax.fori_loop(0, 9, one, 0)


def at_points(fields, line, c):
    value, xslope = forward_both(*[fields[c * 3 + i, 0, line] for i in range(3)])
    yslope = forward_value(*[fields[c * 3 + i, 1, line] for i in range(3)])
    zslope = forward_value(*[fields[c * 3 + i, 2, line] for i in range(3)])
    return value, xslope, yslope, zslope


def apply_operator(above_floor, elements, pressures, chunk, state, slopes, fields, qpoints, ppoints, out, pout):
    spread(elements, chunk, fields)
    if pressures is not None:
        corner = {}
        for i in range(2):
            for j in range(2):
                low = pressures[chunk, i * 2 + j]
                corner[i, j] = forward_linear(low, next_lane(low))
        for q in range(3):
            sides = [forward_linear(corner[i, 0][q], corner[i, 1][q]) for i in range(2)]
            for p in range(3):
                points = forward_linear(sides[0][p], sides[1][p])
                for r in range(3):
                    qpoints[p * 3 + q, r] = points[r]

    def one(line, carry):
        value, slope = [], []
        for c in range(3):
            v, gx, gy, gz = at_points(fields, line, c)
            value.append(v)
            slope.append((gx, gy, gz))
        force = [[None] * 3 for _ in range(3)]
        flux = [[[None] * 3 for _ in range(3)] for _ in range(3)]
        for r in range(3):
            ppoints[line, r] = slope[0][0][r] + slope[1][1][r] + slope[2][2][r]
            wind = [state[chunk, line, r, b] for b in range(3)]
            pressure = qpoints[line, r] if pressures is not None else None
            for a in range(3):
                for b in range(3):
                    g = slope[a][b][r] + value[a][r] * wind[b]
                    if a == b and pressures is not None:
                        g = g - pressure
                    flux[a][b][r] = g
                total = slopes[chunk, line, r, a * 3] * value[0][r]
                for c in range(1, 3):
                    total = total + slopes[chunk, line, r, a * 3 + c] * value[c][r]
                force[a][r] = total
        for c in range(3):
            first = back_both(force[c], flux[c][0])
            second = back_value(flux[c][1])
            third = back_value(flux[c][2])
            for i in range(3):
                fields[c * 3 + i, 0, line] = first[i]
                fields[c * 3 + i, 1, line] = second[i]
                fields[c * 3 + i, 2, line] = third[i]
        return carry

    lax.fori_loop(0, 9, one, 0)

    def gather(ci, carry):
        value, zslope = [], []
        for q in range(3):
            value.append(
                back_both(
                    [fields[ci, 0, p * 3 + q] for p in range(3)],
                    [fields[ci, 1, p * 3 + q] for p in range(3)],
                )
            )
            zslope.append(back_value([fields[ci, 2, p * 3 + q] for p in range(3)]))
        for j in range(3):
            nodes = back_both([value[q][j] for q in range(3)], [zslope[q][j] for q in range(3)])
            out[chunk, ci, j, 0] = nodes[0] + last_lane(jnp.where(above_floor, nodes[2], 0.0))
            out[chunk, ci, j, 1] = nodes[1]
        return carry

    lax.fori_loop(0, 9, gather, 0)
    rows = {}
    for q in range(3):
        sides = []
        for p in range(3):
            sides.append(back_linear([ppoints[p * 3 + q, r] for r in range(3)]))
        for i in range(2):
            rows[i, q] = back_linear([sides[p][i] for p in range(3)])
    for i in range(2):
        for j in range(2):
            low, high = back_linear([rows[i, q][j] for q in range(3)])
            pout[chunk, i * 2 + j] = low + last_lane(jnp.where(above_floor, high, 0.0))


def pick(row, k):
    lane = lax.broadcasted_iota(jnp.int32, (1, 128), 1)
    return jnp.sum(jnp.where(lane == k, row, 0.0), axis=1, keepdims=True)


def solve(row):
    entries = {}
    at = 0
    for i in range(4):
        for j in range(i, 4):
            entries[i, j] = pick(row, at) + pick(row, 10)
            at += 1
    m = [[entries[min(i, j), max(i, j)] for j in range(1, 4)] + [entries[0, i]] for i in range(1, 4)]
    for k in range(2):
        inverse = 1.0 / m[k][k]
        for i in range(k + 1, 3):
            factor = m[i][k] * inverse
            for j in range(k + 1, 4):
                m[i][j] = m[i][j] - factor * m[k][j]
    t = [None] * 3
    for k in (2, 1, 0):
        total = m[k][3]
        for j in range(k + 1, 3):
            total = total - m[k][j] * t[j]
        t[k] = total / m[k][k]
    return t


def kernel(sizes, state_in, grad_in, wall_in, level_in, vel_out, pres_out,
           raw, nodes, ends, reach, even, odd, stiff, u0, us, u1, u2, u3, p1, p2, p3, keep_e, friction,
           wind, slopes, fields, qpoints, ppoints, out, pout, block, side, natural, plane_sum, line_sum,
           near_send, near_recv, part_send, part_recv, plane_send, plane_recv, line_send, line_recv):
    gx, gy, gz = lax.axis_index("gx"), lax.axis_index("gy"), lax.axis_index("gz")

    def device(o):
        return tuple(lax.rem(a + d + n, n) for a, d, n in zip((gx, gy, gz), o, sizes))

    others = [(a, b, 0) for a in range(sizes[0]) for b in range(sizes[1]) if (a, b) != (0, 0)]
    along = [(0, 0, d) for d in range(1, sizes[2])]
    partners = {tuple(d % n for d, n in zip(o, sizes)) for o in NEAR + others + along}
    partners = sorted(partners - {(0, 0, 0)})

    side[...] = jnp.zeros_like(side)
    plane_sum[...] = jnp.zeros_like(plane_sum)
    line_sum[...] = jnp.zeros_like(line_sum)

    barrier = pltpu.get_barrier_semaphore()
    for o in partners:
        pl.semaphore_signal(barrier, inc=1, device_id=device(o), device_id_type=MESH)

    lane = lax.broadcasted_iota(jnp.int32, (8, 128), 1)
    sub = lax.broadcasted_iota(jnp.int32, (8, 128), 0)

    for x in range(4):
        spot = pl.ds((x % 2) * 4, 4)
        mask = 1.0 - wall_in[x].astype(F32)
        for c in range(3):
            raw[c, x // 2, spot] = mask * grad_in[c, x]
            raw[3 + c, x // 2, spot] = state_in[c, x]
        raw[6, x // 2, spot] = mask
    rows = lax.broadcasted_iota(jnp.int32, (128, 128), 0)
    cols = lax.broadcasted_iota(jnp.int32, (128, 128), 1)
    split = (rows == jnp.where(cols < 64, 2 * cols, 2 * cols - 127)).astype(F32)
    join = (cols == jnp.where(rows < 64, 2 * rows, 2 * rows - 127)).astype(F32)
    parted = jnp.dot(raw[0:7].reshape(112, 128), split, precision=HIGHEST, preferred_element_type=F32)
    parted = parted.reshape(7, 2, 8, 128)
    twice = (rows[:64] == jnp.where(cols[:64] < 64, cols[:64], cols[:64] - 64)).astype(F32)
    density = level_in[...].astype(F32) / (LEVELS - 1)
    drag = PEAK * SHAPE * (1.0 - density) / (SHAPE + density)
    for h in range(2):
        wide = jnp.dot(drag[h], twice, precision=HIGHEST, preferred_element_type=F32)
        for y in range(4):
            raw[7, h, y : y + 1] = wide[y // 2 : y // 2 + 1]
            raw[7, h, y + 4 : y + 5] = wide[y // 2 : y // 2 + 1]
    for h in range(2):
        first = jnp.zeros((8, 128), F32)
        last = jnp.zeros((8, 128), F32)
        for f in range(8):
            v = raw[7, h] if f == 6 else parted[6 if f == 7 else f, h]
            for xl in range(2):
                nodes[f, 2 + 2 * h + xl, 2:6] = v[4 * xl : 4 * xl + 4]
            go = 8 * f
            lower = (lane >= go) & (lane < go + 4)
            upper = (lane >= go + 4) & (lane < go + 8)
            first = jnp.where(lower, pltpu.roll(v, go, 1), first)
            first = jnp.where(upper, pltpu.roll(v, (go + 4 - 64) % 128, 1), first)
            last = jnp.where(lower, pltpu.roll(v, (go - 60) % 128, 1), last)
            last = jnp.where(upper, pltpu.roll(v, (go + 4 - 124) % 128, 1), last)
        for xl in range(2):
            ends[0, 2 * h + xl, 0:4] = last[4 * xl : 4 * xl + 4]
            ends[1, 2 * h + xl, 0:4] = first[4 * xl : 4 * xl + 4]

    pl.semaphore_wait(barrier, len(partners))

    sent = []
    received = []
    for n, o in enumerate(NEAR):
        sx, sy = -o[0], -o[1]
        (xs, xe), (ys, ye) = SOURCE[sx], SOURCE[sy]
        (tx, te), (ty, tf) = TARGET[sx], TARGET[sy]
        if o[2] == 0:
            top = 8 if sx >= 0 and sy >= 0 else 7
            source = nodes.at[0:top, 2 + xs : 2 + xe, 2 + ys : 2 + ye]
            target = nodes.at[0:top, tx:te, ty:tf]
        else:
            which = 0 if o[2] == 1 else 1
            source = ends.at[which, xs:xe, ys:ye]
            target = reach.at[which, tx:te, ty:tf]
        copy = pltpu.make_async_remote_copy(
            src_ref=source, dst_ref=target, send_sem=near_send.at[n], recv_sem=near_recv.at[n],
            device_id=device(o), device_id_type=MESH)
        copy.start()
        sent.append(copy)
        received.append(copy)

    ey = sub % 4 - 1
    z = jnp.where(lane < 96, lane, lane - 128)
    zmin = jnp.where(gz > 0, -3, 0)
    zmax = jnp.where(gz < sizes[2] - 1, 65, 63)
    in_z = (z >= zmin) & (z <= zmax)
    ymin = jnp.where(gy > 0, -1, 0)
    ymax = jnp.where(gy < sizes[1] - 1, 2, 1)
    xmin = jnp.where(gx > 0, -1, 0)
    xmax = jnp.where(gx < sizes[0] - 1, 2, 1)
    ex = [jnp.where(sub < 4, 0, 1), jnp.where(sub < 4, 2, -1)]
    real = [in_z & (ey >= ymin) & (ey <= ymax) & (e >= xmin) & (e <= xmax) for e in ex]
    narrow = [r & (ey <= 1) & (e <= 1) for r, e in zip(real, ex)]
    own_y = (ey >= 0) & (ey <= 1)
    own_wide = in_z & own_y
    own = own_y & (lane < 64)
    zlim = jnp.where(gz < sizes[2] - 1, 64, 96)
    node_z = (lane < 64) | (lane >= zlim)
    above_floor = lane < jnp.where(gz > 0, 128, 96)
    ylim = jnp.where(gy < sizes[1] - 1, 99, 6)
    xlim = jnp.where(gx < sizes[0] - 1, 99, 6)
    node_yz = [node_z & (sub + 8 * h < ylim) for h in range(2)]

    for copy in received:
        copy.wait_recv()

    def widen(x, carry):
        inside = jnp.where(x < xlim, 1.0, 0.0).astype(F32)
        for h in range(2):
            rows8 = pl.ds(8 * h, 8)
            below = reach[0, x, rows8]
            above = reach[1, x, rows8]
            for f in range(8 if h == 0 else 6):
                v = nodes[f, x, rows8]
                go = 8 * f
                e = jnp.where(lane < 96, pltpu.roll(above, (64 - go) % 128, 1), pltpu.roll(below, (124 - go) % 128, 1))
                e = jnp.where(lane < 64, v, e)
                if f == 6:
                    stiff[0, x] = e
                    continue
                ok = node_yz[h]
                if f == 7:
                    ok = ok & (sub >= 2) & (sub < 7)
                even[f, x, rows8] = jnp.where(ok, e * inside, 0.0)
                o = jnp.where(lane < 96, pltpu.roll(above, (60 - go) % 128, 1), pltpu.roll(below, (120 - go) % 128, 1))
                o = jnp.where(lane < 64, pltpu.roll(v, 64, 1), o)
                odd[f, x, rows8] = jnp.where(ok, o * inside, 0.0)
        return carry

    lax.fori_loop(0, 9, widen, 0)

    def to_elements(source, f, x, j):
        return source[f, x, pl.ds(j, 4, stride=2), :]

    def collect(first, target, masks):
        def one(ci, carry):
            c, i = ci // 3, ci % 3
            for j in range(3):
                for k, source in enumerate((even, odd)):
                    for chunk, (low, high) in enumerate(((2, 4), (6, 0))):
                        v = jnp.concatenate(
                            [to_elements(source, first + c, low + i, j), to_elements(source, first + c, high + i, j)], axis=0)
                        if masks is not None:
                            v = jnp.where(masks[chunk], v, 0.0)
                        target[chunk, ci, j, k] = v
            return carry

        lax.fori_loop(0, 9, one, 0)

    collect(0, u0, real)
    collect(3, us, None)
    for i in range(3):
        for j in range(3):
            for k, source in enumerate((even, odd)):
                keep_e[i, j, k] = SCALE * jnp.concatenate(
                    [to_elements(source, 7, 2 + i, j), to_elements(source, 7, 4 + i, j)], axis=0)
    for chunk, (low, high) in enumerate(((2, 4), (6, 0))):
        friction[chunk] = jnp.concatenate([to_elements(stiff, 0, low, 0), to_elements(stiff, 0, high, 0)], axis=0)

    def prepare(chunk, carry):
        spread(us, chunk, fields)

        def one(line, inner):
            for c in range(3):
                v, gx_, gy_, gz_ = at_points(fields, line, c)
                for r in range(3):
                    wind[chunk, line, r, c] = v[r]
                    for b, g in enumerate((gx_, gy_, gz_)):
                        slopes[chunk, line, r, b * 3 + c] = g[r] + friction[chunk] if b == c else g[r]
            return inner

        lax.fori_loop(0, 9, one, 0)
        return carry

    lax.fori_loop(0, 2, prepare, 0)

    def first_step(chunk, carry):
        apply_operator(above_floor, u0, None, chunk, wind, slopes, fields, qpoints, ppoints, out, pout)
        return carry

    lax.fori_loop(0, 2, first_step, 0)

    low_half = sub < 4

    def owners(source, at, last):
        total = {}
        for chunk in range(2):
            for i in range(last + 1):
                v = [at(source, chunk, i, j) for j in range(last + 1)]
                total[chunk, i, 0] = v[0] + last_row(v[last])
                for j in range(1, last):
                    total[chunk, i, j] = v[j]
        return total

    def close(total, last):
        full = {}
        edge = {}
        for j in range(last):
            before = half_turn(total[1, last, j])
            mine = half_turn(total[0, last, j])
            full[0, j] = total[0, 0, j] + jnp.where(low_half, before, mine)
            edge[j] = total[1, 0, j] + mine
            for i in range(1, last):
                full[i, j] = total[0, i, j]
        return full, edge

    def complete(full, edge, last):
        for j in range(last):
            full[last, j] = jnp.where(low_half, half_turn(full[0, j]), half_turn(edge[j]))
        for i in range(last + 1):
            full[i, last] = next_row(full[i, 0])
        return full

    def finish_first(c, carry):
        for k in range(2):
            total = owners(out, lambda s, chunk, i, j: s[chunk, c * 3 + i, j, k], 2)
            full = complete(*close(total, 2), 2)
            for i in range(3):
                for j in range(3):
                    u1[0, c * 3 + i, j, k] = jnp.where(own_wide, full[i, j] * keep_e[i, j, k], 0.0)
        return carry

    lax.fori_loop(0, 3, finish_first, 0)

    def vertex_mask(i, j):
        ok = own_wide & ((lane < 64) | (lane >= zlim))
        ylast = jnp.where(gy < sizes[1] - 1, 99, 2)
        xlast = jnp.where(gx < sizes[0] - 1, 99, 2)
        return ok & (ey + j < ylast) & (ex[0] + i < xlast)

    full = complete(*close(owners(pout, lambda s, chunk, i, j: s[chunk, i * 2 + j], 1), 1), 1)
    for i in range(2):
        for j in range(2):
            p1[0, i * 2 + j] = jnp.where(vertex_mask(i, j), -SCALE * full[i, j], 0.0)

    apply_operator(above_floor, u1, p1, 0, wind, slopes, fields, qpoints, ppoints, out, pout)

    def store_rows(plane, x, parity, v, step):
        block[plane, x, pl.ds(parity, 4, stride=step), :] = v

    for n in range(7):
        last = 2 if n < 6 else 1
        c, k = n // 2, n % 2

        def at(i, j):
            return out[0, c * 3 + i, j, k] if n < 6 else pout[0, i * 2 + j]

        for j in range(last):
            v = [at(i, 0) + last_row(at(i, last)) if j == 0 else at(i, j) for i in range(last + 1)]
            if n == 6:
                v = [-SCALE * w for w in v]
            step = 2 // last
            turned = [half_turn(w) for w in v]
            for i in range(last):
                store_rows(n, step * i, j, v[i][0:4], 2)
            store_rows(n, 2, j, (v[last] + turned[0])[0:4], 2)
            for i in range(1, last):
                store_rows(n, 2 + i, j, turned[i][0:4], 2)
            store_rows(n, 4, j, turned[last][0:4], 2)
    vertex_yz = jnp.where(node_yz[0], 1.0, 0.0)
    for x in range(5):
        inside = jnp.where(x + 2 < xlim, 1.0, 0.0).astype(F32)
        for k, source in enumerate((even, odd)):
            mask = SCALE * source[7, x + 2, 0:8]
            for c in range(3):
                block[2 * c + k, x] = block[2 * c + k, x] * mask
        if x % 2 == 0:
            odd_rows = sub % 2 == 1
            block[6, x] = jnp.where(odd_rows, 0.0, block[6, x] * (vertex_yz * inside))
        else:
            block[6, x] = jnp.zeros((8, 128), F32)

    received = []
    for n, o in enumerate(PLANE):
        sx, sy = -o[0], -o[1]
        xs, xe = {-1: (2, 5), 0: (0, 5), 1: (0, 1)}[sx]
        ys, ty, count = {-1: (4, 0, 3), 0: (0, 0, 8), 1: (2, 6, 1)}[sy]
        copy = pltpu.make_async_remote_copy(
            src_ref=block.at[:, xs:xe, ys : ys + count], dst_ref=side.at[n, :, 0 : xe - xs, ty : ty + count],
            send_sem=part_send.at[n], recv_sem=part_recv.at[n], device_id=device(o), device_id_type=MESH)
        copy.start()
        sent.append(copy)
        received.append(copy)

    have = {0: 1.0}
    have_x = {-1: jnp.where(gx > 0, 1.0, 0.0).astype(F32), 1: jnp.where(gx < sizes[0] - 1, 1.0, 0.0).astype(F32)}
    have_y = {-1: jnp.where(gy > 0, 1.0, 0.0).astype(F32), 1: jnp.where(gy < sizes[1] - 1, 1.0, 0.0).astype(F32)}
    for copy in received:
        copy.wait_recv()

    def part(n, plane, x):
        sx, sy = -PLANE[n][0], -PLANE[n][1]
        v = side[n, plane, x]
        if sx:
            v = v * have_x[sx]
        if sy:
            v = v * have_y[sy]
        return v

    slot = {(-o[0], -o[1]): n for n, o in enumerate(PLANE)}

    def join_parts(plane, target, f):
        for x in range(7):
            total = block[plane, x - 2] if x >= 2 else None
            for sx in (-1, 0, 1):
                lo, hi = {-1: (0, 2), 0: (2, 6), 1: (6, 6)}[sx]
                if not lo <= x <= hi:
                    continue
                for sy in (-1, 0, 1):
                    if (sx, sy) != (0, 0):
                        v = part(slot[sx, sy], plane, x - lo)
                        total = v if total is None else total + v
            target[f, x, 0:8] = total

    def join_component(c, carry):
        join_parts(2 * c, even, c)
        join_parts(2 * c + 1, odd, c)
        return carry

    lax.fori_loop(0, 3, join_component, 0)
    join_parts(6, even, 3)
    collect(0, u2, narrow)
    for i in range(2):
        for j in range(2):
            for chunk, (low, high) in enumerate(((2, 4), (6, 0))):
                v = jnp.concatenate(
                    [to_elements(even, 3, low + 2 * i, 2 * j), to_elements(even, 3, high + 2 * i, 2 * j)], axis=0)
                p2[chunk, i * 2 + j] = jnp.where(narrow[chunk], v, 0.0)

    def last_step(chunk, carry):
        apply_operator(above_floor, u2, p2, chunk, wind, slopes, fields, qpoints, ppoints, out, pout)
        return carry

    lax.fori_loop(0, 2, last_step, 0)

    def finish_last(c, carry):
        for k in range(2):
            total = owners(out, lambda s, chunk, i, j: s[chunk, c * 3 + i, j, k], 2)
            full, _ = close(total, 2)
            for i in range(2):
                for j in range(2):
                    u3[0, c * 3 + i, j, k] = full[i, j] * keep_e[i, j, k]
        return carry

    lax.fori_loop(0, 3, finish_last, 0)
    full, _ = close(owners(pout, lambda s, chunk, i, j: s[chunk, i * 2 + j], 1), 1)
    p3[0, 0] = -SCALE * full[0, 0]

    pairs = [(i, j) for i in range(4) for j in range(i, 4)]

    def products(c, sums):
        sums = list(sums)
        for i in range(2):
            for j in range(2):
                for k in range(2):
                    v = [u[0, c * 3 + i, j, k] for u in (u0, u1, u2, u3)]
                    for n, (a, b) in enumerate(pairs):
                        sums[n] = sums[n] + v[a] * v[b]
        return tuple(sums)

    sums = list(lax.fori_loop(0, 3, products, tuple(jnp.zeros((8, 128), F32) for _ in pairs)))
    ps = [None, p1[0, 0], p2[0, 0], p3[0, 0]]
    for n, (a, b) in enumerate(pairs):
        if a:
            sums[n] = sums[n] + ps[a] * ps[b]
    fixed = jnp.zeros((4, 128), F32)
    for x in range(4):
        held = wall_in[x].astype(F32)
        for c in range(3):
            v = held * grad_in[c, x]
            fixed = fixed + v * v
    single = lane[0:1]
    row = jnp.zeros((1, 128), F32)
    for n in range(10):
        total = jnp.sum(jnp.sum(jnp.where(own, sums[n], 0.0), axis=0, keepdims=True), axis=1, keepdims=True)
        row = jnp.where(single == n, total, row)
    total = jnp.sum(jnp.sum(fixed, axis=0, keepdims=True), axis=1, keepdims=True)
    row = jnp.where(single == 10, total, row)

    def exchange(offsets, buffer, value, send_sems, recv_sems):
        buffer[0] = value
        copies = []
        for n, o in enumerate(offsets):
            copy = pltpu.make_async_remote_copy(
                src_ref=buffer.at[0], dst_ref=buffer.at[n + 1], send_sem=send_sems.at[n], recv_sem=recv_sems.at[n],
                device_id=device(o), device_id_type=MESH)
            copy.start()
            copies.append(copy)
        return copies

    def gathered(copies, buffer):
        for copy in copies:
            copy.wait_recv()
        total = buffer[0]
        for n in range(len(copies)):
            total = total + buffer[n + 1]
        return total

    copies = exchange(others, plane_sum, row, plane_send, plane_recv)
    sent += copies

    for n, u in enumerate((u1, u2)):
        for c in range(3):
            packed = []
            for i in range(2):
                for j in range(2):
                    packed.append(jnp.where(lane < 64, u[0, c * 3 + i, j, 0], pltpu.roll(u[0, c * 3 + i, j, 1], 64, 1)))
            flat = jnp.concatenate(packed, axis=0)
            flat = jnp.dot(flat, join, precision=HIGHEST, preferred_element_type=F32)
            for i in range(2):
                for j in range(2):
                    at8 = (i * 2 + j) * 8
                    for e in range(2):
                        natural[n, c, 2 * e + i, pl.ds(j, 2, stride=2), :] = flat[at8 + 4 * e + 1 : at8 + 4 * e + 3]

    row = gathered(copies, plane_sum)
    copies = exchange(along, line_sum, row, line_send, line_recv)
    sent += copies
    row = gathered(copies, line_sum)
    t = solve(row)
    for x in range(4):
        free = wall_in[x] == 0
        for c in range(3):
            b = grad_in[c, x]
            v = t[1] * natural[0, c, x, 0:4] + t[2] * natural[1, c, x, 0:4]
            vel_out[c, x] = jnp.where(free, t[0] * b, (t[0] + t[1] + t[2]) * b) + v
    v = t[1] * p1[0, 0] + t[2] * p2[0, 0]
    for e in range(2):
        pres_out[e] = v[4 * e + 1 : 4 * e + 3, 0:64]

    for copy in sent:
        copy.wait_send()


def local(sizes, state_velocity, objective_gradient, wall_flags, design_levels):
    vm = pltpu.VMEM
    plane, line = sizes[0] * sizes[1], sizes[2]
    tile = (8, 128)
    scratch = [
        vm((8, 2) + tile, F32),
        vm((8, 9, 16, 128), F32),
        vm((2, 4) + tile, F32),
        vm((2, 9, 16, 128), F32),
        vm((8, 9, 16, 128), F32),
        vm((8, 9, 16, 128), F32),
        vm((1, 9) + tile, F32),
        vm((2, 9, 3, 2) + tile, F32),
        vm((2, 9, 3, 2) + tile, F32),
        vm((1, 9, 3, 2) + tile, F32),
        vm((2, 9, 3, 2) + tile, F32),
        vm((1, 9, 3, 2) + tile, F32),
        vm((1, 4) + tile, F32),
        vm((2, 4) + tile, F32),
        vm((1, 1) + tile, F32),
        vm((3, 3, 2) + tile, F32),
        vm((2,) + tile, F32),
        vm((2, 9, 3, 3) + tile, F32),
        vm((2, 9, 3, 9) + tile, F32),
        vm((9, 3, 9) + tile, F32),
        vm((9, 3) + tile, F32),
        vm((9, 3) + tile, F32),
        vm((2, 9, 3, 2) + tile, F32),
        vm((2, 4) + tile, F32),
        vm((7, 5) + tile, F32),
        vm((8, 7, 5) + tile, F32),
        vm((2, 3, 4) + tile, F32),
        vm((plane, 1, 128), F32),
        vm((line, 1, 128), F32),
    ]
    for count in (26, 8, plane - 1, line - 1):
        scratch += [pltpu.SemaphoreType.DMA((count,))] * 2
    return pl.pallas_call(
        functools.partial(kernel, sizes),
        out_shape=(
            jax.ShapeDtypeStruct((3, 4, 4, 128), F32),
            jax.ShapeDtypeStruct((2, 2, 64), F32),
        ),
        in_specs=[pl.BlockSpec(memory_space=pltpu.VMEM)] * 4,
        out_specs=[pl.BlockSpec(memory_space=pltpu.VMEM)] * 2,
        scratch_shapes=scratch,
        compiler_params=pltpu.CompilerParams(
            collective_id=0, has_side_effects=True, vmem_limit_bytes=48 * 1024 * 1024
        ),
    )(state_velocity, objective_gradient, wall_flags, design_levels)


def solution(mesh):
    in_specs = (
        P(None, "gx", "gy", "gz"),
        P(None, "gx", "gy", "gz"),
        P("gx", "gy", "gz"),
        P("gx", "gy", "gz"),
    )
    out_specs = (P(None, "gx", "gy", "gz"), P("gx", "gy", "gz"))
    sizes = tuple(mesh.shape[a] for a in ("gx", "gy", "gz"))
    return jax.shard_map(
        functools.partial(local, sizes), mesh=mesh, in_specs=in_specs, out_specs=out_specs, check_vma=False
    )
```

```python
import functools
import itertools
import math

import jax
import jax.numpy as jnp
from jax import lax
from jax.experimental import pallas as pl
from jax.experimental.pallas import tpu as pltpu
from jax.sharding import PartitionSpec as P

MESH = pl.DeviceIdType.MESH
F32 = jnp.float32
HIGHEST = lax.Precision.HIGHEST

LEVELS = 9
PEAK = 8.0
SHAPE = 0.1

OFFSET = math.sqrt(0.15)
GREETED = 4

SPREAD = 3
LINES = 9
GATHER = 3

RATIO = 5.0 / 8.0
SCALE = (8.0 / 18.0) ** 3

NEAR = [o for o in itertools.product((-1, 0, 1), repeat=3) if o != (0, 0, 0)]
PLANE = [o for o in NEAR if o[2] == 0]

SOURCE = {-1: (2, 4), 0: (0, 4), 1: (0, 3)}
TARGET = {-1: (0, 2), 0: (2, 6), 1: (6, 9)}


def forward_both(a, b, c):
    d = c - a
    w = (b + b) - (a + c)
    s = (4.0 * OFFSET) * w
    m = b - 0.3 * w
    e = OFFSET * d
    return (m - e, b, m + e), (d + s, d, d - s)


def forward_value(a, b, c):
    d = c - a
    w = (b + b) - (a + c)
    m = b - 0.3 * w
    e = OFFSET * d
    return (m - e, b, m + e)


def back_value(f):
    s = f[0] + f[2]
    a = (0.3 * RATIO) * s
    b = (OFFSET * RATIO) * (f[2] - f[0])
    return (a - b, f[1] + (0.4 * RATIO) * s, a + b)


def back_both(f, g):
    s = f[0] + f[2]
    b = (OFFSET * RATIO) * (f[2] - f[0]) + (RATIO * (g[0] + g[2]) + g[1])
    w = (4.0 * OFFSET * RATIO) * (g[0] - g[2])
    a = (0.3 * RATIO) * s - w
    return (a - b, f[1] + (0.4 * RATIO) * s + (w + w), a + b)


def forward_linear(a, b):
    m = 0.5 * (a + b)
    d = OFFSET * (b - a)
    return (m - d, m, m + d)


def back_linear(f):
    m = (0.5 * RATIO) * (f[0] + f[2]) + 0.5 * f[1]
    d = (OFFSET * RATIO) * (f[2] - f[0])
    return (m - d, m + d)


def next_lane(v):
    return pltpu.roll(v, 127, v.ndim - 1)


def last_lane(v):
    return pltpu.roll(v, 1, v.ndim - 1)


def next_row(v):
    return pltpu.roll(v, 7, 0)


def last_row(v):
    return pltpu.roll(v, 1, 0)


def half_turn(v):
    return pltpu.roll(v, 4, 0)


def blocks(count, size, body):
    if size == count:
        body(0)
        return

    def one(n, carry):
        body(n * size)
        return carry

    lax.fori_loop(0, count // size, one, 0)


def spread(elements, chunk, fields):
    def one(c):
        at = pl.ds(c, SPREAD)
        along = []
        for j in range(3):
            even = elements[chunk, at, :, j, 0]
            along.append(forward_both(even, elements[chunk, at, :, j, 1], next_lane(even)))
        for q in range(3):
            value, slope = forward_both(*[along[j][0][q] for j in range(3)])
            zslope = forward_value(*[along[j][1][q] for j in range(3)])
            for p in range(3):
                fields[at, :, 0, p * 3 + q] = value[p]
                fields[at, :, 1, p * 3 + q] = slope[p]
                fields[at, :, 2, p * 3 + q] = zslope[p]

    blocks(3, SPREAD, one)


def at_points(fields, lines, c):
    value, xslope = forward_both(*[fields[c, i, 0, lines] for i in range(3)])
    yslope = forward_value(*[fields[c, i, 1, lines] for i in range(3)])
    zslope = forward_value(*[fields[c, i, 2, lines] for i in range(3)])
    return value, xslope, yslope, zslope


def apply_operator(above_floor, elements, pressures, chunk, state, slopes, fields, qpoints, ppoints, out, pout):
    spread(elements, chunk, fields)
    if pressures is not None:
        corner = {}
        for i in range(2):
            for j in range(2):
                low = pressures[chunk, i * 2 + j]
                corner[i, j] = forward_linear(low, next_lane(low))
        for q in range(3):
            sides = [forward_linear(corner[i, 0][q], corner[i, 1][q]) for i in range(2)]
            for p in range(3):
                points = forward_linear(sides[0][p], sides[1][p])
                for r in range(3):
                    qpoints[r, p * 3 + q] = points[r]

    def one(line):
        lines = pl.ds(line, LINES)
        value, slope = [], []
        for c in range(3):
            v, gx, gy, gz = at_points(fields, lines, c)
            value.append(v)
            slope.append((gx, gy, gz))
        force = [[None] * 3 for _ in range(3)]
        flux = [[[None] * 3 for _ in range(3)] for _ in range(3)]
        for r in range(3):
            ppoints[r, lines] = slope[0][0][r] + slope[1][1][r] + slope[2][2][r]
            wind = [state[chunk, r, b, lines] for b in range(3)]
            pressure = qpoints[r, lines] if pressures is not None else None
            for a in range(3):
                for b in range(3):
                    g = slope[a][b][r] + value[a][r] * wind[b]
                    if a == b and pressures is not None:
                        g = g - pressure
                    flux[a][b][r] = g
                total = slopes[chunk, r, a * 3, lines] * value[0][r]
                for c in range(1, 3):
                    total = total + slopes[chunk, r, a * 3 + c, lines] * value[c][r]
                force[a][r] = total
        for c in range(3):
            first = back_both(force[c], flux[c][0])
            second = back_value(flux[c][1])
            third = back_value(flux[c][2])
            for i in range(3):
                fields[c, i, 0, lines] = first[i]
                fields[c, i, 1, lines] = second[i]
                fields[c, i, 2, lines] = third[i]

    blocks(9, LINES, one)

    def gather(c):
        at = pl.ds(c, GATHER)
        value, zslope = [], []
        for q in range(3):
            value.append(
                back_both(
                    [fields[at, :, 0, p * 3 + q] for p in range(3)],
                    [fields[at, :, 1, p * 3 + q] for p in range(3)],
                )
            )
            zslope.append(back_value([fields[at, :, 2, p * 3 + q] for p in range(3)]))
        for j in range(3):
            nodes = back_both([value[q][j] for q in range(3)], [zslope[q][j] for q in range(3)])
            out[chunk, at, :, j, 0] = nodes[0] + last_lane(jnp.where(above_floor, nodes[2], 0.0))
            out[chunk, at, :, j, 1] = nodes[1]

    blocks(3, GATHER, gather)
    rows = {}
    for q in range(3):
        sides = []
        for p in range(3):
            sides.append(back_linear([ppoints[r, p * 3 + q] for r in range(3)]))
        for i in range(2):
            rows[i, q] = back_linear([sides[p][i] for p in range(3)])
    for i in range(2):
        for j in range(2):
            low, high = back_linear([rows[i, q][j] for q in range(3)])
            pout[chunk, i * 2 + j] = low + last_lane(jnp.where(above_floor, high, 0.0))


def pick(row, k):
    lane = lax.broadcasted_iota(jnp.int32, (1, 128), 1)
    return jnp.sum(jnp.where(lane == k, row, 0.0), axis=1, keepdims=True)


def solve(row):
    entries = {}
    at = 0
    for i in range(4):
        for j in range(i, 4):
            entries[i, j] = pick(row, at) + pick(row, 10)
            at += 1
    m = [[entries[min(i, j), max(i, j)] for j in range(1, 4)] + [entries[0, i]] for i in range(1, 4)]
    for k in range(2):
        inverse = 1.0 / m[k][k]
        for i in range(k + 1, 3):
            factor = m[i][k] * inverse
            for j in range(k + 1, 4):
                m[i][j] = m[i][j] - factor * m[k][j]
    t = [None] * 3
    for k in (2, 1, 0):
        total = m[k][3]
        for j in range(k + 1, 3):
            total = total - m[k][j] * t[j]
        t[k] = total / m[k][k]
    return t


def kernel(sizes, state_far, grad_far, wall_far, level_far, vel_out, pres_out,
           state_in, grad_in, wall_in, level_in, raw, nodes, ends, reach, even, odd, stiff, u0, us, u1, u2, u3, p1, p2, p3, keep_e, friction,
           wind, slopes, fields, qpoints, ppoints, out, pout, block, side, natural, plane_sum, line_sum,
           load, reached, near_send, near_recv, part_send, part_recv, plane_send, plane_recv, line_send, line_recv):
    loads = [
        pltpu.make_async_copy(far, near, load.at[n])
        for n, (far, near) in enumerate(
            ((grad_far, grad_in), (state_far, state_in), (wall_far, wall_in), (level_far, level_in)))
    ]
    for copy in loads:
        copy.start()

    gx, gy, gz = lax.axis_index("gx"), lax.axis_index("gy"), lax.axis_index("gz")

    def device(o):
        return tuple(lax.rem(a + d + n, n) for a, d, n in zip((gx, gy, gz), o, sizes))

    others = [(a, b, 0) for a in range(sizes[0]) for b in range(sizes[1]) if (a, b) != (0, 0)]
    along = [(0, 0, d) for d in range(1, sizes[2])]
    close_by = [(0, 0, d) for d in range(-GREETED, GREETED + 1)]
    partners = {tuple(d % n for d, n in zip(o, sizes)) for o in NEAR + others + close_by}
    partners = sorted(partners - {(0, 0, 0)})

    side[...] = jnp.zeros_like(side)

    barrier = pltpu.get_barrier_semaphore()
    for o in partners:
        pl.semaphore_signal(barrier, inc=1, device_id=device(o), device_id_type=MESH)

    lane = lax.broadcasted_iota(jnp.int32, (8, 128), 1)
    sub = lax.broadcasted_iota(jnp.int32, (8, 128), 0)

    for copy in loads:
        copy.wait()

    for x in range(4):
        spot = pl.ds((x % 2) * 4, 4)
        mask = 1.0 - wall_in[x].astype(F32)
        for c in range(3):
            raw[c, x // 2, spot] = mask * grad_in[c, x]
            raw[3 + c, x // 2, spot] = state_in[c, x]
        raw[6, x // 2, spot] = mask
    rows = lax.broadcasted_iota(jnp.int32, (128, 128), 0)
    cols = lax.broadcasted_iota(jnp.int32, (128, 128), 1)
    split = (rows == jnp.where(cols < 64, 2 * cols, 2 * cols - 127)).astype(F32)
    join = (cols == jnp.where(rows < 64, 2 * rows, 2 * rows - 127)).astype(F32)
    parted = jnp.dot(raw[0:7].reshape(112, 128), split, precision=HIGHEST, preferred_element_type=F32)
    parted = parted.reshape(7, 2, 8, 128)
    twice = (rows[:64] == jnp.where(cols[:64] < 64, cols[:64], cols[:64] - 64)).astype(F32)
    density = level_in[...].astype(F32) / (LEVELS - 1)
    drag = PEAK * SHAPE * (1.0 - density) / (SHAPE + density)
    for h in range(2):
        wide = jnp.dot(drag[h], twice, precision=HIGHEST, preferred_element_type=F32)
        for y in range(4):
            raw[7, h, y : y + 1] = wide[y // 2 : y // 2 + 1]
            raw[7, h, y + 4 : y + 5] = wide[y // 2 : y // 2 + 1]
    for h in range(2):
        first = jnp.zeros((8, 128), F32)
        last = jnp.zeros((8, 128), F32)
        for f in range(8):
            v = raw[7, h] if f == 6 else parted[6 if f == 7 else f, h]
            for xl in range(2):
                nodes[f, 2 + 2 * h + xl, 2:6] = v[4 * xl : 4 * xl + 4]
            go = 8 * f
            lower = (lane >= go) & (lane < go + 4)
            upper = (lane >= go + 4) & (lane < go + 8)
            first = jnp.where(lower, pltpu.roll(v, go, 1), first)
            first = jnp.where(upper, pltpu.roll(v, (go + 4 - 64) % 128, 1), first)
            last = jnp.where(lower, pltpu.roll(v, (go - 60) % 128, 1), last)
            last = jnp.where(upper, pltpu.roll(v, (go + 4 - 124) % 128, 1), last)
        for xl in range(2):
            ends[0, 2 * h + xl, 0:4] = last[4 * xl : 4 * xl + 4]
            ends[1, 2 * h + xl, 0:4] = first[4 * xl : 4 * xl + 4]

    pl.semaphore_wait(barrier, len(partners))

    def tell(n):
        for d in (-1, 1):
            pl.semaphore_signal(
                reached.at[n], inc=1, device_id=device((0, 0, d * GREETED * 2**n)), device_id_type=MESH)

    rounds = 0
    while GREETED * 2**rounds < sizes[2] // 2:
        rounds += 1
    if rounds:
        tell(0)

    sent = []
    received = []
    for n, o in enumerate(NEAR):
        sx, sy = -o[0], -o[1]
        (xs, xe), (ys, ye) = SOURCE[sx], SOURCE[sy]
        (tx, te), (ty, tf) = TARGET[sx], TARGET[sy]
        if o[2] == 0:
            top = 8 if sx >= 0 and sy >= 0 else 7
            source = nodes.at[0:top, 2 + xs : 2 + xe, 2 + ys : 2 + ye]
            target = nodes.at[0:top, tx:te, ty:tf]
        else:
            which = 0 if o[2] == 1 else 1
            source = ends.at[which, xs:xe, ys:ye]
            target = reach.at[which, tx:te, ty:tf]
        copy = pltpu.make_async_remote_copy(
            src_ref=source, dst_ref=target, send_sem=near_send.at[n], recv_sem=near_recv.at[n],
            device_id=device(o), device_id_type=MESH)
        copy.start()
        sent.append(copy)
        received.append(copy)

    ey = sub % 4 - 1
    z = jnp.where(lane < 96, lane, lane - 128)
    zmin = jnp.where(gz > 0, -3, 0)
    zmax = jnp.where(gz < sizes[2] - 1, 65, 63)
    in_z = (z >= zmin) & (z <= zmax)
    ymin = jnp.where(gy > 0, -1, 0)
    ymax = jnp.where(gy < sizes[1] - 1, 2, 1)
    xmin = jnp.where(gx > 0, -1, 0)
    xmax = jnp.where(gx < sizes[0] - 1, 2, 1)
    ex = [jnp.where(sub < 4, 0, 1), jnp.where(sub < 4, 2, -1)]
    real = [in_z & (ey >= ymin) & (ey <= ymax) & (e >= xmin) & (e <= xmax) for e in ex]
    narrow = [r & (ey <= 1) & (e <= 1) for r, e in zip(real, ex)]
    own_y = (ey >= 0) & (ey <= 1)
    own_wide = in_z & own_y
    own = own_y & (lane < 64)
    zlim = jnp.where(gz < sizes[2] - 1, 64, 96)
    node_z = (lane < 64) | (lane >= zlim)
    above_floor = lane < jnp.where(gz > 0, 128, 96)
    ylim = jnp.where(gy < sizes[1] - 1, 99, 6)
    xlim = jnp.where(gx < sizes[0] - 1, 99, 6)
    node_yz = [node_z & (sub + 8 * h < ylim) for h in range(2)]

    for copy in received:
        copy.wait_recv()
    for n in range(1, rounds):
        pl.semaphore_wait(reached.at[n - 1], 2)
        tell(n)

    def widen(x, carry):
        inside = jnp.where(x < xlim, 1.0, 0.0).astype(F32)
        for h in range(2):
            rows8 = pl.ds(8 * h, 8)
            below = reach[0, x, rows8]
            above = reach[1, x, rows8]
            for f in range(8 if h == 0 else 6):
                v = nodes[f, x, rows8]
                go = 8 * f
                e = jnp.where(lane < 96, pltpu.roll(above, (64 - go) % 128, 1), pltpu.roll(below, (124 - go) % 128, 1))
                e = jnp.where(lane < 64, v, e)
                if f == 6:
                    stiff[0, x] = e
                    continue
                ok = node_yz[h]
                if f == 7:
                    ok = ok & (sub >= 2) & (sub < 7)
                even[f, x, rows8] = jnp.where(ok, e * inside, 0.0)
                o = jnp.where(lane < 96, pltpu.roll(above, (60 - go) % 128, 1), pltpu.roll(below, (120 - go) % 128, 1))
                o = jnp.where(lane < 64, pltpu.roll(v, 64, 1), o)
                odd[f, x, rows8] = jnp.where(ok, o * inside, 0.0)
        return carry

    lax.fori_loop(0, 9, widen, 0)

    def to_elements(source, f, x, j):
        return source[f, x, pl.ds(j, 4, stride=2), :]

    def collect(first, target, masks):
        three = pl.ds(first, 3)
        for i in range(3):
            for j in range(3):
                for k, source in enumerate((even, odd)):
                    for chunk, (low, high) in enumerate(((2, 4), (6, 0))):
                        v = jnp.concatenate(
                            [to_elements(source, three, low + i, j), to_elements(source, three, high + i, j)], axis=1)
                        if masks is not None:
                            v = jnp.where(masks[chunk], v, 0.0)
                        target[chunk, :, i, j, k] = v

    collect(0, u0, real)
    collect(3, us, None)
    for i in range(3):
        for j in range(3):
            for k, source in enumerate((even, odd)):
                keep_e[i, j, k] = SCALE * jnp.concatenate(
                    [to_elements(source, 7, 2 + i, j), to_elements(source, 7, 4 + i, j)], axis=0)
    for chunk, (low, high) in enumerate(((2, 4), (6, 0))):
        friction[chunk] = jnp.concatenate([to_elements(stiff, 0, low, 0), to_elements(stiff, 0, high, 0)], axis=0)

    def prepare(chunk, carry):
        spread(us, chunk, fields)

        def one(line):
            lines = pl.ds(line, LINES)
            for c in range(3):
                v, gx_, gy_, gz_ = at_points(fields, lines, c)
                for r in range(3):
                    wind[chunk, r, c, lines] = v[r]
                    for b, g in enumerate((gx_, gy_, gz_)):
                        slopes[chunk, r, b * 3 + c, lines] = g[r] + friction[chunk] if b == c else g[r]

        blocks(9, LINES, one)
        return carry

    lax.fori_loop(0, 2, prepare, 0)

    def first_step(chunk, carry):
        apply_operator(above_floor, u0, None, chunk, wind, slopes, fields, qpoints, ppoints, out, pout)
        return carry

    lax.fori_loop(0, 2, first_step, 0)

    low_half = sub < 4

    def owners(source, at, last):
        total = {}
        for chunk in range(2):
            for i in range(last + 1):
                v = [at(source, chunk, i, j) for j in range(last + 1)]
                total[chunk, i, 0] = v[0] + last_row(v[last])
                for j in range(1, last):
                    total[chunk, i, j] = v[j]
        return total

    def close(total, last):
        full = {}
        edge = {}
        for j in range(last):
            before = half_turn(total[1, last, j])
            mine = half_turn(total[0, last, j])
            full[0, j] = total[0, 0, j] + jnp.where(low_half, before, mine)
            edge[j] = total[1, 0, j] + mine
            for i in range(1, last):
                full[i, j] = total[0, i, j]
        return full, edge

    def complete(full, edge, last):
        for j in range(last):
            full[last, j] = jnp.where(low_half, half_turn(full[0, j]), half_turn(edge[j]))
        for i in range(last + 1):
            full[i, last] = next_row(full[i, 0])
        return full

    def finish_first(c, carry):
        for k in range(2):
            total = owners(out, lambda s, chunk, i, j: s[chunk, c, i, j, k], 2)
            full = complete(*close(total, 2), 2)
            for i in range(3):
                for j in range(3):
                    u1[0, c, i, j, k] = jnp.where(own_wide, full[i, j] * keep_e[i, j, k], 0.0)
        return carry

    lax.fori_loop(0, 3, finish_first, 0)

    def vertex_mask(i, j):
        ok = own_wide & ((lane < 64) | (lane >= zlim))
        ylast = jnp.where(gy < sizes[1] - 1, 99, 2)
        xlast = jnp.where(gx < sizes[0] - 1, 99, 2)
        return ok & (ey + j < ylast) & (ex[0] + i < xlast)

    full = complete(*close(owners(pout, lambda s, chunk, i, j: s[chunk, i * 2 + j], 1), 1), 1)
    for i in range(2):
        for j in range(2):
            p1[0, i * 2 + j] = jnp.where(vertex_mask(i, j), -SCALE * full[i, j], 0.0)

    apply_operator(above_floor, u1, p1, 0, wind, slopes, fields, qpoints, ppoints, out, pout)

    def store_rows(plane, x, parity, v, step):
        block[plane, x, pl.ds(parity, 4, stride=step), :] = v

    for n in range(7):
        last = 2 if n < 6 else 1
        c, k = n // 2, n % 2

        def at(i, j):
            return out[0, c, i, j, k] if n < 6 else pout[0, i * 2 + j]

        for j in range(last):
            v = [at(i, 0) + last_row(at(i, last)) if j == 0 else at(i, j) for i in range(last + 1)]
            if n == 6:
                v = [-SCALE * w for w in v]
            step = 2 // last
            turned = [half_turn(w) for w in v]
            for i in range(last):
                store_rows(n, step * i, j, v[i][0:4], 2)
            store_rows(n, 2, j, (v[last] + turned[0])[0:4], 2)
            for i in range(1, last):
                store_rows(n, 2 + i, j, turned[i][0:4], 2)
            store_rows(n, 4, j, turned[last][0:4], 2)
    vertex_yz = jnp.where(node_yz[0], 1.0, 0.0)
    for x in range(5):
        inside = jnp.where(x + 2 < xlim, 1.0, 0.0).astype(F32)
        for k, source in enumerate((even, odd)):
            mask = SCALE * source[7, x + 2, 0:8]
            for c in range(3):
                block[2 * c + k, x] = block[2 * c + k, x] * mask
        if x % 2 == 0:
            odd_rows = sub % 2 == 1
            block[6, x] = jnp.where(odd_rows, 0.0, block[6, x] * (vertex_yz * inside))
        else:
            block[6, x] = jnp.zeros((8, 128), F32)

    received = []
    for n, o in enumerate(PLANE):
        sx, sy = -o[0], -o[1]
        xs, xe = {-1: (2, 5), 0: (0, 5), 1: (0, 1)}[sx]
        ys, ty, count = {-1: (4, 0, 3), 0: (0, 0, 8), 1: (2, 6, 1)}[sy]
        copy = pltpu.make_async_remote_copy(
            src_ref=block.at[:, xs:xe, ys : ys + count], dst_ref=side.at[n, :, 0 : xe - xs, ty : ty + count],
            send_sem=part_send.at[n], recv_sem=part_recv.at[n], device_id=device(o), device_id_type=MESH)
        copy.start()
        sent.append(copy)
        received.append(copy)

    have = {0: 1.0}
    have_x = {-1: jnp.where(gx > 0, 1.0, 0.0).astype(F32), 1: jnp.where(gx < sizes[0] - 1, 1.0, 0.0).astype(F32)}
    have_y = {-1: jnp.where(gy > 0, 1.0, 0.0).astype(F32), 1: jnp.where(gy < sizes[1] - 1, 1.0, 0.0).astype(F32)}
    for copy in received:
        copy.wait_recv()

    def part(n, plane, x):
        sx, sy = -PLANE[n][0], -PLANE[n][1]
        v = side[n, plane, x]
        if sx:
            v = v * have_x[sx]
        if sy:
            v = v * have_y[sy]
        return v

    slot = {(-o[0], -o[1]): n for n, o in enumerate(PLANE)}

    def join_parts(plane, target, f):
        for x in range(7):
            total = block[plane, x - 2] if x >= 2 else None
            for sx in (-1, 0, 1):
                lo, hi = {-1: (0, 2), 0: (2, 6), 1: (6, 6)}[sx]
                if not lo <= x <= hi:
                    continue
                for sy in (-1, 0, 1):
                    if (sx, sy) != (0, 0):
                        v = part(slot[sx, sy], plane, x - lo)
                        total = v if total is None else total + v
            target[f, x, 0:8] = total

    def join_component(c, carry):
        join_parts(2 * c, even, c)
        join_parts(2 * c + 1, odd, c)
        return carry

    lax.fori_loop(0, 3, join_component, 0)
    join_parts(6, even, 3)
    collect(0, u2, narrow)
    for i in range(2):
        for j in range(2):
            for chunk, (low, high) in enumerate(((2, 4), (6, 0))):
                v = jnp.concatenate(
                    [to_elements(even, 3, low + 2 * i, 2 * j), to_elements(even, 3, high + 2 * i, 2 * j)], axis=0)
                p2[chunk, i * 2 + j] = jnp.where(narrow[chunk], v, 0.0)

    def last_step(chunk, carry):
        apply_operator(above_floor, u2, p2, chunk, wind, slopes, fields, qpoints, ppoints, out, pout)
        return carry

    lax.fori_loop(0, 2, last_step, 0)

    def finish_last(c, carry):
        for k in range(2):
            total = owners(out, lambda s, chunk, i, j: s[chunk, c, i, j, k], 2)
            full, _ = close(total, 2)
            for i in range(2):
                for j in range(2):
                    u3[0, c, i, j, k] = full[i, j] * keep_e[i, j, k]
        return carry

    lax.fori_loop(0, 3, finish_last, 0)
    full, _ = close(owners(pout, lambda s, chunk, i, j: s[chunk, i * 2 + j], 1), 1)
    p3[0, 0] = -SCALE * full[0, 0]

    pairs = [(i, j) for i in range(4) for j in range(i, 4)]

    def products(c, sums):
        sums = list(sums)
        for i in range(2):
            for j in range(2):
                for k in range(2):
                    v = [u[0, c, i, j, k] for u in (u0, u1, u2, u3)]
                    for n, (a, b) in enumerate(pairs):
                        sums[n] = sums[n] + v[a] * v[b]
        return tuple(sums)

    sums = list(lax.fori_loop(0, 3, products, tuple(jnp.zeros((8, 128), F32) for _ in pairs)))
    ps = [None, p1[0, 0], p2[0, 0], p3[0, 0]]
    for n, (a, b) in enumerate(pairs):
        if a:
            sums[n] = sums[n] + ps[a] * ps[b]
    fixed = jnp.zeros((4, 128), F32)
    for x in range(4):
        held = wall_in[x].astype(F32)
        for c in range(3):
            v = held * grad_in[c, x]
            fixed = fixed + v * v
    single = lane[0:1]
    row = jnp.zeros((1, 128), F32)
    for n in range(10):
        total = jnp.sum(jnp.sum(jnp.where(own, sums[n], 0.0), axis=0, keepdims=True), axis=1, keepdims=True)
        row = jnp.where(single == n, total, row)
    total = jnp.sum(jnp.sum(fixed, axis=0, keepdims=True), axis=1, keepdims=True)
    row = jnp.where(single == 10, total, row)

    def exchange(offsets, buffer, value, send_sems, recv_sems):
        buffer[0] = value
        copies = []
        for n, o in enumerate(offsets):
            copy = pltpu.make_async_remote_copy(
                src_ref=buffer.at[0], dst_ref=buffer.at[n + 1], send_sem=send_sems.at[n], recv_sem=recv_sems.at[n],
                device_id=device(o), device_id_type=MESH)
            copy.start()
            copies.append(copy)
        return copies

    def gathered(copies, buffer):
        for copy in copies:
            copy.wait_recv()
        total = buffer[0]
        for n in range(len(copies)):
            total = total + buffer[n + 1]
        return total

    copies = exchange(others, plane_sum, row, plane_send, plane_recv)
    sent += copies

    for n, u in enumerate((u1, u2)):
        for c in range(3):
            packed = []
            for i in range(2):
                for j in range(2):
                    packed.append(jnp.where(lane < 64, u[0, c, i, j, 0], pltpu.roll(u[0, c, i, j, 1], 64, 1)))
            flat = jnp.concatenate(packed, axis=0)
            flat = jnp.dot(flat, join, precision=HIGHEST, preferred_element_type=F32)
            for i in range(2):
                for j in range(2):
                    at8 = (i * 2 + j) * 8
                    for e in range(2):
                        natural[n, c, 2 * e + i, pl.ds(j, 2, stride=2), :] = flat[at8 + 4 * e + 1 : at8 + 4 * e + 3]

    row = gathered(copies, plane_sum)
    if rounds:
        pl.semaphore_wait(reached.at[rounds - 1], 2)
    copies = exchange(along, line_sum, row, line_send, line_recv)
    sent += copies
    row = gathered(copies, line_sum)
    t = solve(row)
    for x in range(4):
        free = wall_in[x] == 0
        for c in range(3):
            b = grad_in[c, x]
            v = t[1] * natural[0, c, x, 0:4] + t[2] * natural[1, c, x, 0:4]
            vel_out[c, x] = jnp.where(free, t[0] * b, (t[0] + t[1] + t[2]) * b) + v
    v = t[1] * p1[0, 0] + t[2] * p2[0, 0]
    for e in range(2):
        pres_out[e] = v[4 * e + 1 : 4 * e + 3, 0:64]

    for copy in sent:
        copy.wait_send()


def local(sizes, state_velocity, objective_gradient, wall_flags, design_levels):
    vm = pltpu.VMEM
    plane, line = sizes[0] * sizes[1], sizes[2]
    tile = (8, 128)
    scratch = [
        vm((3, 4, 4, 128), F32),
        vm((3, 4, 4, 128), F32),
        vm((4, 4, 128), jnp.int32),
        vm((2, 2, 64), jnp.int32),
        vm((8, 2) + tile, F32),
        vm((8, 9, 16, 128), F32),
        vm((2, 4) + tile, F32),
        vm((2, 9, 16, 128), F32),
        vm((8, 9, 16, 128), F32),
        vm((8, 9, 16, 128), F32),
        vm((1, 9) + tile, F32),
        vm((2, 3, 3, 3, 2) + tile, F32),
        vm((2, 3, 3, 3, 2) + tile, F32),
        vm((1, 3, 3, 3, 2) + tile, F32),
        vm((2, 3, 3, 3, 2) + tile, F32),
        vm((1, 3, 3, 3, 2) + tile, F32),
        vm((1, 4) + tile, F32),
        vm((2, 4) + tile, F32),
        vm((1, 1) + tile, F32),
        vm((3, 3, 2) + tile, F32),
        vm((2,) + tile, F32),
        vm((2, 3, 3, 9) + tile, F32),
        vm((2, 3, 9, 9) + tile, F32),
        vm((3, 3, 3, 9) + tile, F32),
        vm((3, 9) + tile, F32),
        vm((3, 9) + tile, F32),
        vm((2, 3, 3, 3, 2) + tile, F32),
        vm((2, 4) + tile, F32),
        vm((7, 5) + tile, F32),
        vm((8, 7, 5) + tile, F32),
        vm((2, 3, 4) + tile, F32),
        vm((plane, 1, 128), F32),
        vm((line, 1, 128), F32),
    ]
    scratch += [pltpu.SemaphoreType.DMA((4,)), pltpu.SemaphoreType.REGULAR((4,))]
    for count in (26, 8, plane - 1, line - 1):
        scratch += [pltpu.SemaphoreType.DMA((count,))] * 2
    return pl.pallas_call(
        functools.partial(kernel, sizes),
        out_shape=(
            jax.ShapeDtypeStruct((3, 4, 4, 128), F32),
            jax.ShapeDtypeStruct((2, 2, 64), F32),
        ),
        in_specs=[pl.BlockSpec(memory_space=pl.ANY)] * 4,
        out_specs=[pl.BlockSpec(memory_space=pltpu.VMEM)] * 2,
        scratch_shapes=scratch,
        compiler_params=pltpu.CompilerParams(
            collective_id=0, has_side_effects=True, vmem_limit_bytes=56 * 1024 * 1024
        ),
    )(state_velocity, objective_gradient, wall_flags, design_levels)


def solution(mesh):
    in_specs = (
        P(None, "gx", "gy", "gz"),
        P(None, "gx", "gy", "gz"),
        P("gx", "gy", "gz"),
        P("gx", "gy", "gz"),
    )
    out_specs = (P(None, "gx", "gy", "gz"), P("gx", "gy", "gz"))
    sizes = tuple(mesh.shape[a] for a in ("gx", "gy", "gz"))
    return jax.shard_map(
        functools.partial(local, sizes), mesh=mesh, in_specs=in_specs, out_specs=out_specs, check_vma=False
    )
```

```python
import functools
import itertools
import math

import jax
import jax.numpy as jnp
from jax import lax
from jax.experimental import pallas as pl
from jax.experimental.pallas import tpu as pltpu
from jax.sharding import PartitionSpec as P

MESH = pl.DeviceIdType.MESH
F32 = jnp.float32
HIGHEST = lax.Precision.HIGHEST

LEVELS = 9
PEAK = 8.0
SHAPE = 0.1

OFFSET = math.sqrt(0.15)
SPREAD = 3
LINES = 9
GATHER = 3

RATIO = 5.0 / 8.0
SCALE = (8.0 / 18.0) ** 3

NEAR = [o for o in itertools.product((-1, 0, 1), repeat=3) if o != (0, 0, 0)]
NEAR.sort(key=lambda o: (o[2] == 0, -sum(map(abs, o))))
PLANE = [o for o in NEAR if o[2] == 0]

SOURCE = {-1: (2, 4), 0: (0, 4), 1: (0, 3)}
TARGET = {-1: (0, 2), 0: (2, 6), 1: (6, 9)}


def forward_both(a, b, c):
    d = c - a
    w = (b + b) - (a + c)
    s = (4.0 * OFFSET) * w
    m = b - 0.3 * w
    e = OFFSET * d
    return (m - e, b, m + e), (d + s, d, d - s)


def forward_value(a, b, c):
    d = c - a
    w = (b + b) - (a + c)
    m = b - 0.3 * w
    e = OFFSET * d
    return (m - e, b, m + e)


def back_value(f):
    s = f[0] + f[2]
    a = (0.3 * RATIO) * s
    b = (OFFSET * RATIO) * (f[2] - f[0])
    return (a - b, f[1] + (0.4 * RATIO) * s, a + b)


def back_both(f, g):
    s = f[0] + f[2]
    b = (OFFSET * RATIO) * (f[2] - f[0]) + (RATIO * (g[0] + g[2]) + g[1])
    w = (4.0 * OFFSET * RATIO) * (g[0] - g[2])
    a = (0.3 * RATIO) * s - w
    return (a - b, f[1] + (0.4 * RATIO) * s + (w + w), a + b)


def forward_linear(a, b):
    m = 0.5 * (a + b)
    d = OFFSET * (b - a)
    return (m - d, m, m + d)


def back_linear(f):
    m = (0.5 * RATIO) * (f[0] + f[2]) + 0.5 * f[1]
    d = (OFFSET * RATIO) * (f[2] - f[0])
    return (m - d, m + d)


def next_lane(v):
    return pltpu.roll(v, 127, v.ndim - 1)


def last_lane(v):
    return pltpu.roll(v, 1, v.ndim - 1)


def next_row(v):
    return pltpu.roll(v, 7, 0)


def last_row(v):
    return pltpu.roll(v, 1, 0)


def half_turn(v):
    return pltpu.roll(v, 4, 0)


def blocks(count, size, body):
    if size == count:
        body(0)
        return

    def one(n, carry):
        body(n * size)
        return carry

    lax.fori_loop(0, count // size, one, 0)


def spread(elements, chunk, fields):
    def one(c):
        at = pl.ds(c, SPREAD)
        along = []
        for j in range(3):
            even = elements[chunk, at, :, j, 0]
            along.append(forward_both(even, elements[chunk, at, :, j, 1], next_lane(even)))
        for q in range(3):
            value, slope = forward_both(*[along[j][0][q] for j in range(3)])
            zslope = forward_value(*[along[j][1][q] for j in range(3)])
            for p in range(3):
                fields[at, :, 0, p * 3 + q] = value[p]
                fields[at, :, 1, p * 3 + q] = slope[p]
                fields[at, :, 2, p * 3 + q] = zslope[p]

    blocks(3, SPREAD, one)


def at_points(fields, lines, c):
    value, xslope = forward_both(*[fields[c, i, 0, lines] for i in range(3)])
    yslope = forward_value(*[fields[c, i, 1, lines] for i in range(3)])
    zslope = forward_value(*[fields[c, i, 2, lines] for i in range(3)])
    return value, xslope, yslope, zslope


def apply_operator(above_floor, elements, pressures, chunk, state, slopes, fields, qpoints, ppoints, out, pout):
    spread(elements, chunk, fields)
    if pressures is not None:
        corner = {}
        for i in range(2):
            for j in range(2):
                low = pressures[chunk, i * 2 + j]
                corner[i, j] = forward_linear(low, next_lane(low))
        for q in range(3):
            sides = [forward_linear(corner[i, 0][q], corner[i, 1][q]) for i in range(2)]
            for p in range(3):
                points = forward_linear(sides[0][p], sides[1][p])
                for r in range(3):
                    qpoints[r, p * 3 + q] = points[r]

    def one(line):
        lines = pl.ds(line, LINES)
        value, slope = [], []
        for c in range(3):
            v, gx, gy, gz = at_points(fields, lines, c)
            value.append(v)
            slope.append((gx, gy, gz))
        force = [[None] * 3 for _ in range(3)]
        flux = [[[None] * 3 for _ in range(3)] for _ in range(3)]
        for r in range(3):
            ppoints[r, lines] = slope[0][0][r] + slope[1][1][r] + slope[2][2][r]
            wind = [state[chunk, r, b, lines] for b in range(3)]
            pressure = qpoints[r, lines] if pressures is not None else None
            for a in range(3):
                for b in range(3):
                    g = slope[a][b][r] + value[a][r] * wind[b]
                    if a == b and pressures is not None:
                        g = g - pressure
                    flux[a][b][r] = g
                total = slopes[chunk, r, a * 3, lines] * value[0][r]
                for c in range(1, 3):
                    total = total + slopes[chunk, r, a * 3 + c, lines] * value[c][r]
                force[a][r] = total
        for c in range(3):
            first = back_both(force[c], flux[c][0])
            second = back_value(flux[c][1])
            third = back_value(flux[c][2])
            for i in range(3):
                fields[c, i, 0, lines] = first[i]
                fields[c, i, 1, lines] = second[i]
                fields[c, i, 2, lines] = third[i]

    blocks(9, LINES, one)

    def gather(c):
        at = pl.ds(c, GATHER)
        value, zslope = [], []
        for q in range(3):
            value.append(
                back_both(
                    [fields[at, :, 0, p * 3 + q] for p in range(3)],
                    [fields[at, :, 1, p * 3 + q] for p in range(3)],
                )
            )
            zslope.append(back_value([fields[at, :, 2, p * 3 + q] for p in range(3)]))
        for j in range(3):
            nodes = back_both([value[q][j] for q in range(3)], [zslope[q][j] for q in range(3)])
            out[chunk, at, :, j, 0] = nodes[0] + last_lane(jnp.where(above_floor, nodes[2], 0.0))
            out[chunk, at, :, j, 1] = nodes[1]

    blocks(3, GATHER, gather)
    rows = {}
    for q in range(3):
        sides = []
        for p in range(3):
            sides.append(back_linear([ppoints[r, p * 3 + q] for r in range(3)]))
        for i in range(2):
            rows[i, q] = back_linear([sides[p][i] for p in range(3)])
    for i in range(2):
        for j in range(2):
            low, high = back_linear([rows[i, q][j] for q in range(3)])
            pout[chunk, i * 2 + j] = low + last_lane(jnp.where(above_floor, high, 0.0))


def pick(row, k):
    lane = lax.broadcasted_iota(jnp.int32, (1, 128), 1)
    return jnp.sum(jnp.where(lane == k, row, 0.0), axis=1, keepdims=True)


def solve(row):
    entries = {}
    at = 0
    for i in range(4):
        for j in range(i, 4):
            entries[i, j] = pick(row, at) + pick(row, 10)
            at += 1
    m = [[entries[min(i, j), max(i, j)] for j in range(1, 4)] + [entries[0, i]] for i in range(1, 4)]
    for k in range(2):
        inverse = 1.0 / m[k][k]
        for i in range(k + 1, 3):
            factor = m[i][k] * inverse
            for j in range(k + 1, 4):
                m[i][j] = m[i][j] - factor * m[k][j]
    t = [None] * 3
    for k in (2, 1, 0):
        total = m[k][3]
        for j in range(k + 1, 3):
            total = total - m[k][j] * t[j]
        t[k] = total / m[k][k]
    return t


def kernel(sizes, state_far, grad_far, wall_far, level_far, vel_out, pres_out,
           state_in, grad_in, wall_in, level_in, raw, nodes, ends, reach, even, odd, stiff, u0, us, u1, u2, u3, p1, p2, p3, keep_e, friction,
           wind, slopes, fields, qpoints, ppoints, out, pout, block, side, natural, plane_sum, line_sum,
           load, reached, across, send, recv):
    loads = [
        pltpu.make_async_copy(far, near, load.at[n])
        for n, (far, near) in enumerate(
            ((grad_far, grad_in), (state_far, state_in), (wall_far, wall_in), (level_far, level_in)))
    ]
    for copy in loads:
        copy.start()

    gx, gy, gz = lax.axis_index("gx"), lax.axis_index("gy"), lax.axis_index("gz")

    def device(o):
        return tuple(lax.rem(a + d + n, n) for a, d, n in zip((gx, gy, gz), o, sizes))

    others = [(a, b, 0) for a in range(sizes[0]) for b in range(sizes[1]) if (a, b) != (0, 0)]
    along = [(0, 0, d) for d in range(1, sizes[2])]
    partners = {tuple(d % n for d, n in zip(o, sizes)) for o in NEAR}
    partners = sorted(partners - {(0, 0, 0)})

    side[...] = jnp.zeros_like(side)

    barrier = pltpu.get_barrier_semaphore()
    for o in partners:
        pl.semaphore_signal(barrier, inc=1, device_id=device(o), device_id_type=MESH)

    lane = lax.broadcasted_iota(jnp.int32, (8, 128), 1)
    sub = lax.broadcasted_iota(jnp.int32, (8, 128), 0)

    for copy in loads:
        copy.wait()

    for x in range(4):
        spot = pl.ds((x % 2) * 4, 4)
        mask = 1.0 - wall_in[x].astype(F32)
        for c in range(3):
            raw[c, x // 2, spot] = mask * grad_in[c, x]
            raw[3 + c, x // 2, spot] = state_in[c, x]
        raw[6, x // 2, spot] = mask
    rows = lax.broadcasted_iota(jnp.int32, (128, 128), 0)
    cols = lax.broadcasted_iota(jnp.int32, (128, 128), 1)
    split = (rows == jnp.where(cols < 64, 2 * cols, 2 * cols - 127)).astype(F32)
    join = (cols == jnp.where(rows < 64, 2 * rows, 2 * rows - 127)).astype(F32)
    parted = jnp.dot(raw[0:7].reshape(112, 128), split, precision=HIGHEST, preferred_element_type=F32)
    parted = parted.reshape(7, 2, 8, 128)
    twice = (rows[:64] == jnp.where(cols[:64] < 64, cols[:64], cols[:64] - 64)).astype(F32)
    density = level_in[...].astype(F32) / (LEVELS - 1)
    drag = PEAK * SHAPE * (1.0 - density) / (SHAPE + density)
    for h in range(2):
        wide = jnp.dot(drag[h], twice, precision=HIGHEST, preferred_element_type=F32)
        for y in range(4):
            raw[7, h, y : y + 1] = wide[y // 2 : y // 2 + 1]
            raw[7, h, y + 4 : y + 5] = wide[y // 2 : y // 2 + 1]
    for h in range(2):
        first = jnp.zeros((8, 128), F32)
        last = jnp.zeros((8, 128), F32)
        for f in range(8):
            v = raw[7, h] if f == 6 else parted[6 if f == 7 else f, h]
            for xl in range(2):
                nodes[f, 2 + 2 * h + xl, 2:6] = v[4 * xl : 4 * xl + 4]
            go = 8 * f
            lower = (lane >= go) & (lane < go + 4)
            upper = (lane >= go + 4) & (lane < go + 8)
            first = jnp.where(lower, pltpu.roll(v, go, 1), first)
            first = jnp.where(upper, pltpu.roll(v, (go + 4 - 64) % 128, 1), first)
            last = jnp.where(lower, pltpu.roll(v, (go - 60) % 128, 1), last)
            last = jnp.where(upper, pltpu.roll(v, (go + 4 - 124) % 128, 1), last)
        for xl in range(2):
            ends[0, 2 * h + xl, 0:4] = last[4 * xl : 4 * xl + 4]
            ends[1, 2 * h + xl, 0:4] = first[4 * xl : 4 * xl + 4]

    pl.semaphore_wait(barrier, len(partners))

    def tell(n):
        for d in (-1, 1):
            pl.semaphore_signal(
                reached.at[n], inc=1, device_id=device((0, 0, d * 2**n)), device_id_type=MESH)

    rounds = 0
    while 2**rounds < sizes[2] // 2:
        rounds += 1
    if rounds:
        tell(0)

    for o in NEAR:
        sx, sy = -o[0], -o[1]
        (xs, xe), (ys, ye) = SOURCE[sx], SOURCE[sy]
        (tx, te), (ty, tf) = TARGET[sx], TARGET[sy]
        if o[2] == 0:
            source = nodes.at[:, 2 + xs : 2 + xe, 2 + ys : 2 + ye]
            target = nodes.at[:, tx:te, ty:tf]
            group = 0
        else:
            group = 1
            which = 0 if o[2] == 1 else 1
            source = ends.at[which, xs:xe, ys:ye]
            target = reach.at[which, tx:te, ty:tf]
        pltpu.make_async_remote_copy(
            src_ref=source, dst_ref=target, send_sem=send.at[group], recv_sem=recv.at[group],
            device_id=device(o), device_id_type=MESH).start()

    in_all = [
        nodes.at[:, 0:5, 0:13],
        reach.at[:, :, 0:9],
        side.at[0:7, :, 0:1],
        plane_sum.at[1 : len(others) + 1],
        line_sum.at[1 : len(along) + 1],
    ]

    def arrived(group):
        ref = in_all[group]
        pltpu.make_async_copy(ref, ref, recv.at[group]).wait()

    ey = sub % 4 - 1
    z = jnp.where(lane < 96, lane, lane - 128)
    zmin = jnp.where(gz > 0, -3, 0)
    zmax = jnp.where(gz < sizes[2] - 1, 65, 63)
    in_z = (z >= zmin) & (z <= zmax)
    ymin = jnp.where(gy > 0, -1, 0)
    ymax = jnp.where(gy < sizes[1] - 1, 2, 1)
    xmin = jnp.where(gx > 0, -1, 0)
    xmax = jnp.where(gx < sizes[0] - 1, 2, 1)
    ex = [jnp.where(sub < 4, 0, 1), jnp.where(sub < 4, 2, -1)]
    real = [in_z & (ey >= ymin) & (ey <= ymax) & (e >= xmin) & (e <= xmax) for e in ex]
    narrow = [r & (ey <= 1) & (e <= 1) for r, e in zip(real, ex)]
    own_y = (ey >= 0) & (ey <= 1)
    own_wide = in_z & own_y
    own = own_y & (lane < 64)
    zlim = jnp.where(gz < sizes[2] - 1, 64, 96)
    node_z = (lane < 64) | (lane >= zlim)
    above_floor = lane < jnp.where(gz > 0, 128, 96)
    ylim = jnp.where(gy < sizes[1] - 1, 99, 6)
    xlim = jnp.where(gx < sizes[0] - 1, 99, 6)
    node_yz = [node_z & (sub + 8 * h < ylim) for h in range(2)]

    if rounds > 1:
        pl.semaphore_wait(reached.at[0], 2)
        tell(1)
    arrived(0)
    arrived(1)
    if sizes[0] > 6:
        for d in (-2, 2):
            pl.semaphore_signal(across, inc=1, device_id=device((d, 0, 0)), device_id_type=MESH)

    def widen(x, carry):
        inside = jnp.where(x < xlim, 1.0, 0.0).astype(F32)
        for h in range(2):
            rows8 = pl.ds(8 * h, 8)
            below = reach[0, x, rows8]
            above = reach[1, x, rows8]
            for f in range(8 if h == 0 else 6):
                v = nodes[f, x, rows8]
                go = 8 * f
                e = jnp.where(lane < 96, pltpu.roll(above, (64 - go) % 128, 1), pltpu.roll(below, (124 - go) % 128, 1))
                e = jnp.where(lane < 64, v, e)
                if f == 6:
                    stiff[0, x] = e
                    continue
                ok = node_yz[h]
                if f == 7:
                    ok = ok & (sub >= 2) & (sub < 7)
                even[f, x, rows8] = jnp.where(ok, e * inside, 0.0)
                o = jnp.where(lane < 96, pltpu.roll(above, (60 - go) % 128, 1), pltpu.roll(below, (120 - go) % 128, 1))
                o = jnp.where(lane < 64, pltpu.roll(v, 64, 1), o)
                odd[f, x, rows8] = jnp.where(ok, o * inside, 0.0)
        return carry

    lax.fori_loop(0, 9, widen, 0)

    def to_elements(source, f, x, j):
        return source[f, x, pl.ds(j, 4, stride=2), :]

    def collect(first, target, masks):
        three = pl.ds(first, 3)
        for i in range(3):
            for j in range(3):
                for k, source in enumerate((even, odd)):
                    for chunk, (low, high) in enumerate(((2, 4), (6, 0))):
                        v = jnp.concatenate(
                            [to_elements(source, three, low + i, j), to_elements(source, three, high + i, j)], axis=1)
                        if masks is not None:
                            v = jnp.where(masks[chunk], v, 0.0)
                        target[chunk, :, i, j, k] = v

    collect(0, u0, real)
    collect(3, us, None)
    for i in range(3):
        for j in range(3):
            for k, source in enumerate((even, odd)):
                keep_e[i, j, k] = SCALE * jnp.concatenate(
                    [to_elements(source, 7, 2 + i, j), to_elements(source, 7, 4 + i, j)], axis=0)
    for chunk, (low, high) in enumerate(((2, 4), (6, 0))):
        friction[chunk] = jnp.concatenate([to_elements(stiff, 0, low, 0), to_elements(stiff, 0, high, 0)], axis=0)

    def prepare(chunk, carry):
        spread(us, chunk, fields)

        def one(line):
            lines = pl.ds(line, LINES)
            for c in range(3):
                v, gx_, gy_, gz_ = at_points(fields, lines, c)
                for r in range(3):
                    wind[chunk, r, c, lines] = v[r]
                    for b, g in enumerate((gx_, gy_, gz_)):
                        slopes[chunk, r, b * 3 + c, lines] = g[r] + friction[chunk] if b == c else g[r]

        blocks(9, LINES, one)
        return carry

    lax.fori_loop(0, 2, prepare, 0)

    def first_step(chunk, carry):
        apply_operator(above_floor, u0, None, chunk, wind, slopes, fields, qpoints, ppoints, out, pout)
        return carry

    lax.fori_loop(0, 2, first_step, 0)

    low_half = sub < 4

    def owners(source, at, last):
        total = {}
        for chunk in range(2):
            for i in range(last + 1):
                v = [at(source, chunk, i, j) for j in range(last + 1)]
                total[chunk, i, 0] = v[0] + last_row(v[last])
                for j in range(1, last):
                    total[chunk, i, j] = v[j]
        return total

    def close(total, last):
        full = {}
        edge = {}
        for j in range(last):
            before = half_turn(total[1, last, j])
            mine = half_turn(total[0, last, j])
            full[0, j] = total[0, 0, j] + jnp.where(low_half, before, mine)
            edge[j] = total[1, 0, j] + mine
            for i in range(1, last):
                full[i, j] = total[0, i, j]
        return full, edge

    def complete(full, edge, last):
        for j in range(last):
            full[last, j] = jnp.where(low_half, half_turn(full[0, j]), half_turn(edge[j]))
        for i in range(last + 1):
            full[i, last] = next_row(full[i, 0])
        return full

    def finish_first(c, carry):
        for k in range(2):
            total = owners(out, lambda s, chunk, i, j: s[chunk, c, i, j, k], 2)
            full = complete(*close(total, 2), 2)
            for i in range(3):
                for j in range(3):
                    u1[0, c, i, j, k] = jnp.where(own_wide, full[i, j] * keep_e[i, j, k], 0.0)
        return carry

    lax.fori_loop(0, 3, finish_first, 0)

    def vertex_mask(i, j):
        ok = own_wide & ((lane < 64) | (lane >= zlim))
        ylast = jnp.where(gy < sizes[1] - 1, 99, 2)
        xlast = jnp.where(gx < sizes[0] - 1, 99, 2)
        return ok & (ey + j < ylast) & (ex[0] + i < xlast)

    full = complete(*close(owners(pout, lambda s, chunk, i, j: s[chunk, i * 2 + j], 1), 1), 1)
    for i in range(2):
        for j in range(2):
            p1[0, i * 2 + j] = jnp.where(vertex_mask(i, j), -SCALE * full[i, j], 0.0)

    if rounds > 2:
        pl.semaphore_wait(reached.at[1], 2)
        tell(2)

    apply_operator(above_floor, u1, p1, 0, wind, slopes, fields, qpoints, ppoints, out, pout)

    def store_rows(plane, x, parity, v, step):
        block[plane, x, pl.ds(parity, 4, stride=step), :] = v

    for n in range(7):
        last = 2 if n < 6 else 1
        c, k = n // 2, n % 2

        def at(i, j):
            return out[0, c, i, j, k] if n < 6 else pout[0, i * 2 + j]

        for j in range(last):
            v = [at(i, 0) + last_row(at(i, last)) if j == 0 else at(i, j) for i in range(last + 1)]
            if n == 6:
                v = [-SCALE * w for w in v]
            step = 2 // last
            turned = [half_turn(w) for w in v]
            for i in range(last):
                store_rows(n, step * i, j, v[i][0:4], 2)
            store_rows(n, 2, j, (v[last] + turned[0])[0:4], 2)
            for i in range(1, last):
                store_rows(n, 2 + i, j, turned[i][0:4], 2)
            store_rows(n, 4, j, turned[last][0:4], 2)
    vertex_yz = jnp.where(node_yz[0], 1.0, 0.0)
    for x in range(5):
        inside = jnp.where(x + 2 < xlim, 1.0, 0.0).astype(F32)
        for k, source in enumerate((even, odd)):
            mask = SCALE * source[7, x + 2, 0:8]
            for c in range(3):
                block[2 * c + k, x] = block[2 * c + k, x] * mask
        if x % 2 == 0:
            odd_rows = sub % 2 == 1
            block[6, x] = jnp.where(odd_rows, 0.0, block[6, x] * (vertex_yz * inside))
        else:
            block[6, x] = jnp.zeros((8, 128), F32)

    for n, o in enumerate(PLANE):
        sx, sy = -o[0], -o[1]
        xs, xe = {-1: (2, 5), 0: (0, 5), 1: (0, 1)}[sx]
        ys, ty, count = {-1: (4, 0, 3), 0: (2, 2, 5), 1: (2, 6, 1)}[sy]
        pltpu.make_async_remote_copy(
            src_ref=block.at[:, xs:xe, ys : ys + count], dst_ref=side.at[n, :, 0 : xe - xs, ty : ty + count],
            send_sem=send.at[2], recv_sem=recv.at[2], device_id=device(o), device_id_type=MESH).start()

    have = {0: 1.0}
    have_x = {-1: jnp.where(gx > 0, 1.0, 0.0).astype(F32), 1: jnp.where(gx < sizes[0] - 1, 1.0, 0.0).astype(F32)}
    have_y = {-1: jnp.where(gy > 0, 1.0, 0.0).astype(F32), 1: jnp.where(gy < sizes[1] - 1, 1.0, 0.0).astype(F32)}
    arrived(2)
    if rounds > 3:
        pl.semaphore_wait(reached.at[2], 2)
        tell(3)

    def part(n, plane, x):
        sx, sy = -PLANE[n][0], -PLANE[n][1]
        v = side[n, plane, x]
        if sx:
            v = v * have_x[sx]
        if sy:
            v = v * have_y[sy]
        return v

    slot = {(-o[0], -o[1]): n for n, o in enumerate(PLANE)}

    def join_parts(plane, target, f):
        for x in range(7):
            total = block[plane, x - 2] if x >= 2 else None
            for sx in (-1, 0, 1):
                lo, hi = {-1: (0, 2), 0: (2, 6), 1: (6, 6)}[sx]
                if not lo <= x <= hi:
                    continue
                for sy in (-1, 0, 1):
                    if (sx, sy) != (0, 0):
                        v = part(slot[sx, sy], plane, x - lo)
                        total = v if total is None else total + v
            target[f, x, 0:8] = total

    def join_component(c, carry):
        join_parts(2 * c, even, c)
        join_parts(2 * c + 1, odd, c)
        return carry

    lax.fori_loop(0, 3, join_component, 0)
    join_parts(6, even, 3)
    collect(0, u2, narrow)
    for i in range(2):
        for j in range(2):
            for chunk, (low, high) in enumerate(((2, 4), (6, 0))):
                v = jnp.concatenate(
                    [to_elements(even, 3, low + 2 * i, 2 * j), to_elements(even, 3, high + 2 * i, 2 * j)], axis=0)
                p2[chunk, i * 2 + j] = jnp.where(narrow[chunk], v, 0.0)

    def last_step(chunk, carry):
        apply_operator(above_floor, u2, p2, chunk, wind, slopes, fields, qpoints, ppoints, out, pout)
        return carry

    lax.fori_loop(0, 2, last_step, 0)

    def finish_last(c, carry):
        for k in range(2):
            total = owners(out, lambda s, chunk, i, j: s[chunk, c, i, j, k], 2)
            full, _ = close(total, 2)
            for i in range(2):
                for j in range(2):
                    u3[0, c, i, j, k] = full[i, j] * keep_e[i, j, k]
        return carry

    lax.fori_loop(0, 3, finish_last, 0)
    full, _ = close(owners(pout, lambda s, chunk, i, j: s[chunk, i * 2 + j], 1), 1)
    p3[0, 0] = -SCALE * full[0, 0]

    pairs = [(i, j) for i in range(4) for j in range(i, 4)]

    def products(c, sums):
        sums = list(sums)
        for i in range(2):
            for j in range(2):
                for k in range(2):
                    v = [u[0, c, i, j, k] for u in (u0, u1, u2, u3)]
                    for n, (a, b) in enumerate(pairs):
                        sums[n] = sums[n] + v[a] * v[b]
        return tuple(sums)

    sums = list(lax.fori_loop(0, 3, products, tuple(jnp.zeros((8, 128), F32) for _ in pairs)))
    ps = [None, p1[0, 0], p2[0, 0], p3[0, 0]]
    for n, (a, b) in enumerate(pairs):
        if a:
            sums[n] = sums[n] + ps[a] * ps[b]
    fixed = jnp.zeros((4, 128), F32)
    for x in range(4):
        held = wall_in[x].astype(F32)
        for c in range(3):
            v = held * grad_in[c, x]
            fixed = fixed + v * v
    single = lane[0:1]
    row = jnp.zeros((1, 128), F32)
    for n in range(10):
        total = jnp.sum(jnp.sum(jnp.where(own, sums[n], 0.0), axis=0, keepdims=True), axis=1, keepdims=True)
        row = jnp.where(single == n, total, row)
    total = jnp.sum(jnp.sum(fixed, axis=0, keepdims=True), axis=1, keepdims=True)
    row = jnp.where(single == 10, total, row)

    def exchange(group, offsets, buffer, value):
        buffer[0] = value
        for n, o in enumerate(offsets):
            pltpu.make_async_remote_copy(
                src_ref=buffer.at[0], dst_ref=buffer.at[n + 1], send_sem=send.at[group], recv_sem=recv.at[group],
                device_id=device(o), device_id_type=MESH).start()

    def gathered(group, buffer):
        arrived(group)
        return jnp.sum(buffer[...], axis=0)

    if sizes[0] > 6:
        pl.semaphore_wait(across, 2)
    exchange(3, others, plane_sum, row)

    for n, u in enumerate((u1, u2)):
        for c in range(3):
            packed = []
            for i in range(2):
                for j in range(2):
                    packed.append(jnp.where(lane < 64, u[0, c, i, j, 0], pltpu.roll(u[0, c, i, j, 1], 64, 1)))
            flat = jnp.concatenate(packed, axis=0)
            flat = jnp.dot(flat, join, precision=HIGHEST, preferred_element_type=F32)
            for i in range(2):
                for j in range(2):
                    at8 = (i * 2 + j) * 8
                    for e in range(2):
                        natural[n, c, 2 * e + i, pl.ds(j, 2, stride=2), :] = flat[at8 + 4 * e + 1 : at8 + 4 * e + 3]

    row = gathered(3, plane_sum)
    if rounds:
        pl.semaphore_wait(reached.at[rounds - 1], 2)
    exchange(4, along, line_sum, row)
    row = gathered(4, line_sum)
    t = solve(row)
    for x in range(4):
        free = wall_in[x] == 0
        for c in range(3):
            b = grad_in[c, x]
            v = t[1] * natural[0, c, x, 0:4] + t[2] * natural[1, c, x, 0:4]
            vel_out[c, x] = jnp.where(free, t[0] * b, (t[0] + t[1] + t[2]) * b) + v
    v = t[1] * p1[0, 0] + t[2] * p2[0, 0]
    for e in range(2):
        pres_out[e] = v[4 * e + 1 : 4 * e + 3, 0:64]

    for group, ref in enumerate(in_all):
        pltpu.make_async_copy(ref, ref, send.at[group]).wait()


def local(sizes, state_velocity, objective_gradient, wall_flags, design_levels):
    vm = pltpu.VMEM
    plane, line = sizes[0] * sizes[1], sizes[2]
    tile = (8, 128)
    scratch = [
        vm((3, 4, 4, 128), F32),
        vm((3, 4, 4, 128), F32),
        vm((4, 4, 128), jnp.int32),
        vm((2, 2, 64), jnp.int32),
        vm((8, 2) + tile, F32),
        vm((8, 9, 16, 128), F32),
        vm((2, 4) + tile, F32),
        vm((2, 9, 16, 128), F32),
        vm((8, 9, 16, 128), F32),
        vm((8, 9, 16, 128), F32),
        vm((1, 9) + tile, F32),
        vm((2, 3, 3, 3, 2) + tile, F32),
        vm((2, 3, 3, 3, 2) + tile, F32),
        vm((1, 3, 3, 3, 2) + tile, F32),
        vm((2, 3, 3, 3, 2) + tile, F32),
        vm((1, 3, 3, 3, 2) + tile, F32),
        vm((1, 4) + tile, F32),
        vm((2, 4) + tile, F32),
        vm((1, 1) + tile, F32),
        vm((3, 3, 2) + tile, F32),
        vm((2,) + tile, F32),
        vm((2, 3, 3, 9) + tile, F32),
        vm((2, 3, 9, 9) + tile, F32),
        vm((3, 3, 3, 9) + tile, F32),
        vm((3, 9) + tile, F32),
        vm((3, 9) + tile, F32),
        vm((2, 3, 3, 3, 2) + tile, F32),
        vm((2, 4) + tile, F32),
        vm((7, 5) + tile, F32),
        vm((8, 7, 5) + tile, F32),
        vm((2, 3, 4) + tile, F32),
        vm((plane, 1, 128), F32),
        vm((line, 1, 128), F32),
    ]
    scratch += [
        pltpu.SemaphoreType.DMA((4,)),
        pltpu.SemaphoreType.REGULAR((4,)),
        pltpu.SemaphoreType.REGULAR,
        pltpu.SemaphoreType.DMA((5,)),
        pltpu.SemaphoreType.DMA((5,)),
    ]
    return pl.pallas_call(
        functools.partial(kernel, sizes),
        out_shape=(
            jax.ShapeDtypeStruct((3, 4, 4, 128), F32),
            jax.ShapeDtypeStruct((2, 2, 64), F32),
        ),
        in_specs=[pl.BlockSpec(memory_space=pl.ANY)] * 4,
        out_specs=[pl.BlockSpec(memory_space=pltpu.VMEM)] * 2,
        scratch_shapes=scratch,
        compiler_params=pltpu.CompilerParams(
            collective_id=0, has_side_effects=True, vmem_limit_bytes=56 * 1024 * 1024
        ),
    )(state_velocity, objective_gradient, wall_flags, design_levels)


def solution(mesh):
    in_specs = (
        P(None, "gx", "gy", "gz"),
        P(None, "gx", "gy", "gz"),
        P("gx", "gy", "gz"),
        P("gx", "gy", "gz"),
    )
    out_specs = (P(None, "gx", "gy", "gz"), P("gx", "gy", "gz"))
    sizes = tuple(mesh.shape[a] for a in ("gx", "gy", "gz"))
    return jax.shard_map(
        functools.partial(local, sizes), mesh=mesh, in_specs=in_specs, out_specs=out_specs, check_vma=False
    )
```

```python
import functools
import itertools
import math

import jax
import jax.numpy as jnp
from jax import lax
from jax.experimental import pallas as pl
from jax.experimental.pallas import tpu as pltpu
from jax.sharding import PartitionSpec as P

MESH = pl.DeviceIdType.MESH
F32 = jnp.float32
HIGHEST = lax.Precision.HIGHEST

LEVELS = 9
PEAK = 8.0
SHAPE = 0.1

OFFSET = math.sqrt(0.15)
WIDEN = 9
SPREAD = 3
LINES = 9
GATHER = 3

RATIO = 5.0 / 8.0
SCALE = (8.0 / 18.0) ** 3

NEAR = [o for o in itertools.product((-1, 0, 1), repeat=3) if o != (0, 0, 0)]
NEAR.sort(key=lambda o: (o[2] == 0, -sum(map(abs, o))))
PLANE = [o for o in NEAR if o[2] == 0]

SOURCE = {-1: (2, 4), 0: (0, 4), 1: (0, 3)}
TARGET = {-1: (0, 2), 0: (2, 6), 1: (6, 9)}


def forward_both(a, b, c):
    d = c - a
    w = (b + b) - (a + c)
    s = (4.0 * OFFSET) * w
    m = b - 0.3 * w
    e = OFFSET * d
    return (m - e, b, m + e), (d + s, d, d - s)


def forward_value(a, b, c):
    d = c - a
    w = (b + b) - (a + c)
    m = b - 0.3 * w
    e = OFFSET * d
    return (m - e, b, m + e)


def back_value(f):
    s = f[0] + f[2]
    a = (0.3 * RATIO) * s
    b = (OFFSET * RATIO) * (f[2] - f[0])
    return (a - b, f[1] + (0.4 * RATIO) * s, a + b)


def back_both(f, g):
    s = f[0] + f[2]
    b = (OFFSET * RATIO) * (f[2] - f[0]) + (RATIO * (g[0] + g[2]) + g[1])
    w = (4.0 * OFFSET * RATIO) * (g[0] - g[2])
    a = (0.3 * RATIO) * s - w
    return (a - b, f[1] + (0.4 * RATIO) * s + (w + w), a + b)


def forward_linear(a, b):
    m = 0.5 * (a + b)
    d = OFFSET * (b - a)
    return (m - d, m, m + d)


def back_linear(f):
    m = (0.5 * RATIO) * (f[0] + f[2]) + 0.5 * f[1]
    d = (OFFSET * RATIO) * (f[2] - f[0])
    return (m - d, m + d)


def next_lane(v):
    return pltpu.roll(v, 127, v.ndim - 1)


def last_lane(v):
    return pltpu.roll(v, 1, v.ndim - 1)


def next_row(v):
    return pltpu.roll(v, 7, 0)


def last_row(v):
    return pltpu.roll(v, 1, 0)


def half_turn(v):
    return pltpu.roll(v, 4, 0)


def blocks(count, size, body):
    if size == count:
        body(0)
        return

    def one(n, carry):
        body(n * size)
        return carry

    lax.fori_loop(0, count // size, one, 0)


def spread(elements, chunk, fields):
    def one(c):
        at = pl.ds(c, SPREAD)
        along = []
        for j in range(3):
            even = elements[chunk, at, :, j, 0]
            along.append(forward_both(even, elements[chunk, at, :, j, 1], next_lane(even)))
        for q in range(3):
            value, slope = forward_both(*[along[j][0][q] for j in range(3)])
            zslope = forward_value(*[along[j][1][q] for j in range(3)])
            for p in range(3):
                fields[at, :, 0, p * 3 + q] = value[p]
                fields[at, :, 1, p * 3 + q] = slope[p]
                fields[at, :, 2, p * 3 + q] = zslope[p]

    blocks(3, SPREAD, one)


def at_points(fields, lines, c):
    value, xslope = forward_both(*[fields[c, i, 0, lines] for i in range(3)])
    yslope = forward_value(*[fields[c, i, 1, lines] for i in range(3)])
    zslope = forward_value(*[fields[c, i, 2, lines] for i in range(3)])
    return value, xslope, yslope, zslope


def apply_operator(above_floor, elements, pressures, chunk, state, slopes, fields, qpoints, ppoints, out, pout):
    spread(elements, chunk, fields)
    if pressures is not None:
        corner = {}
        for i in range(2):
            for j in range(2):
                low = pressures[chunk, i * 2 + j]
                corner[i, j] = forward_linear(low, next_lane(low))
        for q in range(3):
            sides = [forward_linear(corner[i, 0][q], corner[i, 1][q]) for i in range(2)]
            for p in range(3):
                points = forward_linear(sides[0][p], sides[1][p])
                for r in range(3):
                    qpoints[r, p * 3 + q] = points[r]

    def one(line):
        lines = pl.ds(line, LINES)
        value, slope = [], []
        for c in range(3):
            v, gx, gy, gz = at_points(fields, lines, c)
            value.append(v)
            slope.append((gx, gy, gz))
        force = [[None] * 3 for _ in range(3)]
        flux = [[[None] * 3 for _ in range(3)] for _ in range(3)]
        for r in range(3):
            ppoints[r, lines] = slope[0][0][r] + slope[1][1][r] + slope[2][2][r]
            wind = [state[chunk, r, b, lines] for b in range(3)]
            pressure = qpoints[r, lines] if pressures is not None else None
            for a in range(3):
                for b in range(3):
                    g = slope[a][b][r] + value[a][r] * wind[b]
                    if a == b and pressures is not None:
                        g = g - pressure
                    flux[a][b][r] = g
                total = slopes[chunk, r, a * 3, lines] * value[0][r]
                for c in range(1, 3):
                    total = total + slopes[chunk, r, a * 3 + c, lines] * value[c][r]
                force[a][r] = total
        for c in range(3):
            first = back_both(force[c], flux[c][0])
            second = back_value(flux[c][1])
            third = back_value(flux[c][2])
            for i in range(3):
                fields[c, i, 0, lines] = first[i]
                fields[c, i, 1, lines] = second[i]
                fields[c, i, 2, lines] = third[i]

    blocks(9, LINES, one)

    def gather(c):
        at = pl.ds(c, GATHER)
        value, zslope = [], []
        for q in range(3):
            value.append(
                back_both(
                    [fields[at, :, 0, p * 3 + q] for p in range(3)],
                    [fields[at, :, 1, p * 3 + q] for p in range(3)],
                )
            )
            zslope.append(back_value([fields[at, :, 2, p * 3 + q] for p in range(3)]))
        for j in range(3):
            nodes = back_both([value[q][j] for q in range(3)], [zslope[q][j] for q in range(3)])
            out[chunk, at, :, j, 0] = nodes[0] + last_lane(jnp.where(above_floor, nodes[2], 0.0))
            out[chunk, at, :, j, 1] = nodes[1]

    blocks(3, GATHER, gather)
    rows = {}
    for q in range(3):
        sides = []
        for p in range(3):
            sides.append(back_linear([ppoints[r, p * 3 + q] for r in range(3)]))
        for i in range(2):
            rows[i, q] = back_linear([sides[p][i] for p in range(3)])
    for i in range(2):
        for j in range(2):
            low, high = back_linear([rows[i, q][j] for q in range(3)])
            pout[chunk, i * 2 + j] = low + last_lane(jnp.where(above_floor, high, 0.0))


def pick(row, k):
    lane = lax.broadcasted_iota(jnp.int32, (1, 128), 1)
    return jnp.sum(jnp.where(lane == k, row, 0.0), axis=1, keepdims=True)


def solve(row):
    entries = {}
    at = 0
    for i in range(4):
        for j in range(i, 4):
            entries[i, j] = pick(row, at) + pick(row, 10)
            at += 1
    m = [[entries[min(i, j), max(i, j)] for j in range(1, 4)] + [entries[0, i]] for i in range(1, 4)]
    for k in range(2):
        inverse = 1.0 / m[k][k]
        for i in range(k + 1, 3):
            factor = m[i][k] * inverse
            for j in range(k + 1, 4):
                m[i][j] = m[i][j] - factor * m[k][j]
    t = [None] * 3
    for k in (2, 1, 0):
        total = m[k][3]
        for j in range(k + 1, 3):
            total = total - m[k][j] * t[j]
        t[k] = total / m[k][k]
    return t


def kernel(sizes, state_far, grad_far, wall_far, level_far, vel_out, pres_out,
           state_in, grad_in, wall_in, level_in, raw, nodes, ends, reach, even, odd, stiff, u0, us, u1, u2, u3, p1, p2, p3, keep_e, friction,
           wind, slopes, fields, qpoints, ppoints, out, pout, block, side, natural, plane_sum, line_sum,
           load, reached, across, send, recv):
    loads = [
        pltpu.make_async_copy(far, near, load.at[n])
        for n, (far, near) in enumerate(
            ((grad_far, grad_in), (state_far, state_in), (wall_far, wall_in), (level_far, level_in)))
    ]
    for copy in loads:
        copy.start()

    gx, gy, gz = lax.axis_index("gx"), lax.axis_index("gy"), lax.axis_index("gz")

    def device(o):
        return tuple(lax.rem(a + d + n, n) for a, d, n in zip((gx, gy, gz), o, sizes))

    others = [(a, b, 0) for a in range(sizes[0]) for b in range(sizes[1]) if (a, b) != (0, 0)]
    along = [(0, 0, d) for d in range(1, sizes[2])]
    partners = {tuple(d % n for d, n in zip(o, sizes)) for o in NEAR}
    partners = sorted(partners - {(0, 0, 0)})

    side[...] = jnp.zeros_like(side)

    barrier = pltpu.get_barrier_semaphore()
    for o in partners:
        pl.semaphore_signal(barrier, inc=1, device_id=device(o), device_id_type=MESH)

    lane = lax.broadcasted_iota(jnp.int32, (8, 128), 1)
    sub = lax.broadcasted_iota(jnp.int32, (8, 128), 0)

    for copy in loads:
        copy.wait()

    for x in range(4):
        spot = pl.ds((x % 2) * 4, 4)
        mask = 1.0 - wall_in[x].astype(F32)
        for c in range(3):
            raw[c, x // 2, spot] = mask * grad_in[c, x]
            raw[3 + c, x // 2, spot] = state_in[c, x]
        raw[6, x // 2, spot] = mask
    rows = lax.broadcasted_iota(jnp.int32, (128, 128), 0)
    cols = lax.broadcasted_iota(jnp.int32, (128, 128), 1)
    split = (rows == jnp.where(cols < 64, 2 * cols, 2 * cols - 127)).astype(F32)
    join = (cols == jnp.where(rows < 64, 2 * rows, 2 * rows - 127)).astype(F32)
    parted = jnp.dot(raw[0:7].reshape(112, 128), split, precision=HIGHEST, preferred_element_type=F32)
    parted = parted.reshape(7, 2, 8, 128)
    twice = (rows[:64] == jnp.where(cols[:64] < 64, cols[:64], cols[:64] - 64)).astype(F32)
    density = level_in[...].astype(F32) / (LEVELS - 1)
    drag = PEAK * SHAPE * (1.0 - density) / (SHAPE + density)
    for h in range(2):
        wide = jnp.dot(drag[h], twice, precision=HIGHEST, preferred_element_type=F32)
        for y in range(4):
            raw[7, h, y : y + 1] = wide[y // 2 : y // 2 + 1]
            raw[7, h, y + 4 : y + 5] = wide[y // 2 : y // 2 + 1]
    for h in range(2):
        first = jnp.zeros((8, 128), F32)
        last = jnp.zeros((8, 128), F32)
        for f in range(8):
            v = raw[7, h] if f == 6 else parted[6 if f == 7 else f, h]
            for xl in range(2):
                nodes[f, 2 + 2 * h + xl, 2:6] = v[4 * xl : 4 * xl + 4]
            go = 8 * f
            lower = (lane >= go) & (lane < go + 4)
            upper = (lane >= go + 4) & (lane < go + 8)
            first = jnp.where(lower, pltpu.roll(v, go, 1), first)
            first = jnp.where(upper, pltpu.roll(v, (go + 4 - 64) % 128, 1), first)
            last = jnp.where(lower, pltpu.roll(v, (go - 60) % 128, 1), last)
            last = jnp.where(upper, pltpu.roll(v, (go + 4 - 124) % 128, 1), last)
        for xl in range(2):
            ends[0, 2 * h + xl, 0:4] = last[4 * xl : 4 * xl + 4]
            ends[1, 2 * h + xl, 0:4] = first[4 * xl : 4 * xl + 4]

    pl.semaphore_wait(barrier, len(partners))

    def tell(n):
        for d in (-1, 1):
            pl.semaphore_signal(
                reached.at[n], inc=1, device_id=device((0, 0, d * 2**n)), device_id_type=MESH)

    rounds = 0
    while 2**rounds < sizes[2] // 2:
        rounds += 1
    if rounds:
        tell(0)

    for o in NEAR:
        sx, sy = -o[0], -o[1]
        (xs, xe), (ys, ye) = SOURCE[sx], SOURCE[sy]
        (tx, te), (ty, tf) = TARGET[sx], TARGET[sy]
        if o[2] == 0:
            source = nodes.at[:, 2 + xs : 2 + xe, 2 + ys : 2 + ye]
            target = nodes.at[:, tx:te, ty:tf]
            group = 0
        else:
            group = 1
            which = 0 if o[2] == 1 else 1
            source = ends.at[which, xs:xe, ys:ye]
            target = reach.at[which, tx:te, ty:tf]
        pltpu.make_async_remote_copy(
            src_ref=source, dst_ref=target, send_sem=send.at[group], recv_sem=recv.at[group],
            device_id=device(o), device_id_type=MESH).start()

    in_all = [
        nodes.at[:, 0:5, 0:13],
        reach.at[:, :, 0:9],
        side.at[0:7, :, 0:1],
        plane_sum.at[1 : len(others) + 1],
        line_sum.at[1 : len(along) + 1],
    ]

    def arrived(group):
        ref = in_all[group]
        pltpu.make_async_copy(ref, ref, recv.at[group]).wait()

    ey = sub % 4 - 1
    z = jnp.where(lane < 96, lane, lane - 128)
    zmin = jnp.where(gz > 0, -3, 0)
    zmax = jnp.where(gz < sizes[2] - 1, 65, 63)
    in_z = (z >= zmin) & (z <= zmax)
    ymin = jnp.where(gy > 0, -1, 0)
    ymax = jnp.where(gy < sizes[1] - 1, 2, 1)
    xmin = jnp.where(gx > 0, -1, 0)
    xmax = jnp.where(gx < sizes[0] - 1, 2, 1)
    ex = [jnp.where(sub < 4, 0, 1), jnp.where(sub < 4, 2, -1)]
    real = [in_z & (ey >= ymin) & (ey <= ymax) & (e >= xmin) & (e <= xmax) for e in ex]
    narrow = [r & (ey <= 1) & (e <= 1) for r, e in zip(real, ex)]
    own_y = (ey >= 0) & (ey <= 1)
    own_wide = in_z & own_y
    own = own_y & (lane < 64)
    zlim = jnp.where(gz < sizes[2] - 1, 64, 96)
    node_z = (lane < 64) | (lane >= zlim)
    above_floor = lane < jnp.where(gz > 0, 128, 96)
    ylim = jnp.where(gy < sizes[1] - 1, 99, 6)
    xlim = jnp.where(gx < sizes[0] - 1, 99, 6)
    node_yz = [node_z & (sub + 8 * h < ylim) for h in range(2)]

    if rounds > 1:
        pl.semaphore_wait(reached.at[0], 2)
        tell(1)
    arrived(0)
    arrived(1)
    if sizes[0] > 6:
        for d in (-2, 2):
            pl.semaphore_signal(across, inc=1, device_id=device((d, 0, 0)), device_id_type=MESH)

    def widen(first):
        xs = pl.ds(first, WIDEN)
        column = first + lax.broadcasted_iota(jnp.int32, (WIDEN, 8, 128), 0)
        inside = column < xlim
        for h in range(2):
            rows8 = pl.ds(8 * h, 8)
            below = reach[0, xs, rows8]
            above = reach[1, xs, rows8]
            ok = inside & node_yz[h]
            for f in range(8 if h == 0 else 6):
                v = nodes[f, xs, rows8]
                go = 8 * f
                e = jnp.where(lane < 96, pltpu.roll(above, (64 - go) % 128, 2), pltpu.roll(below, (124 - go) % 128, 2))
                e = jnp.where(lane < 64, v, e)
                if f == 6:
                    stiff[0, xs] = e
                    continue
                here = ok & ((sub >= 2) & (sub < 7)) if f == 7 else ok
                even[f, xs, rows8] = jnp.where(here, e, 0.0)
                o = jnp.where(lane < 96, pltpu.roll(above, (60 - go) % 128, 2), pltpu.roll(below, (120 - go) % 128, 2))
                o = jnp.where(lane < 64, pltpu.roll(v, 64, 2), o)
                odd[f, xs, rows8] = jnp.where(here, o, 0.0)

    blocks(9, WIDEN, widen)

    def to_elements(source, f, x, j):
        return source[f, x, pl.ds(j, 4, stride=2), :]

    def collect(first, target, masks):
        three = pl.ds(first, 3)
        for i in range(3):
            for j in range(3):
                for k, source in enumerate((even, odd)):
                    for chunk, (low, high) in enumerate(((2, 4), (6, 0))):
                        v = jnp.concatenate(
                            [to_elements(source, three, low + i, j), to_elements(source, three, high + i, j)], axis=1)
                        if masks is not None:
                            v = jnp.where(masks[chunk], v, 0.0)
                        target[chunk, :, i, j, k] = v

    collect(0, u0, real)
    collect(3, us, None)
    for i in range(3):
        for j in range(3):
            for k, source in enumerate((even, odd)):
                keep_e[i, j, k] = SCALE * jnp.concatenate(
                    [to_elements(source, 7, 2 + i, j), to_elements(source, 7, 4 + i, j)], axis=0)
    for chunk, (low, high) in enumerate(((2, 4), (6, 0))):
        friction[chunk] = jnp.concatenate([to_elements(stiff, 0, low, 0), to_elements(stiff, 0, high, 0)], axis=0)

    def prepare(chunk, carry):
        spread(us, chunk, fields)

        def one(line):
            lines = pl.ds(line, LINES)
            for c in range(3):
                v, gx_, gy_, gz_ = at_points(fields, lines, c)
                for r in range(3):
                    wind[chunk, r, c, lines] = v[r]
                    for b, g in enumerate((gx_, gy_, gz_)):
                        slopes[chunk, r, b * 3 + c, lines] = g[r] + friction[chunk] if b == c else g[r]

        blocks(9, LINES, one)
        return carry

    for chunk in range(2):
        prepare(chunk, 0)

    def first_step(chunk, carry):
        apply_operator(above_floor, u0, None, chunk, wind, slopes, fields, qpoints, ppoints, out, pout)
        return carry

    for chunk in range(2):
        first_step(chunk, 0)

    low_half = sub < 4

    def owners(source, at, last):
        total = {}
        for chunk in range(2):
            for i in range(last + 1):
                v = [at(source, chunk, i, j) for j in range(last + 1)]
                total[chunk, i, 0] = v[0] + last_row(v[last])
                for j in range(1, last):
                    total[chunk, i, j] = v[j]
        return total

    def close(total, last):
        full = {}
        edge = {}
        for j in range(last):
            before = half_turn(total[1, last, j])
            mine = half_turn(total[0, last, j])
            full[0, j] = total[0, 0, j] + jnp.where(low_half, before, mine)
            edge[j] = total[1, 0, j] + mine
            for i in range(1, last):
                full[i, j] = total[0, i, j]
        return full, edge

    def complete(full, edge, last):
        for j in range(last):
            full[last, j] = jnp.where(low_half, half_turn(full[0, j]), half_turn(edge[j]))
        for i in range(last + 1):
            full[i, last] = next_row(full[i, 0])
        return full

    def finish_first(c, carry):
        for k in range(2):
            total = owners(out, lambda s, chunk, i, j: s[chunk, c, i, j, k], 2)
            full = complete(*close(total, 2), 2)
            for i in range(3):
                for j in range(3):
                    u1[0, c, i, j, k] = jnp.where(own_wide, full[i, j] * keep_e[i, j, k], 0.0)
        return carry

    [finish_first(c, 0) for c in range(3)]

    def vertex_mask(i, j):
        ok = own_wide & ((lane < 64) | (lane >= zlim))
        ylast = jnp.where(gy < sizes[1] - 1, 99, 2)
        xlast = jnp.where(gx < sizes[0] - 1, 99, 2)
        return ok & (ey + j < ylast) & (ex[0] + i < xlast)

    full = complete(*close(owners(pout, lambda s, chunk, i, j: s[chunk, i * 2 + j], 1), 1), 1)
    for i in range(2):
        for j in range(2):
            p1[0, i * 2 + j] = jnp.where(vertex_mask(i, j), -SCALE * full[i, j], 0.0)

    if rounds > 2:
        pl.semaphore_wait(reached.at[1], 2)
        tell(2)

    apply_operator(above_floor, u1, p1, 0, wind, slopes, fields, qpoints, ppoints, out, pout)

    def store_rows(plane, x, parity, v, step):
        block[plane, x, pl.ds(parity, 4, stride=step), :] = v

    for n in range(7):
        last = 2 if n < 6 else 1
        c, k = n // 2, n % 2

        def at(i, j):
            return out[0, c, i, j, k] if n < 6 else pout[0, i * 2 + j]

        for j in range(last):
            v = [at(i, 0) + last_row(at(i, last)) if j == 0 else at(i, j) for i in range(last + 1)]
            if n == 6:
                v = [-SCALE * w for w in v]
            step = 2 // last
            turned = [half_turn(w) for w in v]
            for i in range(last):
                store_rows(n, step * i, j, v[i][0:4], 2)
            store_rows(n, 2, j, (v[last] + turned[0])[0:4], 2)
            for i in range(1, last):
                store_rows(n, 2 + i, j, turned[i][0:4], 2)
            store_rows(n, 4, j, turned[last][0:4], 2)
    vertex_yz = jnp.where(node_yz[0], 1.0, 0.0)
    for x in range(5):
        inside = jnp.where(x + 2 < xlim, 1.0, 0.0).astype(F32)
        for k, source in enumerate((even, odd)):
            mask = SCALE * source[7, x + 2, 0:8]
            for c in range(3):
                block[2 * c + k, x] = block[2 * c + k, x] * mask
        if x % 2 == 0:
            odd_rows = sub % 2 == 1
            block[6, x] = jnp.where(odd_rows, 0.0, block[6, x] * (vertex_yz * inside))
        else:
            block[6, x] = jnp.zeros((8, 128), F32)

    for n, o in enumerate(PLANE):
        sx, sy = -o[0], -o[1]
        xs, xe = {-1: (2, 5), 0: (0, 5), 1: (0, 1)}[sx]
        ys, ty, count = {-1: (4, 0, 3), 0: (2, 2, 5), 1: (2, 6, 1)}[sy]
        pltpu.make_async_remote_copy(
            src_ref=block.at[:, xs:xe, ys : ys + count], dst_ref=side.at[n, :, 0 : xe - xs, ty : ty + count],
            send_sem=send.at[2], recv_sem=recv.at[2], device_id=device(o), device_id_type=MESH).start()

    have = {0: 1.0}
    have_x = {-1: jnp.where(gx > 0, 1.0, 0.0).astype(F32), 1: jnp.where(gx < sizes[0] - 1, 1.0, 0.0).astype(F32)}
    have_y = {-1: jnp.where(gy > 0, 1.0, 0.0).astype(F32), 1: jnp.where(gy < sizes[1] - 1, 1.0, 0.0).astype(F32)}
    arrived(2)
    if rounds > 3:
        pl.semaphore_wait(reached.at[2], 2)
        tell(3)

    def part(n, plane, x):
        sx, sy = -PLANE[n][0], -PLANE[n][1]
        v = side[n, plane, x]
        if sx:
            v = v * have_x[sx]
        if sy:
            v = v * have_y[sy]
        return v

    slot = {(-o[0], -o[1]): n for n, o in enumerate(PLANE)}

    def join_parts(plane, target, f):
        for x in range(7):
            total = block[plane, x - 2] if x >= 2 else None
            for sx in (-1, 0, 1):
                lo, hi = {-1: (0, 2), 0: (2, 6), 1: (6, 6)}[sx]
                if not lo <= x <= hi:
                    continue
                for sy in (-1, 0, 1):
                    if (sx, sy) != (0, 0):
                        v = part(slot[sx, sy], plane, x - lo)
                        total = v if total is None else total + v
            target[f, x, 0:8] = total

    def join_component(c, carry):
        join_parts(2 * c, even, c)
        join_parts(2 * c + 1, odd, c)
        return carry

    [join_component(c, 0) for c in range(3)]
    join_parts(6, even, 3)
    collect(0, u2, narrow)
    for i in range(2):
        for j in range(2):
            for chunk, (low, high) in enumerate(((2, 4), (6, 0))):
                v = jnp.concatenate(
                    [to_elements(even, 3, low + 2 * i, 2 * j), to_elements(even, 3, high + 2 * i, 2 * j)], axis=0)
                p2[chunk, i * 2 + j] = jnp.where(narrow[chunk], v, 0.0)

    def last_step(chunk, carry):
        apply_operator(above_floor, u2, p2, chunk, wind, slopes, fields, qpoints, ppoints, out, pout)
        return carry

    for chunk in range(2):
        last_step(chunk, 0)

    def finish_last(c, carry):
        for k in range(2):
            total = owners(out, lambda s, chunk, i, j: s[chunk, c, i, j, k], 2)
            full, _ = close(total, 2)
            for i in range(2):
                for j in range(2):
                    u3[0, c, i, j, k] = full[i, j] * keep_e[i, j, k]
        return carry

    [finish_last(c, 0) for c in range(3)]
    full, _ = close(owners(pout, lambda s, chunk, i, j: s[chunk, i * 2 + j], 1), 1)
    p3[0, 0] = -SCALE * full[0, 0]

    pairs = [(i, j) for i in range(4) for j in range(i, 4)]

    def products(c, sums):
        sums = list(sums)
        for i in range(2):
            for j in range(2):
                for k in range(2):
                    v = [u[0, c, i, j, k] for u in (u0, u1, u2, u3)]
                    for n, (a, b) in enumerate(pairs):
                        sums[n] = sums[n] + v[a] * v[b]
        return tuple(sums)

    sums = list(lax.fori_loop(0, 3, products, tuple(jnp.zeros((8, 128), F32) for _ in pairs)))
    ps = [None, p1[0, 0], p2[0, 0], p3[0, 0]]
    for n, (a, b) in enumerate(pairs):
        if a:
            sums[n] = sums[n] + ps[a] * ps[b]
    fixed = jnp.zeros((4, 128), F32)
    for x in range(4):
        held = wall_in[x].astype(F32)
        for c in range(3):
            v = held * grad_in[c, x]
            fixed = fixed + v * v
    single = lane[0:1]
    row = jnp.zeros((1, 128), F32)
    for n in range(10):
        total = jnp.sum(jnp.sum(jnp.where(own, sums[n], 0.0), axis=0, keepdims=True), axis=1, keepdims=True)
        row = jnp.where(single == n, total, row)
    total = jnp.sum(jnp.sum(fixed, axis=0, keepdims=True), axis=1, keepdims=True)
    row = jnp.where(single == 10, total, row)

    def exchange(group, offsets, buffer, value):
        buffer[0] = value
        for n, o in enumerate(offsets):
            pltpu.make_async_remote_copy(
                src_ref=buffer.at[0], dst_ref=buffer.at[n + 1], send_sem=send.at[group], recv_sem=recv.at[group],
                device_id=device(o), device_id_type=MESH).start()

    def gathered(group, buffer):
        arrived(group)
        return jnp.sum(buffer[...], axis=0)

    if sizes[0] > 6:
        pl.semaphore_wait(across, 2)
    exchange(3, others, plane_sum, row)

    for n, u in enumerate((u1, u2)):
        for c in range(3):
            packed = []
            for i in range(2):
                for j in range(2):
                    packed.append(jnp.where(lane < 64, u[0, c, i, j, 0], pltpu.roll(u[0, c, i, j, 1], 64, 1)))
            flat = jnp.concatenate(packed, axis=0)
            flat = jnp.dot(flat, join, precision=HIGHEST, preferred_element_type=F32)
            for i in range(2):
                for j in range(2):
                    at8 = (i * 2 + j) * 8
                    for e in range(2):
                        natural[n, c, 2 * e + i, pl.ds(j, 2, stride=2), :] = flat[at8 + 4 * e + 1 : at8 + 4 * e + 3]

    row = gathered(3, plane_sum)
    if rounds:
        pl.semaphore_wait(reached.at[rounds - 1], 2)
    exchange(4, along, line_sum, row)
    row = gathered(4, line_sum)
    t = solve(row)
    for x in range(4):
        free = wall_in[x] == 0
        for c in range(3):
            b = grad_in[c, x]
            v = t[1] * natural[0, c, x, 0:4] + t[2] * natural[1, c, x, 0:4]
            vel_out[c, x] = jnp.where(free, t[0] * b, (t[0] + t[1] + t[2]) * b) + v
    v = t[1] * p1[0, 0] + t[2] * p2[0, 0]
    for e in range(2):
        pres_out[e] = v[4 * e + 1 : 4 * e + 3, 0:64]

    for group, ref in enumerate(in_all):
        pltpu.make_async_copy(ref, ref, send.at[group]).wait()


def hand_over(vel_in, pres_in, vel_out, pres_out, done):
    copies = [
        pltpu.make_async_copy(vel_in, vel_out, done.at[0]),
        pltpu.make_async_copy(pres_in, pres_out, done.at[1]),
    ]
    for copy in copies:
        copy.start()
    for copy in copies:
        copy.wait()


def local(sizes, state_velocity, objective_gradient, wall_flags, design_levels):
    vm = pltpu.VMEM
    plane, line = sizes[0] * sizes[1], sizes[2]
    tile = (8, 128)
    scratch = [
        vm((3, 4, 4, 128), F32),
        vm((3, 4, 4, 128), F32),
        vm((4, 4, 128), jnp.int32),
        vm((2, 2, 64), jnp.int32),
        vm((8, 2) + tile, F32),
        vm((8, 9, 16, 128), F32),
        vm((2, 4) + tile, F32),
        vm((2, 9, 16, 128), F32),
        vm((8, 9, 16, 128), F32),
        vm((8, 9, 16, 128), F32),
        vm((1, 9) + tile, F32),
        vm((2, 3, 3, 3, 2) + tile, F32),
        vm((2, 3, 3, 3, 2) + tile, F32),
        vm((1, 3, 3, 3, 2) + tile, F32),
        vm((2, 3, 3, 3, 2) + tile, F32),
        vm((1, 3, 3, 3, 2) + tile, F32),
        vm((1, 4) + tile, F32),
        vm((2, 4) + tile, F32),
        vm((1, 1) + tile, F32),
        vm((3, 3, 2) + tile, F32),
        vm((2,) + tile, F32),
        vm((2, 3, 3, 9) + tile, F32),
        vm((2, 3, 9, 9) + tile, F32),
        vm((3, 3, 3, 9) + tile, F32),
        vm((3, 9) + tile, F32),
        vm((3, 9) + tile, F32),
        vm((2, 3, 3, 3, 2) + tile, F32),
        vm((2, 4) + tile, F32),
        vm((7, 5) + tile, F32),
        vm((8, 7, 5) + tile, F32),
        vm((2, 3, 4) + tile, F32),
        vm((plane, 1, 128), F32),
        vm((line, 1, 128), F32),
    ]
    scratch += [
        pltpu.SemaphoreType.DMA((4,)),
        pltpu.SemaphoreType.REGULAR((4,)),
        pltpu.SemaphoreType.REGULAR,
        pltpu.SemaphoreType.DMA((5,)),
        pltpu.SemaphoreType.DMA((5,)),
    ]
    shapes = (
        jax.ShapeDtypeStruct((3, 4, 4, 128), F32),
        jax.ShapeDtypeStruct((2, 2, 64), F32),
    )
    grant = 56 * 1024 * 1024
    iterate = pl.pallas_call(
        functools.partial(kernel, sizes),
        out_shape=shapes,
        in_specs=[pl.BlockSpec(memory_space=pl.ANY)] * 4,
        out_specs=[pl.BlockSpec(memory_space=pltpu.VMEM)] * 2,
        scratch_shapes=scratch,
        compiler_params=pltpu.CompilerParams(
            collective_id=0, has_side_effects=True, vmem_limit_bytes=grant
        ),
    )(state_velocity, objective_gradient, wall_flags, design_levels)
    return pl.pallas_call(
        hand_over,
        out_shape=shapes,
        in_specs=[pl.BlockSpec(memory_space=pl.ANY)] * 2,
        out_specs=[pl.BlockSpec(memory_space=pl.ANY)] * 2,
        scratch_shapes=[pltpu.SemaphoreType.DMA((2,))],
        compiler_params=pltpu.CompilerParams(vmem_limit_bytes=grant),
    )(*iterate)


def solution(mesh):
    in_specs = (
        P(None, "gx", "gy", "gz"),
        P(None, "gx", "gy", "gz"),
        P("gx", "gy", "gz"),
        P("gx", "gy", "gz"),
    )
    out_specs = (P(None, "gx", "gy", "gz"), P("gx", "gy", "gz"))
    sizes = tuple(mesh.shape[a] for a in ("gx", "gy", "gz"))
    return jax.shard_map(
        functools.partial(local, sizes), mesh=mesh, in_specs=in_specs, out_specs=out_specs, check_vma=False
    )
```

```python
import functools
import itertools
import math

import jax
import jax.numpy as jnp
from jax import lax
from jax.experimental import pallas as pl
from jax.experimental.pallas import tpu as pltpu
from jax.sharding import PartitionSpec as P

MESH = pl.DeviceIdType.MESH
F32 = jnp.float32
HIGHEST = lax.Precision.HIGHEST

LEVELS = 9
PEAK = 8.0
SHAPE = 0.1

OFFSET = math.sqrt(0.15)
WIDEN = 9
SPREAD = 3
LINES = 9
GATHER = 3

RATIO = 5.0 / 8.0
SCALE = (8.0 / 18.0) ** 3

NEAR = [o for o in itertools.product((-1, 0, 1), repeat=3) if o != (0, 0, 0)]
NEAR.sort(key=lambda o: (o[2] == 0, -sum(map(abs, o))))
PLANE = [o for o in NEAR if o[2] == 0]

SOURCE = {-1: (2, 4), 0: (0, 4), 1: (0, 3)}
TARGET = {-1: (0, 2), 0: (2, 6), 1: (6, 9)}

PART_ROWS = {-1: (4, 0, 3), 0: (2, 2, 5), 1: (2, 6, 1)}


def forward_both(a, b, c):
    d = c - a
    w = (b + b) - (a + c)
    s = (4.0 * OFFSET) * w
    m = b - 0.3 * w
    e = OFFSET * d
    return (m - e, b, m + e), (d + s, d, d - s)


def forward_value(a, b, c):
    d = c - a
    w = (b + b) - (a + c)
    m = b - 0.3 * w
    e = OFFSET * d
    return (m - e, b, m + e)


def back_value(f):
    s = f[0] + f[2]
    a = (0.3 * RATIO) * s
    b = (OFFSET * RATIO) * (f[2] - f[0])
    return (a - b, f[1] + (0.4 * RATIO) * s, a + b)


def back_both(f, g):
    s = f[0] + f[2]
    b = (OFFSET * RATIO) * (f[2] - f[0]) + (RATIO * (g[0] + g[2]) + g[1])
    w = (4.0 * OFFSET * RATIO) * (g[0] - g[2])
    a = (0.3 * RATIO) * s - w
    return (a - b, f[1] + (0.4 * RATIO) * s + (w + w), a + b)


def forward_linear(a, b):
    m = 0.5 * (a + b)
    d = OFFSET * (b - a)
    return (m - d, m, m + d)


def back_linear(f):
    m = (0.5 * RATIO) * (f[0] + f[2]) + 0.5 * f[1]
    d = (OFFSET * RATIO) * (f[2] - f[0])
    return (m - d, m + d)


def next_lane(v):
    return pltpu.roll(v, 127, v.ndim - 1)


def last_lane(v):
    return pltpu.roll(v, 1, v.ndim - 1)


def next_row(v):
    return pltpu.roll(v, 7, 0)


def last_row(v):
    return pltpu.roll(v, 1, 0)


def half_turn(v):
    return pltpu.roll(v, 4, 0)


def blocks(count, size, body):
    if size == count:
        body(0)
        return

    def one(n, carry):
        body(n * size)
        return carry

    lax.fori_loop(0, count // size, one, 0)


def spread(elements, chunk, fields):
    def one(c):
        at = pl.ds(c, SPREAD)
        along = []
        for j in range(3):
            even = elements[chunk, at, :, j, 0]
            along.append(forward_both(even, elements[chunk, at, :, j, 1], next_lane(even)))
        for q in range(3):
            value, slope = forward_both(*[along[j][0][q] for j in range(3)])
            zslope = forward_value(*[along[j][1][q] for j in range(3)])
            for p in range(3):
                fields[at, :, 0, p * 3 + q] = value[p]
                fields[at, :, 1, p * 3 + q] = slope[p]
                fields[at, :, 2, p * 3 + q] = zslope[p]

    blocks(3, SPREAD, one)


def at_points(fields, lines, c):
    value, xslope = forward_both(*[fields[c, i, 0, lines] for i in range(3)])
    yslope = forward_value(*[fields[c, i, 1, lines] for i in range(3)])
    zslope = forward_value(*[fields[c, i, 2, lines] for i in range(3)])
    return value, xslope, yslope, zslope


def apply_operator(above_floor, elements, pressures, chunk, state, slopes, fields, qpoints, ppoints, out, pout):
    low_half = lax.broadcasted_iota(jnp.int32, (8, 128), 0) < 4
    planes = [0, 1, 2] if chunk == 0 else [0]
    spread(elements, chunk, fields)
    if pressures is not None:
        corner = {}
        for i in range(2):
            for j in range(2):
                low = pressures[chunk, i * 2 + j]
                corner[i, j] = forward_linear(low, next_lane(low))
        for q in range(3):
            sides = [forward_linear(corner[i, 0][q], corner[i, 1][q]) for i in range(2)]
            for p in range(3):
                points = forward_linear(sides[0][p], sides[1][p])
                for r in range(3):
                    qpoints[r, p * 3 + q] = points[r]

    def one(line):
        lines = pl.ds(line, LINES)
        value, slope = [], []
        for c in range(3):
            v, gx, gy, gz = at_points(fields, lines, c)
            value.append(v)
            slope.append((gx, gy, gz))
        force = [[None] * 3 for _ in range(3)]
        flux = [[[None] * 3 for _ in range(3)] for _ in range(3)]
        for r in range(3):
            ppoints[r, lines] = slope[0][0][r] + slope[1][1][r] + slope[2][2][r]
            wind = [state[chunk, r, b, lines] for b in range(3)]
            pressure = qpoints[r, lines] if pressures is not None else None
            for a in range(3):
                for b in range(3):
                    g = slope[a][b][r] + value[a][r] * wind[b]
                    if a == b and pressures is not None:
                        g = g - pressure
                    flux[a][b][r] = g
                total = slopes[chunk, r, a * 3, lines] * value[0][r]
                for c in range(1, 3):
                    total = total + slopes[chunk, r, a * 3 + c, lines] * value[c][r]
                force[a][r] = total
        for c in range(3):
            first = back_both(force[c], flux[c][0])
            second = back_value(flux[c][1])
            third = back_value(flux[c][2])
            if chunk == 1:
                first, second, third = [[jnp.where(low_half, v[0], v[2])] for v in (first, second, third)]
            for i in planes:
                fields[c, i, 0, lines] = first[i]
                fields[c, i, 1, lines] = second[i]
                fields[c, i, 2, lines] = third[i]

    blocks(9, LINES, one)

    def gather(c):
        at = pl.ds(c, GATHER)
        value, zslope = [], []
        for q in range(3):
            value.append(
                back_both(
                    [fields[at, 0 : len(planes), 0, p * 3 + q] for p in range(3)],
                    [fields[at, 0 : len(planes), 1, p * 3 + q] for p in range(3)],
                )
            )
            zslope.append(back_value([fields[at, 0 : len(planes), 2, p * 3 + q] for p in range(3)]))
        for j in range(3):
            nodes = back_both([value[q][j] for q in range(3)], [zslope[q][j] for q in range(3)])
            out[chunk, at, 0 : len(planes), j, 0] = nodes[0] + last_lane(jnp.where(above_floor, nodes[2], 0.0))
            out[chunk, at, 0 : len(planes), j, 1] = nodes[1]

    blocks(3, GATHER, gather)
    rows = {}
    for q in range(3):
        sides = []
        for p in range(3):
            v = back_linear([ppoints[r, p * 3 + q] for r in range(3)])
            sides.append(v if chunk == 0 else [jnp.where(low_half, v[0], v[1])])
        for i in planes[:2]:
            rows[i, q] = back_linear([sides[p][i] for p in range(3)])
    for i in planes[:2]:
        for j in range(2):
            low, high = back_linear([rows[i, q][j] for q in range(3)])
            pout[chunk, i * 2 + j] = low + last_lane(jnp.where(above_floor, high, 0.0))


def pick(row, k):
    lane = lax.broadcasted_iota(jnp.int32, (1, 128), 1)
    return jnp.sum(jnp.where(lane == k, row, 0.0), axis=1, keepdims=True)


def solve(row):
    entries = {}
    at = 0
    for i in range(4):
        for j in range(i, 4):
            entries[i, j] = pick(row, at) + pick(row, 10)
            at += 1
    m = [[entries[min(i, j), max(i, j)] for j in range(1, 4)] + [entries[0, i]] for i in range(1, 4)]
    for k in range(2):
        inverse = 1.0 / m[k][k]
        for i in range(k + 1, 3):
            factor = m[i][k] * inverse
            for j in range(k + 1, 4):
                m[i][j] = m[i][j] - factor * m[k][j]
    t = [None] * 3
    for k in (2, 1, 0):
        total = m[k][3]
        for j in range(k + 1, 3):
            total = total - m[k][j] * t[j]
        t[k] = total / m[k][k]
    return t


def kernel(sizes, state_far, grad_far, wall_far, level_far, vel_out, pres_out,
           state_in, grad_in, wall_in, level_in, raw, nodes, ends, reach, even, odd, stiff, u0, us, u1, u2, u3, p1, p2, p3, keep_e, friction,
           wind, slopes, fields, qpoints, ppoints, out, pout, block, side, natural, plane_sum, line_sum,
           load, reached, across, send, recv):
    loads = [
        pltpu.make_async_copy(far, near, load.at[n])
        for n, (far, near) in enumerate(
            ((grad_far, grad_in), (state_far, state_in), (wall_far, wall_in), (level_far, level_in)))
    ]
    for copy in loads:
        copy.start()

    gx, gy, gz = lax.axis_index("gx"), lax.axis_index("gy"), lax.axis_index("gz")

    def device(o):
        return tuple(lax.rem(a + d + n, n) for a, d, n in zip((gx, gy, gz), o, sizes))

    others = [(a, b, 0) for a in range(sizes[0]) for b in range(sizes[1]) if (a, b) != (0, 0)]
    along = [(0, 0, d) for d in range(1, sizes[2])]
    partners = {tuple(d % n for d, n in zip(o, sizes)) for o in NEAR}

    def far_first(offsets):
        return sorted(offsets, key=lambda o: (-sum(min(d, n - d) for d, n in zip(o, sizes)), o))

    partners, others, along = far_first(partners - {(0, 0, 0)}), far_first(others), far_first(along)

    barrier = pltpu.get_barrier_semaphore()
    for o in partners:
        pl.semaphore_signal(barrier, inc=1, device_id=device(o), device_id_type=MESH)

    lane = lax.broadcasted_iota(jnp.int32, (8, 128), 1)
    sub = lax.broadcasted_iota(jnp.int32, (8, 128), 0)

    for n, o in enumerate(PLANE):
        first, count = PART_ROWS[-o[1]][1:]
        for lo, hi in ((0, first), (first + count, 8)):
            if lo < hi:
                side[n, :, :, lo:hi] = jnp.zeros((7, 5, hi - lo, 128), F32)

    for copy in loads:
        copy.wait()

    for x in range(4):
        spot = pl.ds((x % 2) * 4, 4)
        mask = 1.0 - wall_in[x].astype(F32)
        for c in range(3):
            raw[c, x // 2, spot] = mask * grad_in[c, x]
            raw[3 + c, x // 2, spot] = state_in[c, x]
        raw[6, x // 2, spot] = mask
    rows = lax.broadcasted_iota(jnp.int32, (128, 128), 0)
    cols = lax.broadcasted_iota(jnp.int32, (128, 128), 1)
    split = (rows == jnp.where(cols < 64, 2 * cols, 2 * cols - 127)).astype(F32)
    join = (cols == jnp.where(rows < 64, 2 * rows, 2 * rows - 127)).astype(F32)
    parted = jnp.dot(raw[0:7].reshape(112, 128), split, precision=HIGHEST, preferred_element_type=F32)
    parted = parted.reshape(7, 2, 8, 128)
    twice = (rows[:64] == jnp.where(cols[:64] < 64, cols[:64], cols[:64] - 64)).astype(F32)
    density = level_in[...].astype(F32) / (LEVELS - 1)
    drag = PEAK * SHAPE * (1.0 - density) / (SHAPE + density)
    for h in range(2):
        wide = jnp.dot(drag[h], twice, precision=HIGHEST, preferred_element_type=F32)
        for y in range(4):
            raw[7, h, y : y + 1] = wide[y // 2 : y // 2 + 1]
            raw[7, h, y + 4 : y + 5] = wide[y // 2 : y // 2 + 1]
    for h in range(2):
        first = jnp.zeros((8, 128), F32)
        last = jnp.zeros((8, 128), F32)
        for f in range(8):
            v = raw[7, h] if f == 6 else parted[6 if f == 7 else f, h]
            for xl in range(2):
                nodes[f, 2 + 2 * h + xl, 2:6] = v[4 * xl : 4 * xl + 4]
            go = 8 * f
            lower = (lane >= go) & (lane < go + 4)
            upper = (lane >= go + 4) & (lane < go + 8)
            first = jnp.where(lower, pltpu.roll(v, go, 1), first)
            first = jnp.where(upper, pltpu.roll(v, (go + 4 - 64) % 128, 1), first)
            last = jnp.where(lower, pltpu.roll(v, (go - 60) % 128, 1), last)
            last = jnp.where(upper, pltpu.roll(v, (go + 4 - 124) % 128, 1), last)
        for xl in range(2):
            ends[0, 2 * h + xl, 0:4] = last[4 * xl : 4 * xl + 4]
            ends[1, 2 * h + xl, 0:4] = first[4 * xl : 4 * xl + 4]

    pl.semaphore_wait(barrier, len(partners))

    def tell(n):
        for d in (-1, 1):
            pl.semaphore_signal(
                reached.at[n], inc=1, device_id=device((0, 0, d * 2**n)), device_id_type=MESH)

    rounds = 0
    while 2**rounds < sizes[2] // 2:
        rounds += 1
    if rounds:
        tell(0)

    for o in NEAR:
        sx, sy = -o[0], -o[1]
        (xs, xe), (ys, ye) = SOURCE[sx], SOURCE[sy]
        (tx, te), (ty, tf) = TARGET[sx], TARGET[sy]
        if o[2] == 0:
            source = nodes.at[:, 2 + xs : 2 + xe, 2 + ys : 2 + ye]
            target = nodes.at[:, tx:te, ty:tf]
            group = 0
        else:
            group = 1
            which = 0 if o[2] == 1 else 1
            source = ends.at[which, xs:xe, ys:ye]
            target = reach.at[which, tx:te, ty:tf]
        pltpu.make_async_remote_copy(
            src_ref=source, dst_ref=target, send_sem=send.at[group], recv_sem=recv.at[group],
            device_id=device(o), device_id_type=MESH).start()

    in_all = [
        nodes.at[:, 0:5, 0:13],
        reach.at[:, :, 0:9],
        side.at[0:7, :, 0:1],
        plane_sum.at[1 : len(others) + 1],
        line_sum.at[1 : len(along) + 1],
    ]

    def arrived(group):
        ref = in_all[group]
        pltpu.make_async_copy(ref, ref, recv.at[group]).wait()

    ey = sub % 4 - 1
    z = jnp.where(lane < 96, lane, lane - 128)
    zmin = jnp.where(gz > 0, -3, 0)
    zmax = jnp.where(gz < sizes[2] - 1, 65, 63)
    in_z = (z >= zmin) & (z <= zmax)
    ymin = jnp.where(gy > 0, -1, 0)
    ymax = jnp.where(gy < sizes[1] - 1, 2, 1)
    xmin = jnp.where(gx > 0, -1, 0)
    xmax = jnp.where(gx < sizes[0] - 1, 2, 1)
    ex = [jnp.where(sub < 4, 0, 1), jnp.where(sub < 4, 2, -1)]
    real = [in_z & (ey >= ymin) & (ey <= ymax) & (e >= xmin) & (e <= xmax) for e in ex]
    narrow = [r & (ey <= 1) & (e <= 1) for r, e in zip(real, ex)]
    own_y = (ey >= 0) & (ey <= 1)
    own_wide = in_z & own_y
    own = own_y & (lane < 64)
    zlim = jnp.where(gz < sizes[2] - 1, 64, 96)
    node_z = (lane < 64) | (lane >= zlim)
    above_floor = lane < jnp.where(gz > 0, 128, 96)
    ylim = jnp.where(gy < sizes[1] - 1, 99, 6)
    xlim = jnp.where(gx < sizes[0] - 1, 99, 6)
    node_yz = [node_z & (sub + 8 * h < ylim) for h in range(2)]

    if rounds > 1:
        pl.semaphore_wait(reached.at[0], 2)
        tell(1)
    arrived(0)
    arrived(1)
    if sizes[0] > 6:
        for d in (-2, 2):
            pl.semaphore_signal(across, inc=1, device_id=device((d, 0, 0)), device_id_type=MESH)

    def widen(first):
        xs = pl.ds(first, WIDEN)
        column = first + lax.broadcasted_iota(jnp.int32, (WIDEN, 8, 128), 0)
        inside = column < xlim
        for h in range(2):
            rows8 = pl.ds(8 * h, 8)
            below = reach[0, xs, rows8]
            above = reach[1, xs, rows8]
            ok = inside & node_yz[h]
            for f in range(8 if h == 0 else 6):
                v = nodes[f, xs, rows8]
                go = 8 * f
                e = jnp.where(lane < 96, pltpu.roll(above, (64 - go) % 128, 2), pltpu.roll(below, (124 - go) % 128, 2))
                e = jnp.where(lane < 64, v, e)
                if f == 6:
                    stiff[0, xs] = e
                    continue
                here = ok & ((sub >= 2) & (sub < 7)) if f == 7 else ok
                even[f, xs, rows8] = jnp.where(here, e, 0.0)
                o = jnp.where(lane < 96, pltpu.roll(above, (60 - go) % 128, 2), pltpu.roll(below, (120 - go) % 128, 2))
                o = jnp.where(lane < 64, pltpu.roll(v, 64, 2), o)
                odd[f, xs, rows8] = jnp.where(here, o, 0.0)

    blocks(9, WIDEN, widen)

    def to_elements(source, f, x, j):
        return source[f, x, pl.ds(j, 4, stride=2), :]

    def collect(first, target, masks):
        three = pl.ds(first, 3)
        for i in range(3):
            for j in range(3):
                for k, source in enumerate((even, odd)):
                    for chunk, (low, high) in enumerate(((2, 4), (6, 0))):
                        v = jnp.concatenate(
                            [to_elements(source, three, low + i, j), to_elements(source, three, high + i, j)], axis=1)
                        if masks is not None:
                            v = jnp.where(masks[chunk], v, 0.0)
                        target[chunk, :, i, j, k] = v

    collect(0, u0, real)
    collect(3, us, None)
    for i in range(3):
        for j in range(3):
            for k, source in enumerate((even, odd)):
                keep_e[i, j, k] = SCALE * jnp.concatenate(
                    [to_elements(source, 7, 2 + i, j), to_elements(source, 7, 4 + i, j)], axis=0)
    for chunk, (low, high) in enumerate(((2, 4), (6, 0))):
        friction[chunk] = jnp.concatenate([to_elements(stiff, 0, low, 0), to_elements(stiff, 0, high, 0)], axis=0)

    def prepare(chunk, carry):
        spread(us, chunk, fields)

        def one(line):
            lines = pl.ds(line, LINES)
            for c in range(3):
                v, gx_, gy_, gz_ = at_points(fields, lines, c)
                for r in range(3):
                    wind[chunk, r, c, lines] = v[r]
                    for b, g in enumerate((gx_, gy_, gz_)):
                        slopes[chunk, r, b * 3 + c, lines] = g[r] + friction[chunk] if b == c else g[r]

        blocks(9, LINES, one)
        return carry

    for chunk in range(2):
        prepare(chunk, 0)

    def first_step(chunk, carry):
        apply_operator(above_floor, u0, None, chunk, wind, slopes, fields, qpoints, ppoints, out, pout)
        return carry

    for chunk in range(2):
        first_step(chunk, 0)

    low_half = sub < 4

    def owners(source, at, last):
        total = {}
        for chunk in range(2):
            for i in range(last + 1) if chunk == 0 else (0,):
                v = [at(source, chunk, i, j) for j in range(last + 1)]
                total[chunk, i, 0] = v[0] + last_row(v[last])
                for j in range(1, last):
                    total[chunk, i, j] = v[j]
        for j in range(last):
            total[1, last, j] = total[1, 0, j]
        return total

    def close(total, last):
        full = {}
        edge = {}
        for j in range(last):
            before = half_turn(total[1, last, j])
            mine = half_turn(total[0, last, j])
            full[0, j] = total[0, 0, j] + jnp.where(low_half, before, mine)
            edge[j] = total[1, 0, j] + mine
            for i in range(1, last):
                full[i, j] = total[0, i, j]
        return full, edge

    def complete(full, edge, last):
        for j in range(last):
            full[last, j] = jnp.where(low_half, half_turn(full[0, j]), half_turn(edge[j]))
        for i in range(last + 1):
            full[i, last] = next_row(full[i, 0])
        return full

    def finish_first(c, carry):
        for k in range(2):
            total = owners(out, lambda s, chunk, i, j: s[chunk, c, i, j, k], 2)
            full = complete(*close(total, 2), 2)
            for i in range(3):
                for j in range(3):
                    u1[0, c, i, j, k] = jnp.where(own_wide, full[i, j] * keep_e[i, j, k], 0.0)
        return carry

    [finish_first(c, 0) for c in range(3)]

    def vertex_mask(i, j):
        ok = own_wide & ((lane < 64) | (lane >= zlim))
        ylast = jnp.where(gy < sizes[1] - 1, 99, 2)
        xlast = jnp.where(gx < sizes[0] - 1, 99, 2)
        return ok & (ey + j < ylast) & (ex[0] + i < xlast)

    full = complete(*close(owners(pout, lambda s, chunk, i, j: s[chunk, i * 2 + j], 1), 1), 1)
    for i in range(2):
        for j in range(2):
            p1[0, i * 2 + j] = jnp.where(vertex_mask(i, j), -SCALE * full[i, j], 0.0)

    if rounds > 2:
        pl.semaphore_wait(reached.at[1], 2)
        tell(2)

    apply_operator(above_floor, u1, p1, 0, wind, slopes, fields, qpoints, ppoints, out, pout)

    def store_rows(plane, x, parity, v, step):
        block[plane, x, pl.ds(parity, 4, stride=step), :] = v

    for n in range(7):
        last = 2 if n < 6 else 1
        c, k = n // 2, n % 2

        def at(i, j):
            return out[0, c, i, j, k] if n < 6 else pout[0, i * 2 + j]

        for j in range(last):
            v = [at(i, 0) + last_row(at(i, last)) if j == 0 else at(i, j) for i in range(last + 1)]
            if n == 6:
                v = [-SCALE * w for w in v]
            step = 2 // last
            turned = [half_turn(w) for w in v]
            for i in range(last):
                store_rows(n, step * i, j, v[i][0:4], 2)
            store_rows(n, 2, j, (v[last] + turned[0])[0:4], 2)
            for i in range(1, last):
                store_rows(n, 2 + i, j, turned[i][0:4], 2)
            store_rows(n, 4, j, turned[last][0:4], 2)
    vertex_yz = jnp.where(node_yz[0], 1.0, 0.0)
    for x in range(5):
        inside = jnp.where(x + 2 < xlim, 1.0, 0.0).astype(F32)
        for k, source in enumerate((even, odd)):
            mask = SCALE * source[7, x + 2, 0:8]
            for c in range(3):
                block[2 * c + k, x] = block[2 * c + k, x] * mask
        if x % 2 == 0:
            odd_rows = sub % 2 == 1
            block[6, x] = jnp.where(odd_rows, 0.0, block[6, x] * (vertex_yz * inside))
        else:
            block[6, x] = jnp.zeros((8, 128), F32)

    for n, o in enumerate(PLANE):
        sx, sy = -o[0], -o[1]
        xs, xe = {-1: (2, 5), 0: (0, 5), 1: (0, 1)}[sx]
        ys, ty, count = PART_ROWS[sy]
        pltpu.make_async_remote_copy(
            src_ref=block.at[:, xs:xe, ys : ys + count], dst_ref=side.at[n, :, 0 : xe - xs, ty : ty + count],
            send_sem=send.at[2], recv_sem=recv.at[2], device_id=device(o), device_id_type=MESH).start()

    have = {0: 1.0}
    have_x = {-1: jnp.where(gx > 0, 1.0, 0.0).astype(F32), 1: jnp.where(gx < sizes[0] - 1, 1.0, 0.0).astype(F32)}
    have_y = {-1: jnp.where(gy > 0, 1.0, 0.0).astype(F32), 1: jnp.where(gy < sizes[1] - 1, 1.0, 0.0).astype(F32)}
    arrived(2)
    if rounds > 3:
        pl.semaphore_wait(reached.at[2], 2)
        tell(3)

    def part(n, plane, x):
        sx, sy = -PLANE[n][0], -PLANE[n][1]
        v = side[n, plane, x]
        if sx:
            v = v * have_x[sx]
        if sy:
            v = v * have_y[sy]
        return v

    slot = {(-o[0], -o[1]): n for n, o in enumerate(PLANE)}

    def join_parts(plane, target, f):
        for x in range(7):
            total = block[plane, x - 2] if x >= 2 else None
            for sx in (-1, 0, 1):
                lo, hi = {-1: (0, 2), 0: (2, 6), 1: (6, 6)}[sx]
                if not lo <= x <= hi:
                    continue
                for sy in (-1, 0, 1):
                    if (sx, sy) != (0, 0):
                        v = part(slot[sx, sy], plane, x - lo)
                        total = v if total is None else total + v
            target[f, x, 0:8] = total

    def join_component(c, carry):
        join_parts(2 * c, even, c)
        join_parts(2 * c + 1, odd, c)
        return carry

    [join_component(c, 0) for c in range(3)]
    join_parts(6, even, 3)
    collect(0, u2, narrow)
    for i in range(2):
        for j in range(2):
            for chunk, (low, high) in enumerate(((2, 4), (6, 0))):
                v = jnp.concatenate(
                    [to_elements(even, 3, low + 2 * i, 2 * j), to_elements(even, 3, high + 2 * i, 2 * j)], axis=0)
                p2[chunk, i * 2 + j] = jnp.where(narrow[chunk], v, 0.0)

    def last_step(chunk, carry):
        apply_operator(above_floor, u2, p2, chunk, wind, slopes, fields, qpoints, ppoints, out, pout)
        return carry

    for chunk in range(2):
        last_step(chunk, 0)

    def finish_last(c, carry):
        for k in range(2):
            total = owners(out, lambda s, chunk, i, j: s[chunk, c, i, j, k], 2)
            full, _ = close(total, 2)
            for i in range(2):
                for j in range(2):
                    u3[0, c, i, j, k] = full[i, j] * keep_e[i, j, k]
        return carry

    [finish_last(c, 0) for c in range(3)]
    full, _ = close(owners(pout, lambda s, chunk, i, j: s[chunk, i * 2 + j], 1), 1)
    p3[0, 0] = -SCALE * full[0, 0]

    pairs = [(i, j) for i in range(4) for j in range(i, 4)]

    def products(c, sums):
        sums = list(sums)
        for i in range(2):
            for j in range(2):
                for k in range(2):
                    v = [u[0, c, i, j, k] for u in (u0, u1, u2, u3)]
                    for n, (a, b) in enumerate(pairs):
                        sums[n] = sums[n] + v[a] * v[b]
        return tuple(sums)

    sums = list(lax.fori_loop(0, 3, products, tuple(jnp.zeros((8, 128), F32) for _ in pairs)))
    ps = [None, p1[0, 0], p2[0, 0], p3[0, 0]]
    for n, (a, b) in enumerate(pairs):
        if a:
            sums[n] = sums[n] + ps[a] * ps[b]
    fixed = jnp.zeros((4, 128), F32)
    for x in range(4):
        held = wall_in[x].astype(F32)
        for c in range(3):
            v = held * grad_in[c, x]
            fixed = fixed + v * v
    single = lane[0:1]
    row = jnp.zeros((1, 128), F32)
    for n in range(10):
        total = jnp.sum(jnp.sum(jnp.where(own, sums[n], 0.0), axis=0, keepdims=True), axis=1, keepdims=True)
        row = jnp.where(single == n, total, row)
    total = jnp.sum(jnp.sum(fixed, axis=0, keepdims=True), axis=1, keepdims=True)
    row = jnp.where(single == 10, total, row)

    def exchange(group, offsets, buffer, value):
        buffer[0:1] = value
        for n, o in enumerate(offsets):
            pltpu.make_async_remote_copy(
                src_ref=buffer.at[0:1], dst_ref=buffer.at[n + 1 : n + 2], send_sem=send.at[group], recv_sem=recv.at[group],
                device_id=device(o), device_id_type=MESH).start()

    def gathered(group, buffer):
        arrived(group)
        return jnp.sum(buffer[...], axis=0, keepdims=True)

    if sizes[0] > 6:
        pl.semaphore_wait(across, 2)
    exchange(3, others, plane_sum, row)

    for n, u in enumerate((u1, u2)):
        for c in range(3):
            packed = []
            for i in range(2):
                for j in range(2):
                    packed.append(jnp.where(lane < 64, u[0, c, i, j, 0], pltpu.roll(u[0, c, i, j, 1], 64, 1)))
            flat = jnp.concatenate(packed, axis=0)
            flat = jnp.dot(flat, join, precision=HIGHEST, preferred_element_type=F32)
            for i in range(2):
                for j in range(2):
                    at8 = (i * 2 + j) * 8
                    for e in range(2):
                        natural[n, c, 2 * e + i, pl.ds(j, 2, stride=2), :] = flat[at8 + 4 * e + 1 : at8 + 4 * e + 3]

    row = gathered(3, plane_sum)
    if rounds:
        pl.semaphore_wait(reached.at[rounds - 1], 2)
    exchange(4, along, line_sum, row)
    row = gathered(4, line_sum)
    t = solve(row)
    for x in range(4):
        free = wall_in[x] == 0
        for c in range(3):
            b = grad_in[c, x]
            v = t[1] * natural[0, c, x, 0:4] + t[2] * natural[1, c, x, 0:4]
            vel_out[c, x] = jnp.where(free, t[0] * b, (t[0] + t[1] + t[2]) * b) + v
    v = t[1] * p1[0, 0] + t[2] * p2[0, 0]
    for e in range(2):
        pres_out[e] = v[4 * e + 1 : 4 * e + 3, 0:64]

    for group, ref in enumerate(in_all):
        pltpu.make_async_copy(ref, ref, send.at[group]).wait()


def hand_over(vel_in, pres_in, vel_out, pres_out, vel, pres, done):
    for stage in (((vel_in, vel), (pres_in, pres)), ((vel, vel_out), (pres, pres_out))):
        copies = [pltpu.make_async_copy(a, b, done.at[n]) for n, (a, b) in enumerate(stage)]
        for copy in copies:
            copy.start()
        for copy in copies:
            copy.wait()


def local(sizes, state_velocity, objective_gradient, wall_flags, design_levels):
    vm = pltpu.VMEM
    plane, line = sizes[0] * sizes[1], sizes[2]
    tile = (8, 128)
    scratch = [
        vm((3, 4, 4, 128), F32),
        vm((3, 4, 4, 128), F32),
        vm((4, 4, 128), jnp.int32),
        vm((2, 2, 64), jnp.int32),
        vm((8, 2) + tile, F32),
        vm((8, 9, 16, 128), F32),
        vm((2, 4) + tile, F32),
        vm((2, 9, 16, 128), F32),
        vm((8, 9, 16, 128), F32),
        vm((8, 9, 16, 128), F32),
        vm((1, 9) + tile, F32),
        vm((2, 3, 3, 3, 2) + tile, F32),
        vm((2, 3, 3, 3, 2) + tile, F32),
        vm((1, 3, 3, 3, 2) + tile, F32),
        vm((2, 3, 3, 3, 2) + tile, F32),
        vm((1, 3, 3, 3, 2) + tile, F32),
        vm((1, 4) + tile, F32),
        vm((2, 4) + tile, F32),
        vm((1, 1) + tile, F32),
        vm((3, 3, 2) + tile, F32),
        vm((2,) + tile, F32),
        vm((2, 3, 3, 9) + tile, F32),
        vm((2, 3, 9, 9) + tile, F32),
        vm((3, 3, 3, 9) + tile, F32),
        vm((3, 9) + tile, F32),
        vm((3, 9) + tile, F32),
        vm((2, 3, 3, 3, 2) + tile, F32),
        vm((2, 4) + tile, F32),
        vm((7, 5) + tile, F32),
        vm((8, 7, 5) + tile, F32),
        vm((2, 3, 4) + tile, F32),
        vm((plane, 128), F32),
        vm((line, 128), F32),
    ]
    scratch += [
        pltpu.SemaphoreType.DMA((4,)),
        pltpu.SemaphoreType.REGULAR((4,)),
        pltpu.SemaphoreType.REGULAR,
        pltpu.SemaphoreType.DMA((5,)),
        pltpu.SemaphoreType.DMA((5,)),
    ]
    shapes = (
        jax.ShapeDtypeStruct((3, 4, 4, 128), F32),
        jax.ShapeDtypeStruct((2, 2, 64), F32),
    )
    grant = 56 * 1024 * 1024
    iterate = pl.pallas_call(
        functools.partial(kernel, sizes),
        out_shape=shapes,
        in_specs=[pl.BlockSpec(memory_space=pl.ANY)] * 4,
        out_specs=[pl.BlockSpec(memory_space=pltpu.VMEM)] * 2,
        scratch_shapes=scratch,
        compiler_params=pltpu.CompilerParams(
            collective_id=0, has_side_effects=True, vmem_limit_bytes=grant
        ),
    )(state_velocity, objective_gradient, wall_flags, design_levels)
    return pl.pallas_call(
        hand_over,
        out_shape=shapes,
        in_specs=[pl.BlockSpec(memory_space=pl.ANY)] * 2,
        out_specs=[pl.BlockSpec(memory_space=pl.ANY)] * 2,
        scratch_shapes=[vm((3, 4, 4, 128), F32), vm((2, 2, 64), F32), pltpu.SemaphoreType.DMA((2,))],
        compiler_params=pltpu.CompilerParams(vmem_limit_bytes=grant),
    )(*iterate)


def solution(mesh):
    in_specs = (
        P(None, "gx", "gy", "gz"),
        P(None, "gx", "gy", "gz"),
        P("gx", "gy", "gz"),
        P("gx", "gy", "gz"),
    )
    out_specs = (P(None, "gx", "gy", "gz"), P("gx", "gy", "gz"))
    sizes = tuple(mesh.shape[a] for a in ("gx", "gy", "gz"))
    return jax.shard_map(
        functools.partial(local, sizes), mesh=mesh, in_specs=in_specs, out_specs=out_specs, check_vma=False
    )
```

```python
import functools
import itertools
import math

import jax
import jax.numpy as jnp
from jax import lax
from jax.experimental import pallas as pl
from jax.experimental.pallas import tpu as pltpu
from jax.sharding import PartitionSpec as P

MESH = pl.DeviceIdType.MESH
F32 = jnp.float32
HIGHEST = lax.Precision.HIGHEST

LEVELS = 9
PEAK = 8.0
SHAPE = 0.1

OFFSET = math.sqrt(0.15)
WIDEN = 9
SPREAD = 3
LINES = 9
GATHER = 3

RATIO = 5.0 / 8.0
SCALE = (8.0 / 18.0) ** 3

NEAR = [o for o in itertools.product((-1, 0, 1), repeat=3) if o != (0, 0, 0)]
NEAR.sort(key=lambda o: (o[2] == 0, -sum(map(abs, o))))
PLANE = [o for o in NEAR if o[2] == 0]

SOURCE = {-1: (2, 4), 0: (0, 4), 1: (0, 3)}
TARGET = {-1: (0, 2), 0: (2, 6), 1: (6, 9)}

PART_ROWS = {-1: (4, 0, 3), 0: (2, 2, 5), 1: (2, 6, 1)}


def forward_both(a, b, c):
    d = c - a
    w = (b + b) - (a + c)
    s = (4.0 * OFFSET) * w
    m = b - 0.3 * w
    e = OFFSET * d
    return (m - e, b, m + e), (d + s, d, d - s)


def forward_value(a, b, c):
    d = c - a
    w = (b + b) - (a + c)
    m = b - 0.3 * w
    e = OFFSET * d
    return (m - e, b, m + e)


def back_value(f):
    s = f[0] + f[2]
    a = (0.3 * RATIO) * s
    b = (OFFSET * RATIO) * (f[2] - f[0])
    return (a - b, f[1] + (0.4 * RATIO) * s, a + b)


def back_both(f, g):
    s = f[0] + f[2]
    b = (OFFSET * RATIO) * (f[2] - f[0]) + (RATIO * (g[0] + g[2]) + g[1])
    w = (4.0 * OFFSET * RATIO) * (g[0] - g[2])
    a = (0.3 * RATIO) * s - w
    return (a - b, f[1] + (0.4 * RATIO) * s + (w + w), a + b)


def forward_linear(a, b):
    m = 0.5 * (a + b)
    d = OFFSET * (b - a)
    return (m - d, m, m + d)


def back_linear(f):
    m = (0.5 * RATIO) * (f[0] + f[2]) + 0.5 * f[1]
    d = (OFFSET * RATIO) * (f[2] - f[0])
    return (m - d, m + d)


def next_lane(v):
    return pltpu.roll(v, 127, v.ndim - 1)


def last_lane(v):
    return pltpu.roll(v, 1, v.ndim - 1)


def next_row(v):
    return pltpu.roll(v, 7, 0)


def last_row(v):
    return pltpu.roll(v, 1, 0)


def half_turn(v):
    return pltpu.roll(v, 4, 0)


def blocks(count, size, body):
    if size == count:
        body(0)
        return

    def one(n, carry):
        body(n * size)
        return carry

    lax.fori_loop(0, count // size, one, 0)


def spread(elements, chunk, fields):
    def one(c):
        at = pl.ds(c, SPREAD)
        along = []
        for j in range(3):
            even = elements[chunk, at, :, j, 0]
            along.append(forward_both(even, elements[chunk, at, :, j, 1], next_lane(even)))
        for q in range(3):
            value, slope = forward_both(*[along[j][0][q] for j in range(3)])
            zslope = forward_value(*[along[j][1][q] for j in range(3)])
            for p in range(3):
                fields[at, :, 0, p * 3 + q] = value[p]
                fields[at, :, 1, p * 3 + q] = slope[p]
                fields[at, :, 2, p * 3 + q] = zslope[p]

    blocks(3, SPREAD, one)


def at_points(fields, lines, c):
    value, xslope = forward_both(*[fields[c, i, 0, lines] for i in range(3)])
    yslope = forward_value(*[fields[c, i, 1, lines] for i in range(3)])
    zslope = forward_value(*[fields[c, i, 2, lines] for i in range(3)])
    return value, xslope, yslope, zslope


def apply_operator(above_floor, elements, pressures, chunk, state, slopes, fields, qpoints, ppoints, out, pout):
    low_half = lax.broadcasted_iota(jnp.int32, (8, 128), 0) < 4
    planes = [0, 1, 2] if chunk == 0 else [0]
    spread(elements, chunk, fields)
    if pressures is not None:
        corner = {}
        for i in range(2):
            for j in range(2):
                low = pressures[chunk, i * 2 + j]
                corner[i, j] = forward_linear(low, next_lane(low))
        for q in range(3):
            sides = [forward_linear(corner[i, 0][q], corner[i, 1][q]) for i in range(2)]
            for p in range(3):
                points = forward_linear(sides[0][p], sides[1][p])
                for r in range(3):
                    qpoints[r, p * 3 + q] = points[r]

    def one(line):
        lines = pl.ds(line, LINES)
        value, slope = [], []
        for c in range(3):
            v, gx, gy, gz = at_points(fields, lines, c)
            value.append(v)
            slope.append((gx, gy, gz))
        force = [[None] * 3 for _ in range(3)]
        flux = [[[None] * 3 for _ in range(3)] for _ in range(3)]
        for r in range(3):
            ppoints[r, lines] = slope[0][0][r] + slope[1][1][r] + slope[2][2][r]
            wind = [state[chunk, r, b, lines] for b in range(3)]
            pressure = qpoints[r, lines] if pressures is not None else None
            for a in range(3):
                for b in range(3):
                    g = slope[a][b][r] + value[a][r] * wind[b]
                    if a == b and pressures is not None:
                        g = g - pressure
                    flux[a][b][r] = g
                total = slopes[chunk, r, a * 3, lines] * value[0][r]
                for c in range(1, 3):
                    total = total + slopes[chunk, r, a * 3 + c, lines] * value[c][r]
                force[a][r] = total
        for c in range(3):
            first = back_both(force[c], flux[c][0])
            second = back_value(flux[c][1])
            third = back_value(flux[c][2])
            if chunk == 1:
                first, second, third = [[jnp.where(low_half, v[0], v[2])] for v in (first, second, third)]
            for i in planes:
                fields[c, i, 0, lines] = first[i]
                fields[c, i, 1, lines] = second[i]
                fields[c, i, 2, lines] = third[i]

    blocks(9, LINES, one)

    def gather(c):
        at = pl.ds(c, GATHER)
        value, zslope = [], []
        for q in range(3):
            value.append(
                back_both(
                    [fields[at, 0 : len(planes), 0, p * 3 + q] for p in range(3)],
                    [fields[at, 0 : len(planes), 1, p * 3 + q] for p in range(3)],
                )
            )
            zslope.append(back_value([fields[at, 0 : len(planes), 2, p * 3 + q] for p in range(3)]))
        for j in range(3):
            nodes = back_both([value[q][j] for q in range(3)], [zslope[q][j] for q in range(3)])
            out[chunk, at, 0 : len(planes), j, 0] = nodes[0] + last_lane(jnp.where(above_floor, nodes[2], 0.0))
            out[chunk, at, 0 : len(planes), j, 1] = nodes[1]

    blocks(3, GATHER, gather)
    rows = {}
    for q in range(3):
        sides = []
        for p in range(3):
            v = back_linear([ppoints[r, p * 3 + q] for r in range(3)])
            sides.append(v if chunk == 0 else [jnp.where(low_half, v[0], v[1])])
        for i in planes[:2]:
            rows[i, q] = back_linear([sides[p][i] for p in range(3)])
    for i in planes[:2]:
        for j in range(2):
            low, high = back_linear([rows[i, q][j] for q in range(3)])
            pout[chunk, i * 2 + j] = low + last_lane(jnp.where(above_floor, high, 0.0))


def pick(row, k):
    lane = lax.broadcasted_iota(jnp.int32, (1, 128), 1)
    return jnp.sum(jnp.where(lane == k, row, 0.0), axis=1, keepdims=True)


def solve(row):
    entries = {}
    at = 0
    for i in range(4):
        for j in range(i, 4):
            entries[i, j] = pick(row, at) + pick(row, 10)
            at += 1
    m = [[entries[min(i, j), max(i, j)] for j in range(1, 4)] + [entries[0, i]] for i in range(1, 4)]
    for k in range(2):
        inverse = 1.0 / m[k][k]
        for i in range(k + 1, 3):
            factor = m[i][k] * inverse
            for j in range(k + 1, 4):
                m[i][j] = m[i][j] - factor * m[k][j]
    t = [None] * 3
    for k in (2, 1, 0):
        total = m[k][3]
        for j in range(k + 1, 3):
            total = total - m[k][j] * t[j]
        t[k] = total / m[k][k]
    return t


def kernel(sizes, state_far, grad_far, wall_far, level_far, vel_out, pres_out,
           state_in, grad_in, wall_in, level_in, raw, nodes, ends, reach, even, odd, stiff, u0, us, u1, u2, u3, p1, p2, p3, keep_e, friction,
           wind, slopes, fields, qpoints, ppoints, out, pout, block, side, natural, plane_sum, line_sum,
           load, reached, across, send, recv):
    loads = [
        pltpu.make_async_copy(far, near, load.at[n])
        for n, (far, near) in enumerate(
            ((grad_far, grad_in), (state_far, state_in), (wall_far, wall_in), (level_far, level_in)))
    ]
    for copy in loads:
        copy.start()

    gx, gy, gz = lax.axis_index("gx"), lax.axis_index("gy"), lax.axis_index("gz")

    def device(o):
        return tuple(lax.rem(a + d + n, n) for a, d, n in zip((gx, gy, gz), o, sizes))

    others = [(a, b, 0) for a in range(sizes[0]) for b in range(sizes[1]) if (a, b) != (0, 0)]
    along = [(0, 0, d) for d in range(1, sizes[2])]
    partners = {tuple(d % n for d, n in zip(o, sizes)) for o in NEAR}

    def far_first(offsets):
        return sorted(offsets, key=lambda o: (-sum(min(d, n - d) for d, n in zip(o, sizes)), o))

    partners, others, along = far_first(partners - {(0, 0, 0)}), far_first(others), far_first(along)

    barrier = pltpu.get_barrier_semaphore()
    for o in partners:
        pl.semaphore_signal(barrier, inc=1, device_id=device(o), device_id_type=MESH)

    lane = lax.broadcasted_iota(jnp.int32, (8, 128), 1)
    sub = lax.broadcasted_iota(jnp.int32, (8, 128), 0)

    for n, o in enumerate(PLANE):
        first, count = PART_ROWS[-o[1]][1:]
        for lo, hi in ((0, first), (first + count, 8)):
            if lo < hi:
                side[n, :, :, lo:hi] = jnp.zeros((7, 5, hi - lo, 128), F32)

    for copy in loads:
        copy.wait()

    for x in range(4):
        spot = pl.ds((x % 2) * 4, 4)
        mask = 1.0 - wall_in[x].astype(F32)
        for c in range(3):
            raw[c, x // 2, spot] = mask * grad_in[c, x]
            raw[3 + c, x // 2, spot] = state_in[c, x]
        raw[6, x // 2, spot] = mask
    rows = lax.broadcasted_iota(jnp.int32, (128, 128), 0)
    cols = lax.broadcasted_iota(jnp.int32, (128, 128), 1)
    split = (rows == jnp.where(cols < 64, 2 * cols, 2 * cols - 127)).astype(F32)
    join = (cols == jnp.where(rows < 64, 2 * rows, 2 * rows - 127)).astype(F32)
    parted = jnp.dot(raw[0:7].reshape(112, 128), split, precision=HIGHEST, preferred_element_type=F32)
    parted = parted.reshape(7, 2, 8, 128)
    twice = (rows[:64] == jnp.where(cols[:64] < 64, cols[:64], cols[:64] - 64)).astype(F32)
    density = level_in[...].astype(F32) / (LEVELS - 1)
    drag = PEAK * SHAPE * (1.0 - density) / (SHAPE + density)
    for h in range(2):
        wide = jnp.dot(drag[h], twice, precision=HIGHEST, preferred_element_type=F32)
        for y in range(4):
            raw[7, h, y : y + 1] = wide[y // 2 : y // 2 + 1]
            raw[7, h, y + 4 : y + 5] = wide[y // 2 : y // 2 + 1]
    for h in range(2):
        first = jnp.zeros((8, 128), F32)
        last = jnp.zeros((8, 128), F32)
        for f in range(8):
            v = raw[7, h] if f == 6 else parted[6 if f == 7 else f, h]
            for xl in range(2):
                nodes[f, 2 + 2 * h + xl, 2:6] = v[4 * xl : 4 * xl + 4]
            go = 8 * f
            lower = (lane >= go) & (lane < go + 4)
            upper = (lane >= go + 4) & (lane < go + 8)
            first = jnp.where(lower, pltpu.roll(v, go, 1), first)
            first = jnp.where(upper, pltpu.roll(v, (go + 4 - 64) % 128, 1), first)
            last = jnp.where(lower, pltpu.roll(v, (go - 60) % 128, 1), last)
            last = jnp.where(upper, pltpu.roll(v, (go + 4 - 124) % 128, 1), last)
        for xl in range(2):
            ends[0, 2 * h + xl, 0:4] = last[4 * xl : 4 * xl + 4]
            ends[1, 2 * h + xl, 0:4] = first[4 * xl : 4 * xl + 4]

    pl.semaphore_wait(barrier, len(partners))

    def tell(n):
        for d in (-1, 1):
            pl.semaphore_signal(
                reached.at[n], inc=1, device_id=device((0, 0, d * 2**n)), device_id_type=MESH)

    rounds = 0
    while 2**rounds < sizes[2] // 2:
        rounds += 1
    if rounds:
        tell(0)

    for o in NEAR:
        sx, sy = -o[0], -o[1]
        (xs, xe), (ys, ye) = SOURCE[sx], SOURCE[sy]
        (tx, te), (ty, tf) = TARGET[sx], TARGET[sy]
        if o[2] == 0:
            source = nodes.at[:, 2 + xs : 2 + xe, 2 + ys : 2 + ye]
            target = nodes.at[:, tx:te, ty:tf]
            group = 0
        else:
            group = 1
            which = 0 if o[2] == 1 else 1
            source = ends.at[which, xs:xe, ys:ye]
            target = reach.at[which, tx:te, ty:tf]
        pltpu.make_async_remote_copy(
            src_ref=source, dst_ref=target, send_sem=send.at[group], recv_sem=recv.at[group],
            device_id=device(o), device_id_type=MESH).start()

    in_all = [
        nodes.at[:, 0:5, 0:13],
        reach.at[:, :, 0:9],
        side.at[0:7, :, 0:1],
        plane_sum.at[1 : len(others) + 1],
        line_sum.at[1 : len(along) + 1],
    ]

    def arrived(group):
        ref = in_all[group]
        pltpu.make_async_copy(ref, ref, recv.at[group]).wait()

    ey = sub % 4 - 1
    z = jnp.where(lane < 96, lane, lane - 128)
    zmin = jnp.where(gz > 0, -3, 0)
    zmax = jnp.where(gz < sizes[2] - 1, 65, 63)
    in_z = (z >= zmin) & (z <= zmax)
    ymin = jnp.where(gy > 0, -1, 0)
    ymax = jnp.where(gy < sizes[1] - 1, 2, 1)
    xmin = jnp.where(gx > 0, -1, 0)
    xmax = jnp.where(gx < sizes[0] - 1, 2, 1)
    ex = [jnp.where(sub < 4, 0, 1), jnp.where(sub < 4, 2, -1)]
    real = [in_z & (ey >= ymin) & (ey <= ymax) & (e >= xmin) & (e <= xmax) for e in ex]
    narrow = [r & (ey <= 1) & (e <= 1) for r, e in zip(real, ex)]
    own_y = (ey >= 0) & (ey <= 1)
    own_wide = in_z & own_y
    own = own_y & (lane < 64)
    zlim = jnp.where(gz < sizes[2] - 1, 64, 96)
    node_z = (lane < 64) | (lane >= zlim)
    above_floor = lane < jnp.where(gz > 0, 128, 96)
    ylim = jnp.where(gy < sizes[1] - 1, 99, 6)
    xlim = jnp.where(gx < sizes[0] - 1, 99, 6)
    node_yz = [node_z & (sub + 8 * h < ylim) for h in range(2)]

    if rounds > 1:
        pl.semaphore_wait(reached.at[0], 2)
        tell(1)
    arrived(0)
    arrived(1)
    if sizes[0] > 6:
        for d in (-2, 2):
            pl.semaphore_signal(across, inc=1, device_id=device((d, 0, 0)), device_id_type=MESH)

    def widen(first):
        xs = pl.ds(first, WIDEN)
        column = first + lax.broadcasted_iota(jnp.int32, (WIDEN, 8, 128), 0)
        inside = column < xlim
        for h in range(2):
            rows8 = pl.ds(8 * h, 8)
            below = reach[0, xs, rows8]
            above = reach[1, xs, rows8]
            ok = inside & node_yz[h]
            for f in range(8 if h == 0 else 6):
                v = nodes[f, xs, rows8]
                go = 8 * f
                e = jnp.where(lane < 96, pltpu.roll(above, (64 - go) % 128, 2), pltpu.roll(below, (124 - go) % 128, 2))
                e = jnp.where(lane < 64, v, e)
                if f == 6:
                    stiff[0, xs] = e
                    continue
                here = ok & ((sub >= 2) & (sub < 7)) if f == 7 else ok
                even[f, xs, rows8] = jnp.where(here, e, 0.0)
                o = jnp.where(lane < 96, pltpu.roll(above, (60 - go) % 128, 2), pltpu.roll(below, (120 - go) % 128, 2))
                o = jnp.where(lane < 64, pltpu.roll(v, 64, 2), o)
                odd[f, xs, rows8] = jnp.where(here, o, 0.0)

    blocks(9, WIDEN, widen)

    def to_elements(source, f, x, j):
        return source[f, x, pl.ds(j, 4, stride=2), :]

    def collect(first, target, masks):
        three = pl.ds(first, 3)
        for i in range(3):
            for j in range(3):
                for k, source in enumerate((even, odd)):
                    for chunk, (low, high) in enumerate(((2, 4), (6, 0))):
                        v = jnp.concatenate(
                            [to_elements(source, three, low + i, j), to_elements(source, three, high + i, j)], axis=1)
                        if masks is not None:
                            v = jnp.where(masks[chunk], v, 0.0)
                        target[chunk, :, i, j, k] = v

    collect(0, u0, real)
    collect(3, us, None)
    for i in range(3):
        for j in range(3):
            for k, source in enumerate((even, odd)):
                keep_e[i, j, k] = SCALE * jnp.concatenate(
                    [to_elements(source, 7, 2 + i, j), to_elements(source, 7, 4 + i, j)], axis=0)
    for chunk, (low, high) in enumerate(((2, 4), (6, 0))):
        friction[chunk] = jnp.concatenate([to_elements(stiff, 0, low, 0), to_elements(stiff, 0, high, 0)], axis=0)

    def prepare(chunk, carry):
        spread(us, chunk, fields)

        def one(line):
            lines = pl.ds(line, LINES)
            for c in range(3):
                v, gx_, gy_, gz_ = at_points(fields, lines, c)
                for r in range(3):
                    wind[chunk, r, c, lines] = v[r]
                    for b, g in enumerate((gx_, gy_, gz_)):
                        slopes[chunk, r, b * 3 + c, lines] = g[r] + friction[chunk] if b == c else g[r]

        blocks(9, LINES, one)
        return carry

    for chunk in range(2):
        prepare(chunk, 0)

    def first_step(chunk, carry):
        apply_operator(above_floor, u0, None, chunk, wind, slopes, fields, qpoints, ppoints, out, pout)
        return carry

    for chunk in range(2):
        first_step(chunk, 0)

    low_half = sub < 4

    def owners(source, at, last):
        total = {}
        for chunk in range(2):
            for i in range(last + 1) if chunk == 0 else (0,):
                v = [at(source, chunk, i, j) for j in range(last + 1)]
                total[chunk, i, 0] = v[0] + last_row(v[last])
                for j in range(1, last):
                    total[chunk, i, j] = v[j]
        for j in range(last):
            total[1, last, j] = total[1, 0, j]
        return total

    def close(total, last):
        full = {}
        edge = {}
        for j in range(last):
            before = half_turn(total[1, last, j])
            mine = half_turn(total[0, last, j])
            full[0, j] = total[0, 0, j] + jnp.where(low_half, before, mine)
            edge[j] = total[1, 0, j] + mine
            for i in range(1, last):
                full[i, j] = total[0, i, j]
        return full, edge

    def complete(full, edge, last):
        for j in range(last):
            full[last, j] = jnp.where(low_half, half_turn(full[0, j]), half_turn(edge[j]))
        for i in range(last + 1):
            full[i, last] = next_row(full[i, 0])
        return full

    def finish_first(c, carry):
        for k in range(2):
            total = owners(out, lambda s, chunk, i, j: s[chunk, c, i, j, k], 2)
            full = complete(*close(total, 2), 2)
            for i in range(3):
                for j in range(3):
                    u1[0, c, i, j, k] = jnp.where(own_wide, full[i, j] * keep_e[i, j, k], 0.0)
        return carry

    [finish_first(c, 0) for c in range(3)]

    def vertex_mask(i, j):
        ok = own_wide & ((lane < 64) | (lane >= zlim))
        ylast = jnp.where(gy < sizes[1] - 1, 99, 2)
        xlast = jnp.where(gx < sizes[0] - 1, 99, 2)
        return ok & (ey + j < ylast) & (ex[0] + i < xlast)

    full = complete(*close(owners(pout, lambda s, chunk, i, j: s[chunk, i * 2 + j], 1), 1), 1)
    for i in range(2):
        for j in range(2):
            p1[0, i * 2 + j] = jnp.where(vertex_mask(i, j), -SCALE * full[i, j], 0.0)

    if rounds > 2:
        pl.semaphore_wait(reached.at[1], 2)
        tell(2)

    apply_operator(above_floor, u1, p1, 0, wind, slopes, fields, qpoints, ppoints, out, pout)

    def store_rows(plane, x, parity, v, step):
        block[plane, x, pl.ds(parity, 4, stride=step), :] = v

    for n in range(7):
        last = 2 if n < 6 else 1
        c, k = n // 2, n % 2

        def at(i, j):
            return out[0, c, i, j, k] if n < 6 else pout[0, i * 2 + j]

        for j in range(last):
            v = [at(i, 0) + last_row(at(i, last)) if j == 0 else at(i, j) for i in range(last + 1)]
            if n == 6:
                v = [-SCALE * w for w in v]
            step = 2 // last
            turned = [half_turn(w) for w in v]
            for i in range(last):
                store_rows(n, step * i, j, v[i][0:4], 2)
            store_rows(n, 2, j, (v[last] + turned[0])[0:4], 2)
            for i in range(1, last):
                store_rows(n, 2 + i, j, turned[i][0:4], 2)
            store_rows(n, 4, j, turned[last][0:4], 2)
    vertex_yz = jnp.where(node_yz[0], 1.0, 0.0)
    for x in range(5):
        inside = jnp.where(x + 2 < xlim, 1.0, 0.0).astype(F32)
        for k, source in enumerate((even, odd)):
            mask = SCALE * source[7, x + 2, 0:8]
            for c in range(3):
                block[2 * c + k, x] = block[2 * c + k, x] * mask
        if x % 2 == 0:
            odd_rows = sub % 2 == 1
            block[6, x] = jnp.where(odd_rows, 0.0, block[6, x] * (vertex_yz * inside))
        else:
            block[6, x] = jnp.zeros((8, 128), F32)

    for n, o in enumerate(PLANE):
        sx, sy = -o[0], -o[1]
        xs, xe = {-1: (2, 5), 0: (0, 5), 1: (0, 1)}[sx]
        ys, ty, count = PART_ROWS[sy]
        pltpu.make_async_remote_copy(
            src_ref=block.at[:, xs:xe, ys : ys + count], dst_ref=side.at[n, :, 0 : xe - xs, ty : ty + count],
            send_sem=send.at[2], recv_sem=recv.at[2], device_id=device(o), device_id_type=MESH).start()

    have = {0: 1.0}
    have_x = {-1: jnp.where(gx > 0, 1.0, 0.0).astype(F32), 1: jnp.where(gx < sizes[0] - 1, 1.0, 0.0).astype(F32)}
    have_y = {-1: jnp.where(gy > 0, 1.0, 0.0).astype(F32), 1: jnp.where(gy < sizes[1] - 1, 1.0, 0.0).astype(F32)}
    arrived(2)
    if rounds > 3:
        pl.semaphore_wait(reached.at[2], 2)
        tell(3)

    def part(n, plane, x):
        sx, sy = -PLANE[n][0], -PLANE[n][1]
        v = side[n, plane, x]
        if sx:
            v = v * have_x[sx]
        if sy:
            v = v * have_y[sy]
        return v

    slot = {(-o[0], -o[1]): n for n, o in enumerate(PLANE)}

    def join_parts(plane, target, f):
        for x in range(7):
            total = block[plane, x - 2] if x >= 2 else None
            for sx in (-1, 0, 1):
                lo, hi = {-1: (0, 2), 0: (2, 6), 1: (6, 6)}[sx]
                if not lo <= x <= hi:
                    continue
                for sy in (-1, 0, 1):
                    if (sx, sy) != (0, 0):
                        v = part(slot[sx, sy], plane, x - lo)
                        total = v if total is None else total + v
            target[f, x, 0:8] = total

    def join_component(c, carry):
        join_parts(2 * c, even, c)
        join_parts(2 * c + 1, odd, c)
        return carry

    [join_component(c, 0) for c in range(3)]
    join_parts(6, even, 3)
    collect(0, u2, narrow)
    for i in range(2):
        for j in range(2):
            for chunk, (low, high) in enumerate(((2, 4), (6, 0))):
                v = jnp.concatenate(
                    [to_elements(even, 3, low + 2 * i, 2 * j), to_elements(even, 3, high + 2 * i, 2 * j)], axis=0)
                p2[chunk, i * 2 + j] = jnp.where(narrow[chunk], v, 0.0)

    def last_step(chunk, carry):
        apply_operator(above_floor, u2, p2, chunk, wind, slopes, fields, qpoints, ppoints, out, pout)
        return carry

    for chunk in range(2):
        last_step(chunk, 0)

    def finish_last(c, carry):
        for k in range(2):
            total = owners(out, lambda s, chunk, i, j: s[chunk, c, i, j, k], 2)
            full, _ = close(total, 2)
            for i in range(2):
                for j in range(2):
                    u3[0, c, i, j, k] = full[i, j] * keep_e[i, j, k]
        return carry

    [finish_last(c, 0) for c in range(3)]
    full, _ = close(owners(pout, lambda s, chunk, i, j: s[chunk, i * 2 + j], 1), 1)
    p3[0, 0] = -SCALE * full[0, 0]

    pairs = [(i, j) for i in range(4) for j in range(i, 4)]

    def products(c, sums):
        sums = list(sums)
        for i in range(2):
            for j in range(2):
                for k in range(2):
                    v = [u[0, c, i, j, k] for u in (u0, u1, u2, u3)]
                    for n, (a, b) in enumerate(pairs):
                        sums[n] = sums[n] + v[a] * v[b]
        return tuple(sums)

    sums = [jnp.zeros((8, 128), F32) for _ in pairs]
    for c in range(3):
        sums = list(products(c, sums))
    ps = [None, p1[0, 0], p2[0, 0], p3[0, 0]]
    for n, (a, b) in enumerate(pairs):
        if a:
            sums[n] = sums[n] + ps[a] * ps[b]
    fixed = jnp.zeros((4, 128), F32)
    for x in range(4):
        held = wall_in[x].astype(F32)
        for c in range(3):
            v = held * grad_in[c, x]
            fixed = fixed + v * v
    single = lane[0:1]
    row = jnp.zeros((1, 128), F32)
    for n in range(10):
        total = jnp.sum(jnp.sum(jnp.where(own, sums[n], 0.0), axis=0, keepdims=True), axis=1, keepdims=True)
        row = jnp.where(single == n, total, row)
    total = jnp.sum(jnp.sum(fixed, axis=0, keepdims=True), axis=1, keepdims=True)
    row = jnp.where(single == 10, total, row)

    def exchange(group, offsets, buffer, value):
        buffer[0:1] = value
        for n, o in enumerate(offsets):
            pltpu.make_async_remote_copy(
                src_ref=buffer.at[0:1], dst_ref=buffer.at[n + 1 : n + 2], send_sem=send.at[group], recv_sem=recv.at[group],
                device_id=device(o), device_id_type=MESH).start()

    def gathered(group, buffer):
        arrived(group)
        return jnp.sum(buffer[...], axis=0, keepdims=True)

    if sizes[0] > 6:
        pl.semaphore_wait(across, 2)
    exchange(3, others, plane_sum, row)

    for n, u in enumerate((u1, u2)):
        for c in range(3):
            packed = []
            for i in range(2):
                for j in range(2):
                    packed.append(jnp.where(lane < 64, u[0, c, i, j, 0], pltpu.roll(u[0, c, i, j, 1], 64, 1)))
            flat = jnp.concatenate(packed, axis=0)
            flat = jnp.dot(flat, join, precision=HIGHEST, preferred_element_type=F32)
            for i in range(2):
                for j in range(2):
                    at8 = (i * 2 + j) * 8
                    for e in range(2):
                        natural[n, c, 2 * e + i, pl.ds(j, 2, stride=2), :] = flat[at8 + 4 * e + 1 : at8 + 4 * e + 3]

    row = gathered(3, plane_sum)
    if rounds:
        pl.semaphore_wait(reached.at[rounds - 1], 2)
    exchange(4, along, line_sum, row)
    row = gathered(4, line_sum)
    t = solve(row)
    for x in range(4):
        free = wall_in[x] == 0
        for c in range(3):
            b = grad_in[c, x]
            v = t[1] * natural[0, c, x, 0:4] + t[2] * natural[1, c, x, 0:4]
            vel_out[c, x] = jnp.where(free, t[0] * b, (t[0] + t[1] + t[2]) * b) + v
    v = t[1] * p1[0, 0] + t[2] * p2[0, 0]
    for e in range(2):
        pres_out[e] = v[4 * e + 1 : 4 * e + 3, 0:64]

    for group, ref in enumerate(in_all):
        pltpu.make_async_copy(ref, ref, send.at[group]).wait()


def hand_over(vel_in, pres_in, vel_out, pres_out, vel, pres, done):
    for stage in (((vel_in, vel), (pres_in, pres)), ((vel, vel_out), (pres, pres_out))):
        copies = [pltpu.make_async_copy(a, b, done.at[n]) for n, (a, b) in enumerate(stage)]
        for copy in copies:
            copy.start()
        for copy in copies:
            copy.wait()


def local(sizes, state_velocity, objective_gradient, wall_flags, design_levels):
    vm = pltpu.VMEM
    plane, line = sizes[0] * sizes[1], sizes[2]
    tile = (8, 128)
    scratch = [
        vm((3, 4, 4, 128), F32),
        vm((3, 4, 4, 128), F32),
        vm((4, 4, 128), jnp.int32),
        vm((2, 2, 64), jnp.int32),
        vm((8, 2) + tile, F32),
        vm((8, 9, 16, 128), F32),
        vm((2, 4) + tile, F32),
        vm((2, 9, 16, 128), F32),
        vm((8, 9, 16, 128), F32),
        vm((8, 9, 16, 128), F32),
        vm((1, 9) + tile, F32),
        vm((2, 3, 3, 3, 2) + tile, F32),
        vm((2, 3, 3, 3, 2) + tile, F32),
        vm((1, 3, 3, 3, 2) + tile, F32),
        vm((2, 3, 3, 3, 2) + tile, F32),
        vm((1, 3, 3, 3, 2) + tile, F32),
        vm((1, 4) + tile, F32),
        vm((2, 4) + tile, F32),
        vm((1, 1) + tile, F32),
        vm((3, 3, 2) + tile, F32),
        vm((2,) + tile, F32),
        vm((2, 3, 3, 9) + tile, F32),
        vm((2, 3, 9, 9) + tile, F32),
        vm((3, 3, 3, 9) + tile, F32),
        vm((3, 9) + tile, F32),
        vm((3, 9) + tile, F32),
        vm((2, 3, 3, 3, 2) + tile, F32),
        vm((2, 4) + tile, F32),
        vm((7, 5) + tile, F32),
        vm((8, 7, 5) + tile, F32),
        vm((2, 3, 4) + tile, F32),
        vm((plane, 128), F32),
        vm((line, 128), F32),
    ]
    scratch += [
        pltpu.SemaphoreType.DMA((4,)),
        pltpu.SemaphoreType.REGULAR((4,)),
        pltpu.SemaphoreType.REGULAR,
        pltpu.SemaphoreType.DMA((5,)),
        pltpu.SemaphoreType.DMA((5,)),
    ]
    shapes = (
        jax.ShapeDtypeStruct((3, 4, 4, 128), F32),
        jax.ShapeDtypeStruct((2, 2, 64), F32),
    )
    grant = 56 * 1024 * 1024
    iterate = pl.pallas_call(
        functools.partial(kernel, sizes),
        out_shape=shapes,
        in_specs=[pl.BlockSpec(memory_space=pl.ANY)] * 4,
        out_specs=[pl.BlockSpec(memory_space=pltpu.VMEM)] * 2,
        scratch_shapes=scratch,
        compiler_params=pltpu.CompilerParams(
            collective_id=0, has_side_effects=True, vmem_limit_bytes=grant
        ),
    )(state_velocity, objective_gradient, wall_flags, design_levels)
    return pl.pallas_call(
        hand_over,
        out_shape=shapes,
        in_specs=[pl.BlockSpec(memory_space=pl.ANY)] * 2,
        out_specs=[pl.BlockSpec(memory_space=pl.ANY)] * 2,
        scratch_shapes=[vm((3, 4, 4, 128), F32), vm((2, 2, 64), F32), pltpu.SemaphoreType.DMA((2,))],
        compiler_params=pltpu.CompilerParams(vmem_limit_bytes=grant),
    )(*iterate)


def solution(mesh):
    in_specs = (
        P(None, "gx", "gy", "gz"),
        P(None, "gx", "gy", "gz"),
        P("gx", "gy", "gz"),
        P("gx", "gy", "gz"),
    )
    out_specs = (P(None, "gx", "gy", "gz"), P("gx", "gy", "gz"))
    sizes = tuple(mesh.shape[a] for a in ("gx", "gy", "gz"))
    return jax.shard_map(
        functools.partial(local, sizes), mesh=mesh, in_specs=in_specs, out_specs=out_specs, check_vma=False
    )
```
